32 devices in a mesh: dp: 8 (over z, y), code: 4 (over x, core).
Axes of the slice: x: 2, y: 2, z: 4, core: 2. Of those that a mesh axis runs over, the one named last changes fastest.
Arguments:
- crops_in: bfloat16 [4, 16, 256, 512], P('code', None, 'dp'), may hold values from -6 to 6
- crop_weight: bfloat16 [4, 16], P('code', 'dp'), may hold values from 0.7 to 6
- cotangent: bfloat16 [4, 16, 64, 256], P('code', 'dp'), may hold values from -6 to 6
- conv_copy: bfloat16 [512, 2, 9, 512], replicated, may hold values from -0.09375 to 0.09375
- down_copy: bfloat16 [512, 4, 512], replicated, may hold values from -0.125 to 0.125
- proj_copy: bfloat16 [512, 256], replicated, may hold values from -0.25 to 0.25
- norm_copy: bfloat16 [512, 4], replicated, may hold values from -0.95 to 1.5
- codebook: bfloat16 [16384, 256], P('code'), may hold values from -5 to 5
- conv_master: float32 [512, 2, 9, 512], P('dp', None, None, 'code'), may hold values from -0.09375 to 0.09375
- conv_moment: float32 [512, 2, 9, 512], P('dp', None, None, 'code'), may hold values from -7680 to 7680
- conv_average: float32 [512, 2, 9, 512], P('dp', None, None, 'code'), may hold values from -0.09375 to 0.09375
- down_master: float32 [512, 4, 512], P('dp', None, 'code'), may hold values from -0.125 to 0.125
- down_moment: float32 [512, 4, 512], P('dp', None, 'code'), may hold values from -384 to 384
- down_average: float32 [512, 4, 512], P('dp', None, 'code'), may hold values from -0.125 to 0.125
- proj_master: float32 [512, 256], P('dp', 'code'), may hold values from -0.25 to 0.25
- proj_moment: float32 [512, 256], P('dp', 'code'), may hold values from -512 to 512
- proj_average: float32 [512, 256], P('dp', 'code'), may hold values from -0.25 to 0.25
- norm_master: float32 [512, 4], replicated, may hold values from 0.5 to 1.5
- norm_moment: float32 [512, 4], replicated, may hold values from -192 to 192
- norm_average: float32 [512, 4], replicated, may hold values from 0.5 to 1.5
- code_master: float32 [16384, 256], P('code', 'dp'), may hold values from -5 to 5
- code_moment: float32 [16384, 256], P('code', 'dp'), may hold values from -6 to 6
- code_average: float32 [16384, 256], P('code', 'dp'), may hold values from -5 to 5
- repl_code: int32 [4, 64], replicated, may hold values from 0 to 16383, as said below
- repl_src: int32 [4, 64], replicated, may hold values from 0 to 4095
Outputs:
- quantized: float32 [4, 16, 64, 256], P('code', 'dp')
- input_grad: float32 [4, 16, 256, 512], P('code', None, 'dp')
- conv_moment_new: float32 [512, 2, 9, 512], P('dp', None, None, 'code')
- conv_master_new: float32 [512, 2, 9, 512], P('dp', None, None, 'code')
- conv_average_new: float32 [512, 2, 9, 512], P('dp', None, None, 'code')
- down_moment_new: float32 [512, 4, 512], P('dp', None, 'code')
- down_master_new: float32 [512, 4, 512], P('dp', None, 'code')
- down_average_new: float32 [512, 4, 512], P('dp', None, 'code')
- proj_moment_new: float32 [512, 256], P('dp', 'code')
- proj_master_new: float32 [512, 256], P('dp', 'code')
- proj_average_new: float32 [512, 256], P('dp', 'code')
- norm_moment_new: float32 [512, 4], replicated
- norm_master_new: float32 [512, 4], replicated
- norm_average_new: float32 [512, 4], replicated
- code_moment_new: float32 [16384, 256], P('code', 'dp')
- code_master_new: float32 [16384, 256], P('code', 'dp')
- code_average_new: float32 [16384, 256], P('code', 'dp')
- code_load: float32 [16384], P('code')
The draws below stay inside these ranges and needn't reach their ends.
Inputs may be any that keep to these rules, and one draw needn't show every extreme that they name: `repl_code`: the 4 x 64 codes are all different.
All inputs are finite; a program needn't handle non-finite values.
Results may differ from the reference program's by a relative error of at most 0.014.
Values may be sent and summed in bfloat16 or wider, within the bound.
No kernel may reach another device: no remote copies, remote signals or barrier semaphores. Data moves between devices by JAX's collectives and lax.ppermute only.
A program may use at most 256 MiB of HBM per device.

```python
import math
import jax
import jax.numpy as jnp
from jax import lax

CH = 512
GROUPS = 32
EMB = 256
CODES = 16384
DEPTH = 4
SIDE = 16
NREP = 64
PIX = 256
LAT = 64
SETS = 4
CROPS_SET = 16
CROPS = 64
TOKENS = 4096
CODE_DEV = 4096
N_CODE = 4


def draw_crop_weight(key, part):
    key = jax.random.fold_in(key, 11)
    position = jnp.arange(CROPS_SET, dtype=jnp.float32) / max(CROPS_SET - 1, 1)
    rise = 1.0 + 2.0 * position
    factor = jax.random.uniform(key, (SETS, CROPS_SET), jnp.float32, 0.7, 1.3)
    return (rise[None, :] * factor).astype(jnp.bfloat16)


def draw_norm_copy(key, part):
    key = jax.random.fold_in(key, 12)
    noise = jnp.clip(jax.random.normal(key, (CH, 4), jnp.float32), -3.0, 3.0)
    centre = jnp.array([1.0, 0.0, 1.0, 0.0], jnp.float32)
    spread = jnp.array([0.15, 0.3, 0.15, 0.3], jnp.float32)
    return (centre[None, :] + spread[None, :] * noise).astype(jnp.bfloat16)


def draw_repl_code(key, part):
    key = jax.random.fold_in(key, 13)
    chosen = jax.random.permutation(key, CODES)[:DEPTH * NREP]
    return chosen.reshape(DEPTH, NREP).astype(jnp.int32)


def draw_conv_moment(key, part):
    key = jax.random.fold_in(key, 14)
    sign_key, size_key = jax.random.split(key)
    array_shape = (CH, 2, 9, CH)
    spread_scale = float(CROPS * PIX) ** 0.5
    signs = jnp.where(jax.random.uniform(sign_key, array_shape, jnp.float32) < 0.5, -1.0, 1.0)
    magnitude = 8.0 * spread_scale * jnp.exp(jax.random.uniform(size_key, array_shape, jnp.float32, -0.6931, 0.6931))
    return (signs * magnitude).astype(jnp.float32)


def with_ends(values, key, low, high):
    index_at = [jax.random.randint(jax.random.fold_in(key, axis), (), 0, length) for axis, length in enumerate(values.shape)]
    longest = values.shape.index(max(values.shape))
    beside = index_at[:longest] + [(index_at[longest] + 1) % values.shape[longest]] + index_at[longest + 1:]
    return values.at[tuple(index_at)].set(low).at[tuple(beside)].set(high)


def block_levels(own_key, shape, pieces, smallest, largest):
    def one(axis_at, shards_of):
        steps = jax.random.uniform(jax.random.fold_in(jax.random.fold_in(own_key, 6), axis_at), (shards_of,), jnp.float32, smallest / len(pieces), largest / len(pieces))
        return jnp.repeat(jnp.exp(steps), shape[axis_at] // shards_of).reshape((-1,) + (1,) * (len(shape) - axis_at - 1))

    loudness = one(*pieces[0])
    for cut in pieces[1:]:
        loudness = loudness * one(*cut)
    return loudness


def centred(own_key, extent, scale, bound, pieces=(), kind=jnp.bfloat16):
    entries = scale * jax.random.normal(own_key, extent, jnp.float32)
    if pieces:
        entries = entries * block_levels(own_key, extent, pieces, -0.22, 0.18)
    return jnp.clip(entries, -bound, bound).astype(kind)


def setup_inputs(seed: int = 0) -> dict:
    key_of = jax.random.split(jax.random.key(seed), 26)
    return {
        "crops_in": centred(key_of[0], (SETS, CROPS_SET, PIX, CH), 1.0, 6.0, ((0, 4), (2, 8))),
        "crop_weight": draw_crop_weight(jax.random.fold_in(key_of[25], 71), 0),
        "cotangent": centred(key_of[2], (SETS, CROPS_SET, LAT, EMB), 1.0, 6.0, ((0, 4), (1, 8))),
        "conv_copy": centred(key_of[3], (CH, 2, 9, CH), (9 * CH) ** -0.5, 0.09375),
        "down_copy": centred(key_of[4], (CH, 4, CH), (4 * CH) ** -0.5, 0.125),
        "proj_copy": centred(key_of[5], (CH, EMB), CH ** -0.5, 0.25),
        "norm_copy": draw_norm_copy(jax.random.fold_in(key_of[25], 71), 0),
        "codebook": centred(key_of[7], (CODES, EMB), 1.0, 5.0, ((0, 4),)),
        "conv_master": centred(key_of[8], (CH, 2, 9, CH), (9 * CH) ** -0.5, 0.09375, ((0, 8), (3, 4)), jnp.float32),
        "conv_moment": draw_conv_moment(jax.random.fold_in(key_of[25], 71), 0),
        "conv_average": centred(key_of[10], (CH, 2, 9, CH), (9 * CH) ** -0.5, 0.09375, ((0, 8), (3, 4)), jnp.float32),
        "down_master": centred(key_of[11], (CH, 4, CH), (4 * CH) ** -0.5, 0.125, ((0, 8), (2, 4)), jnp.float32),
        "down_moment": centred(key_of[12], (CH, 4, CH), ((CROPS * LAT) ** 0.5), 384.0, ((0, 8), (2, 4)), jnp.float32),
        "down_average": centred(key_of[13], (CH, 4, CH), (4 * CH) ** -0.5, 0.125, ((0, 8), (2, 4)), jnp.float32),
        "proj_master": centred(key_of[14], (CH, EMB), CH ** -0.5, 0.25, ((0, 8), (1, 4)), jnp.float32),
        "proj_moment": centred(key_of[15], (CH, EMB), ((CROPS * LAT) ** 0.5 * 3 / 2), 512.0, ((0, 8), (1, 4)), jnp.float32),
        "proj_average": centred(key_of[16], (CH, EMB), CH ** -0.5, 0.25, ((0, 8), (1, 4)), jnp.float32),
        "norm_master": jnp.clip(1.0 + 0.1 * jax.random.normal(key_of[17], (CH, 4), jnp.float32), 0.5, 1.5),
        "norm_moment": centred(key_of[18], (CH, 4), ((CROPS * PIX) ** 0.5 / 4), 192.0, (), jnp.float32),
        "norm_average": jnp.clip(1.0 + 0.1 * jax.random.normal(key_of[19], (CH, 4), jnp.float32), 0.5, 1.5),
        "code_master": centred(key_of[20], (CODES, EMB), 1.0, 5.0, ((0, 4), (1, 8)), jnp.float32),
        "code_moment": centred(key_of[21], (CODES, EMB), ((DEPTH * TOKENS / CODES) ** 0.5), 6.0, ((0, 4), (1, 8)), jnp.float32),
        "code_average": centred(key_of[22], (CODES, EMB), 1.0, 5.0, ((0, 4), (1, 8)), jnp.float32),
        "repl_code": draw_repl_code(jax.random.fold_in(key_of[25], 71), 0),
        "repl_src": with_ends(jax.random.randint(key_of[24], (DEPTH, NREP), 0, TOKENS), jax.random.fold_in(key_of[24], 1), 0, TOKENS - 1).astype(jnp.int32),
    }


BETA = 0.0625
EPSILON = 1e-05
MOMENTUM = 0.5
AVERAGE_DECAY = 0.5
COMMIT = 0.25
WEIGHT_RATE = 0.05
NORM_RATE = 0.5
CODE_RATE = 0.5
HIGH = lax.Precision.HIGHEST

@jax.custom_vjp
def low(v):
    return lax.optimization_barrier(v.astype(jnp.bfloat16)).astype(jnp.float32)

@jax.custom_vjp
def low_back(v):
    return v

def low_keep(v):
    return (low(v), None)

def low_pass(kept, grad):
    return (grad,)

def back_keep(v):
    return (v, None)

def back_low(kept, grad):
    return (low(grad),)
low.defvjp(low_keep, low_pass)
low_back.defvjp(back_keep, back_low)

def group_norm(values, gain, bias):
    crops, pixels, channels = values.shape
    grouped = values.reshape(crops, pixels, GROUPS, channels // GROUPS)
    center = lax.optimization_barrier(jnp.mean(grouped, axis=(1, 3), keepdims=True))
    shifted = grouped - center
    spread = lax.optimization_barrier(jnp.mean(shifted * shifted, axis=(1, 3), keepdims=True))
    normed = (shifted * lax.rsqrt(spread + EPSILON)).reshape(crops, pixels, channels)
    return normed * gain + bias

def conv_taps(image, weight):
    crops = image.shape[0]
    grid = image.reshape(crops, SIDE, SIDE, image.shape[2])
    padded = jnp.pad(grid, ((0, 0), (1, 1), (1, 1), (0, 0)))
    result = jnp.zeros((crops, SIDE, SIDE, weight.shape[2]), jnp.float32)
    for tap in range(9):
        window = padded[:, tap // 3:tap // 3 + SIDE, tap % 3:tap % 3 + SIDE, :]
        result = result + jnp.einsum('bhwc,cd->bhwd', window, weight[:, tap, :], precision=HIGH)
    return result.reshape(crops, PIX, weight.shape[2])

def down_taps(image, weight):
    crops = image.shape[0]
    grid = image.reshape(crops, SIDE, SIDE, image.shape[2])
    result = jnp.zeros((crops, SIDE // 2, SIDE // 2, weight.shape[2]), jnp.float32)
    for tap in range(4):
        window = grid[:, tap // 2::2, tap % 2::2, :]
        result = result + jnp.einsum('bhwc,cd->bhwd', window, weight[:, tap, :], precision=HIGH)
    return result.reshape(crops, LAT, weight.shape[2])

def soft_block(rows, weight, codes, norms):
    inner = low_back(jnp.dot(low(rows), codes.T, precision=HIGH))
    scores = (BETA * (2.0 * inner - norms[None, :])).reshape(rows.shape[0], N_CODE, CODE_DEV)
    tops = lax.optimization_barrier(jnp.max(scores, axis=2))
    powers = jnp.exp(scores - tops[:, :, None])
    totals = lax.optimization_barrier(jnp.sum(powers, axis=2))
    shards = codes.reshape(N_CODE, CODE_DEV, codes.shape[1])
    weighted = low_back(jnp.einsum('bck,cke->bce', low(powers), shards, precision=HIGH))
    peak = lax.optimization_barrier(jnp.max(tops, axis=1, keepdims=True))
    scales = jnp.exp(tops - peak)
    whole = lax.optimization_barrier(jnp.sum(totals * scales, axis=1, keepdims=True))
    picked = lax.optimization_barrier(jnp.sum(weighted * scales[:, :, None], axis=1)) / whole
    factor = weight[:, None] * scales / whole
    counts = lax.optimization_barrier(jnp.sum(powers * factor[:, :, None], axis=0)).reshape(-1)
    return (picked, counts)

def nesterov_step(master, moment, average, grad, rate):
    moment_new = MOMENTUM * moment + grad
    master_new = master - rate * (grad + MOMENTUM * moment_new)
    return (moment_new, master_new, AVERAGE_DECAY * average + (1.0 - AVERAGE_DECAY) * master_new)

def reference(crops_in, crop_weight, cotangent, conv_copy, down_copy, proj_copy, norm_copy, codebook, conv_master, conv_moment, conv_average, down_master, down_moment, down_average, proj_master, proj_moment, proj_average, norm_master, norm_moment, norm_average, code_master, code_moment, code_average, repl_code, repl_src):
    inputs = crops_in.astype(jnp.float32).reshape(CROPS, PIX, CH)
    token_weight = jnp.repeat(crop_weight.astype(jnp.float32).reshape(CROPS), LAT)
    block = 512 if TOKENS % 512 == 0 else TOKENS

    def forward(images, conv_weight, down_weight, proj_weight, norm_params, codes):
        out_first = group_norm(images, norm_params[:, 0], norm_params[:, 1])
        act_first = low(jax.nn.silu(out_first))
        conv_first = low_back(conv_taps(act_first, conv_weight[:, 0]))
        out_second = group_norm(conv_first, norm_params[:, 2], norm_params[:, 3])
        act_second = low(jax.nn.silu(out_second))
        conv_second = low_back(conv_taps(act_second, conv_weight[:, 1]))
        summed = low(images + conv_second)
        reduced = low(low_back(down_taps(summed, down_weight)))
        latent = low(low_back(jnp.einsum('blc,ce->ble', reduced, proj_weight, precision=HIGH)))
        residual = latent.reshape(TOKENS, EMB)
        norms = lax.optimization_barrier(jnp.sum(codes * codes, axis=1))

        def run_block(pair):
            return soft_block(pair[0], pair[1], codes, norms)
        run_saved = jax.checkpoint(run_block)
        quantized = jnp.zeros((TOKENS, EMB), jnp.float32)
        loss = jnp.zeros((), jnp.float32)
        counts = jnp.zeros((CODES,), jnp.float32)
        levels = []
        for level in range(DEPTH):
            levels.append(residual)
            picked, block_counts = lax.map(run_saved, (residual.reshape(TOKENS // block, block, EMB), token_weight.reshape(TOKENS // block, block)))
            picked = picked.reshape(TOKENS, EMB)
            counts = counts + lax.optimization_barrier(jnp.sum(block_counts, axis=0))
            residual = residual - picked
            quantized = quantized + picked
            loss = loss + COMMIT * jnp.sum(token_weight * lax.optimization_barrier(jnp.sum(residual * residual, axis=1)))
        return ((quantized, loss), (jnp.stack(levels), counts))
    primal, pullback, aux = jax.vjp(forward, inputs, conv_copy.astype(jnp.float32), down_copy.astype(jnp.float32), proj_copy.astype(jnp.float32), norm_copy.astype(jnp.float32), codebook.astype(jnp.float32), has_aux=True)
    quantized = primal[0]
    grads = pullback((cotangent.astype(jnp.float32).reshape(TOKENS, EMB), jnp.ones((), jnp.float32)))
    grad_in, grad_conv, grad_down, grad_proj, grad_norm, grad_code = grads
    levels, counts = aux
    weight_rate = WEIGHT_RATE / math.sqrt(CROPS * PIX)
    norm_rate = NORM_RATE / math.sqrt(CROPS * PIX)
    code_rate = CODE_RATE / math.sqrt(DEPTH * TOKENS / CODES)
    conv_out = nesterov_step(conv_master, conv_moment, conv_average, grad_conv, weight_rate)
    down_out = nesterov_step(down_master, down_moment, down_average, grad_down, weight_rate)
    proj_out = nesterov_step(proj_master, proj_moment, proj_average, grad_proj, weight_rate)
    norm_out = nesterov_step(norm_master, norm_moment, norm_average, grad_norm, norm_rate)
    flat_code = repl_code.reshape(-1).astype(jnp.int32)
    depth_index = jnp.repeat(jnp.arange(DEPTH, dtype=jnp.int32), NREP)
    source_rows = levels[depth_index, repl_src.reshape(-1).astype(jnp.int32)]
    mean_count = DEPTH * LAT * CROPS / CODES
    share = mean_count / (mean_count + counts)
    code_load = counts / mean_count
    code_moment_new = MOMENTUM * code_moment + grad_code
    stepped = code_master - code_rate * (grad_code + MOMENTUM * code_moment_new)
    old_rows = stepped[flat_code]
    code_master_new = stepped.at[flat_code].set(old_rows + share[flat_code][:, None] * (source_rows - old_rows))
    code_average_new = AVERAGE_DECAY * code_average + (1.0 - AVERAGE_DECAY) * code_master_new
    return (quantized.reshape(SETS, CROPS_SET, LAT, EMB), grad_in.reshape(SETS, CROPS_SET, PIX, CH), conv_out[0], conv_out[1], conv_out[2], down_out[0], down_out[1], down_out[2], proj_out[0], proj_out[1], proj_out[2], norm_out[0], norm_out[1], norm_out[2], code_moment_new, code_master_new, code_average_new, code_load)
```

```python
import functools
import math

import jax
import jax.numpy as jnp
from jax import lax
from jax.experimental import pallas as pl
from jax.experimental.pallas import tpu as pltpu
from jax.sharding import PartitionSpec as P

GROUPS = 32
DEPTH = 4
BETA = 0.0625
EPSILON = 1e-05
MOMENTUM = 0.5
AVERAGE_DECAY = 0.5
COMMIT = 0.25
WEIGHT_RATE = 0.05
NORM_RATE = 0.5
CODE_RATE = 0.5

BF = jnp.bfloat16
F32 = jnp.float32
NT = (((1,), (1,)), ((), ()))
NN = (((1,), (0,)), ((), ()))
TN = (((0,), (0,)), ((), ()))
MIB = 1 << 20


def mm(a, b, dims=NN):
    return lax.dot_general(a, b, dims, preferred_element_type=F32)


def vmem():
    return pl.BlockSpec(memory_space=pltpu.VMEM)


def smem():
    return pl.BlockSpec(memory_space=pltpu.SMEM)


def hbm():
    return pl.BlockSpec(memory_space=pl.ANY)


def group_sum(rows, per_group):
    lanes = rows.shape[1]
    at = lax.broadcasted_iota(jnp.int32, rows.shape, 1)
    step = 1
    while step < per_group:
        up = pltpu.roll(rows, step, 1)
        down = pltpu.roll(rows, lanes - step, 1)
        rows = rows + jnp.where((at & step) != 0, up, down)
        step *= 2
    return rows


def col_sum(values):
    rows, lanes = values.shape
    return jnp.sum(jnp.sum(values.reshape(rows // 8, 8, lanes), axis=0), axis=0, keepdims=True)


def put_shifted(pad_ref, crop, lanes, values, side):
    pixels = values.shape[0]
    col = lax.broadcasted_iota(jnp.int32, values.shape, 0) % side
    left = jnp.where(col == 0, 0.0, pltpu.roll(values, 1, 0))
    right = jnp.where(col == side - 1, 0.0, pltpu.roll(values, pixels - 1, 0))
    for shift, grid in enumerate((left, values, right)):
        pad_ref[crop, shift, side : side + pixels, lanes] = grid.astype(BF)


def zero_borders(pad_ref, side):
    rows = pad_ref.shape[2]
    edge = jnp.zeros((side, pad_ref.shape[3]), BF)
    for crop in range(pad_ref.shape[0]):
        for shift in range(3):
            pad_ref[crop, shift, 0:side, :] = edge
            pad_ref[crop, shift, rows - side : rows, :] = edge


def pixel_order(pixels, side):
    half = side // 2
    lat = half * half
    row = lax.broadcasted_iota(jnp.int32, (pixels, pixels), 0)
    col = lax.broadcasted_iota(jnp.int32, (pixels, pixels), 1)
    tap, pos = row // lat, row % lat
    at = (2 * (pos // half) + tap // 2) * side + 2 * (pos % half) + tap % 2
    return jnp.where(at == col, 1.0, 0.0).astype(BF)


def chunks(channels):
    return [slice(k, k + 128) for k in range(0, channels, 128)]


def norm_stats(read, crops, pixels, channels, per_group):
    count = float(pixels * per_group)
    result = []
    sums = [
        jnp.concatenate([col_sum(read(c, k)) for k in chunks(channels)], axis=1)
        for c in range(crops)
    ]
    means = [group_sum(s, per_group) * (1.0 / count) for s in sums]
    for c in range(crops):
        parts = []
        for k in chunks(channels):
            d = read(c, k) - means[c][:, k]
            parts.append(col_sum(d * d))
        spread = group_sum(jnp.concatenate(parts, axis=1), per_group) * (1.0 / count)
        result.append((means[c], lax.rsqrt(spread + EPSILON)))
    return result


def conv_apply(pad_ref, crop, w_ref, side, pixels):
    total = None
    for b in range(3):
        rows = jnp.concatenate(
            [pad_ref[crop, b, side * a : side * a + pixels, :] for a in range(3)], axis=1
        )
        part = None
        weight = jnp.concatenate([w_ref[3 * a + b] for a in range(3)], axis=0)
        part = mm(rows, weight)
        total = part if total is None else total + part
    return total


def forward_kernel(
    side,
    x_ref,
    norm_ref,
    w_hbm,
    dn_ref,
    pj_ref,
    conv_ref,
    stats_ref,
    sel_ref,
    red_ref,
    lat_ref,
    w_ref,
    pad_ref,
    sum_ref,
    sem,
):
    crops, pixels, channels = x_ref.shape
    per_group = channels // GROUPS
    copies = [pltpu.make_async_copy(w_hbm.at[k], w_ref.at[k], sem.at[k]) for k in range(2)]
    for copy in copies:
        copy.start()
    zero_borders(pad_ref, side)
    for stage in range(2):
        if stage == 0:

            def read(c, k):
                return x_ref[c, :, k].astype(F32)

        else:

            def read(c, k):
                return conv_ref[c, :, k]

        stats = norm_stats(read, crops, pixels, channels, per_group)
        for c in range(crops):
            mean, inverse = stats[c]
            stats_ref[c, 2 * stage : 2 * stage + 1, :] = mean
            stats_ref[c, 2 * stage + 1 : 2 * stage + 2, :] = inverse
            for k in chunks(channels):
                normed = (read(c, k) - mean[:, k]) * inverse[:, k]
                out = normed * norm_ref[2 * stage : 2 * stage + 1, k]
                out = out + norm_ref[2 * stage + 1 : 2 * stage + 2, k]
                put_shifted(pad_ref, c, k, out * jax.nn.sigmoid(out), side)
        copies[stage].wait()
        for c in range(crops):
            total = conv_apply(pad_ref, c, w_ref.at[stage], side, pixels)
            if stage == 0:
                conv_ref[c] = total
            else:
                sum_ref[c] = (x_ref[c].astype(F32) + total).astype(BF)
    order = pixel_order(pixels, side)
    lat = pixels // 4
    for c in range(crops):
        picked = mm(order, sum_ref[c]).astype(BF)
        for tap in range(4):
            sel_ref[tap, c * lat : (c + 1) * lat, :] = picked[tap * lat : (tap + 1) * lat]
    reduced = mm(sel_ref[0], dn_ref[0])
    for tap in range(1, 4):
        reduced = reduced + mm(sel_ref[tap], dn_ref[tap])
    reduced = reduced.astype(BF)
    red_ref[...] = reduced
    lat_ref[...] = mm(reduced, pj_ref[...]).astype(BF)


def forward_call(x, norm, w, dn, pj, side):
    crops, pixels, channels = x.shape
    tokens = crops * pixels // 4
    flops = 4 * crops * pixels * channels * channels * 9
    return pl.pallas_call(
        functools.partial(forward_kernel, side),
        out_shape=[
            jax.ShapeDtypeStruct((crops, pixels, channels), F32),
            jax.ShapeDtypeStruct((crops, 8, channels), F32),
            jax.ShapeDtypeStruct((4, tokens, channels), BF),
            jax.ShapeDtypeStruct((tokens, channels), BF),
            jax.ShapeDtypeStruct((tokens, pj.shape[1]), BF),
        ],
        in_specs=[vmem(), vmem(), hbm(), vmem(), vmem()],
        out_specs=[vmem()] * 5,
        scratch_shapes=[
            pltpu.VMEM(w.shape, BF),
            pltpu.VMEM((crops, 3, pixels + 2 * side, channels), BF),
            pltpu.VMEM((crops, pixels, channels), BF),
            pltpu.SemaphoreType.DMA((2,)),
        ],
        compiler_params=pltpu.CompilerParams(vmem_limit_bytes=44 * MIB),
        cost_estimate=pl.CostEstimate(
            flops=2 * flops, bytes_accessed=16 * MIB, transcendentals=crops * pixels * channels * 2
        ),
        name="residual_forward",
    )(x, norm, w, dn, pj)


TILE = 1024


def quant_kernel(
    n_shard,
    place_ref,
    lat_ref,
    norms_ref,
    weight_ref,
    cot_ref,
    *rest,
):
    shard_hbm = rest[:n_shard]
    q_ref, g_ref, rows_ref, extra_ref, grad_ref = rest[n_shard : n_shard + 5]
    code_ref, score_ref, stack_ref, res_ref, pick_ref, tot_ref, side_ref, acc_ref, count_ref, sem = (
        rest[n_shard + 5 :]
    )
    tokens, width = lat_ref.shape
    codes = code_ref.shape[0]
    shard = codes // n_shard
    copies = [
        pltpu.make_async_copy(
            shard_hbm[k], code_ref.at[pl.ds(k * shard, shard), :], sem.at[k]
        )
        for k in range(n_shard)
    ]
    for copy in copies:
        copy.start()

    def tiles(first, last, init, fn):
        def step(i, carry):
            return fn(pl.multiple_of(i * TILE, TILE), carry)

        return lax.fori_loop(first // TILE, last // TILE, step, init)

    def fold(values, combine):
        out = values[:, :128]
        for k in range(128, values.shape[1], 128):
            out = combine(out, values[:, k : k + 128])
        return out

    residual = lat_ref[...].astype(F32)
    quantized = jnp.zeros((tokens, width), F32)
    for level in range(DEPTH):
        res_ref[level] = residual
        low = residual.astype(BF)
        rows_ref[level] = low
        scaled = low * jnp.asarray(2.0 * BETA, BF)

        def score(at, best):
            s = mm(scaled, code_ref[pl.ds(at, TILE), :], NT) - norms_ref[:, pl.ds(at, TILE)]
            score_ref[:, pl.ds(at, TILE)] = s
            return jnp.maximum(best, fold(s, jnp.maximum))

        best = jnp.full((tokens, 128), -jnp.inf, F32)
        if level == 0:
            for k in range(n_shard):
                copies[k].wait()
                best = tiles(k * shard, (k + 1) * shard, best, score)
        else:
            best = tiles(0, codes, best, score)
        peak = jnp.max(best, axis=1, keepdims=True)
        acc_ref[...] = jnp.zeros((tokens, width), F32)

        def power(at, total):
            p = jnp.exp(score_ref[:, pl.ds(at, TILE)] - peak)
            low_p = p.astype(BF)
            stack_ref[level * tokens : (level + 1) * tokens, pl.ds(at, TILE)] = low_p
            acc_ref[...] += mm(low_p, code_ref[pl.ds(at, TILE), :])
            return total + fold(p, jnp.add)

        total = tiles(0, codes, jnp.zeros((tokens, 128), F32), power)
        inverse = 1.0 / jnp.sum(total, axis=1, keepdims=True)
        picked = acc_ref[...] * inverse
        pick_ref[level] = picked
        tot_ref[level] = jnp.broadcast_to(inverse, (tokens, 128))
        residual = residual - picked
        quantized = quantized + picked
    q_ref[...] = quantized

    weight = weight_ref[...]
    cot = cot_ref[...].astype(F32)
    count_ref[...] = jnp.zeros(count_ref.shape, F32)
    carry = 2.0 * COMMIT * weight * residual
    for level in reversed(range(DEPTH)):
        inverse = tot_ref[level][:, 0:1]
        grad = cot - carry
        down = (grad * inverse).astype(BF)
        total_grad = -jnp.sum(grad * pick_ref[level], axis=1, keepdims=True) * inverse
        share = weight * inverse
        side_ref[:, level * tokens : (level + 1) * tokens] = grad_t(down)
        side_ref[:, (DEPTH + level) * tokens : (DEPTH + level + 1) * tokens] = grad_t(
            rows_ref[level]
        )
        acc_ref[...] = jnp.zeros((tokens, width), F32)

        def back(at, nothing):
            codes_tile = code_ref[pl.ds(at, TILE), :]
            p = stack_ref[level * tokens : (level + 1) * tokens, pl.ds(at, TILE)].astype(F32)
            ds = (mm(down, codes_tile, NT) + total_grad) * p * (2.0 * BETA)
            inner = ds.astype(BF)
            stack_ref[
                (DEPTH + level) * tokens : (DEPTH + level + 1) * tokens, pl.ds(at, TILE)
            ] = inner
            acc_ref[...] += mm(inner, codes_tile)
            weighted = (p * share).reshape(tokens // 8, 8, TILE)
            count_ref[0, :, pl.ds(at, TILE)] += jnp.sum(weighted, axis=0)
            count_ref[1, :, pl.ds(at, TILE)] += jnp.sum(ds.reshape(tokens // 8, 8, TILE), axis=0)
            return nothing

        tiles(0, codes, 0, back)
        carry = carry + acc_ref[...]
        if level > 0:
            carry = carry + 2.0 * COMMIT * weight * res_ref[level]
    g_ref[...] = carry.astype(BF)
    extra_ref[0:1, :] = jnp.sum(count_ref[0], axis=0, keepdims=True)
    extra_ref[1:2, :] = jnp.sum(count_ref[1], axis=0, keepdims=True)

    n_row = grad_ref.shape[1]
    block = grad_ref.shape[2]
    place = place_ref[0]
    sub = 512
    for k in range(n_shard):

        def out(i, nothing):
            at = pl.multiple_of(i * sub, sub)
            part = mm(side_ref[...], stack_ref[:, pl.ds(k * shard + at, sub)]).astype(BF)
            for r in range(n_row):
                grad_ref[k, r ^ place, :, pl.ds(at, sub)] = part[r * block : (r + 1) * block]
            return nothing

        lax.fori_loop(0, shard // sub, out, 0)


def grad_t(values):
    return values.astype(F32).T.astype(BF)


def quant_call(place, latent, norms, weight, cot, shards, n_row):
    tokens, width = latent.shape
    n_shard = len(shards)
    shard = shards[0].shape[0]
    codes = n_shard * shard
    return pl.pallas_call(
        functools.partial(quant_kernel, n_shard),
        out_shape=[
            jax.ShapeDtypeStruct((tokens, width), F32),
            jax.ShapeDtypeStruct((tokens, width), BF),
            jax.ShapeDtypeStruct((DEPTH, tokens, width), BF),
            jax.ShapeDtypeStruct((2, codes), F32),
            jax.ShapeDtypeStruct((n_shard, n_row, width // n_row, shard), BF),
        ],
        in_specs=[smem(), vmem(), vmem(), vmem(), vmem()] + [hbm()] * n_shard,
        out_specs=[vmem()] * 5,
        scratch_shapes=[
            pltpu.VMEM((codes, width), BF),
            pltpu.VMEM((tokens, codes), F32),
            pltpu.VMEM((2 * DEPTH * tokens, codes), BF),
            pltpu.VMEM((DEPTH, tokens, width), F32),
            pltpu.VMEM((DEPTH, tokens, width), F32),
            pltpu.VMEM((DEPTH, tokens, 128), F32),
            pltpu.VMEM((width, 2 * DEPTH * tokens), BF),
            pltpu.VMEM((tokens, width), F32),
            pltpu.VMEM((2, 8, codes), F32),
            pltpu.SemaphoreType.DMA((n_shard,)),
        ],
        compiler_params=pltpu.CompilerParams(vmem_limit_bytes=63 * MIB),
        cost_estimate=pl.CostEstimate(
            flops=48 * tokens * width * codes,
            bytes_accessed=18 * MIB,
            transcendentals=DEPTH * tokens * codes,
        ),
        name="soft_quantize",
    )(place, latent, norms, weight, cot, *shards)


def slope(values):
    sigma = jax.nn.sigmoid(values)
    return sigma * (1.0 + values * (1.0 - sigma))


def put_blocks(place_ref, outs, n_in, n_out, row, value):
    if len(outs) == 1:
        outs[0][row : row + value.shape[0], :] = value.astype(BF)
        return
    rows = value.shape[0] // n_in
    odd = place_ref[1] % 2 == 1
    line = place_ref[1] // 2
    low = value.astype(BF)
    for pair in range(n_out // 2):
        even = low[:, 256 * pair : 256 * pair + 128]
        other = low[:, 256 * pair + 128 : 256 * pair + 256]
        keep = jnp.where(odd, other, even)
        send = jnp.where(odd, even, other)
        for i in range(n_in):
            at = slice(i * rows, (i + 1) * rows)
            outs[0][pair ^ line, i ^ place_ref[0], row : row + rows, :] = keep[at]
            outs[1][pair ^ line, i ^ place_ref[0], row : row + rows, :] = send[at]


def put_proj(place_ref, outs, n_in, n_out, row, value):
    if len(outs) == 1:
        outs[0][row : row + value.shape[0], 0 : value.shape[1]] = value.astype(BF)
        outs[0][row : row + value.shape[0], value.shape[1] :] = jnp.zeros(value.shape, BF)
        return
    channels, width = value.shape
    rows = channels // n_in
    cols = width // n_out
    folded = []
    for i in range(n_in):
        top = value[i * rows : i * rows + rows // 2]
        low = value[i * rows + rows // 2 : (i + 1) * rows]
        folded.append(
            jnp.concatenate(
                [
                    part[:, c * cols : (c + 1) * cols]
                    for c in range(n_out)
                    for part in (top, low)
                ],
                axis=1,
            )
        )
    put_blocks(place_ref, outs, n_in, n_out, row, jnp.concatenate(folded, axis=0))


def norm_back(grad, normed, inverse, gain, per_group, count):
    dn = grad * gain
    first = group_sum(col_sum(dn), per_group) * (1.0 / count)
    second = group_sum(col_sum(dn * normed), per_group) * (1.0 / count)
    return inverse * (dn - first - normed * second)


def conv_back_image(pad_ref, crop, w_ref, side, pixels):
    total = None
    for tap in range(9):
        a, b = tap // 3, tap % 3
        rows = pad_ref[crop, 2 - b, side * (2 - a) : side * (2 - a) + pixels, :]
        part = mm(rows, w_ref[tap], NT)
        total = part if total is None else total + part
    return total


def conv_back_weight(pad_ref, crops, grad, side, pixels, store):
    for tap in range(9):
        a, b = tap // 3, tap % 3
        rows = jnp.concatenate(
            [pad_ref[c, b, side * a : side * a + pixels, :] for c in range(crops)], axis=0
        )
        store(tap, mm(rows, grad, TN))


def act_shifted(pad_ref, read, stats_ref, norm_ref, stage, crops, channels, side):
    for c in range(crops):
        for k in chunks(channels):
            normed = (read(c, k) - stats_ref[c, 2 * stage : 2 * stage + 1, k]) * stats_ref[
                c, 2 * stage + 1 : 2 * stage + 2, k
            ]
            out = normed * norm_ref[2 * stage : 2 * stage + 1, k]
            out = out + norm_ref[2 * stage + 1 : 2 * stage + 2, k]
            put_shifted(pad_ref, c, k, out * jax.nn.sigmoid(out), side)


def act_back(read, dact_ref, stats_ref, norm_ref, stage, crops, pixels, channels, grads_ref, store):
    per_group = channels // GROUPS
    count = float(pixels * per_group)
    for k in chunks(channels):
        gain_row = norm_ref[2 * stage : 2 * stage + 1, k]
        bias_row = norm_ref[2 * stage + 1 : 2 * stage + 2, k]
        grad_gain = jnp.zeros((1, 128), F32)
        grad_bias = jnp.zeros((1, 128), F32)
        for c in range(crops):
            inverse = stats_ref[c, 2 * stage + 1 : 2 * stage + 2, k]
            normed = (read(c, k) - stats_ref[c, 2 * stage : 2 * stage + 1, k]) * inverse
            dout = dact_ref[c, :, k] * slope(normed * gain_row + bias_row)
            grad_gain = grad_gain + col_sum(dout * normed)
            grad_bias = grad_bias + col_sum(dout)
            store(c, k, norm_back(dout, normed, inverse, gain_row, per_group, count))
        grads_ref[0:1, k] = grad_gain
        grads_ref[1:2, k] = grad_bias


def second_kernel(
    side,
    n_out_refs,
    n_in,
    n_out,
    place_ref,
    dlat_ref,
    red_ref,
    sel_ref,
    dn_ref,
    pj_ref,
    conv_ref,
    stats_ref,
    norm_ref,
    w_hbm,
    *rest,
):
    outs = rest[:n_out_refs]
    dsum_ref, dconv_ref, ngrad_ref, w_ref, apad_ref, dpad_ref, dact_ref, sem = rest[n_out_refs:]
    crops, pixels, channels = conv_ref.shape
    copy = pltpu.make_async_copy(w_hbm.at[1], w_ref, sem.at[0])
    copy.start()
    zero_borders(apad_ref, side)
    zero_borders(dpad_ref, side)
    rows = channels // n_in if n_out_refs == 2 else channels
    lat = pixels // 4

    def read(c, k):
        return conv_ref[c, :, k]

    dlat = dlat_ref[...]
    dred = mm(dlat, pj_ref[...], NT).astype(BF)
    order = pixel_order(pixels, side)
    pieces = [mm(dred, dn_ref[tap], NT).astype(BF) for tap in range(4)]
    for c in range(crops):
        mixed = jnp.concatenate([p[c * lat : (c + 1) * lat] for p in pieces], axis=0)
        dsum_ref[c] = mm(order, mixed, TN).astype(BF)
        for k in chunks(channels):
            put_shifted(dpad_ref, c, k, dsum_ref[c, :, k].astype(F32), side)
    copy.wait()
    for c in range(crops):
        dact_ref[c] = conv_back_image(dpad_ref, c, w_ref, side, pixels)

    def store(c, k, value):
        dconv_ref[c, :, k] = value.astype(BF)

    ngrad_ref[...] = jnp.zeros(ngrad_ref.shape, F32)
    act_back(read, dact_ref, stats_ref, norm_ref, 1, crops, pixels, channels, ngrad_ref, store)
    act_shifted(apad_ref, read, stats_ref, norm_ref, 1, crops, channels, side)
    grad = jnp.concatenate([dsum_ref[c] for c in range(crops)], axis=0)
    conv_back_weight(
        apad_ref,
        crops,
        grad,
        side,
        pixels,
        lambda tap, v: put_blocks(place_ref, outs, n_in, n_out, tap * rows, v),
    )
    for tap in range(4):
        put_blocks(place_ref, outs, n_in, n_out, (9 + tap) * rows, mm(sel_ref[tap], dred, TN))
    put_proj(place_ref, outs, n_in, n_out, 13 * rows, mm(red_ref[...], dlat, TN))


def first_weight_kernel(
    side, n_out_refs, n_in, n_out, place_ref, x_ref, stats_ref, norm_ref, dconv_ref, *rest
):
    outs = rest[:n_out_refs]
    (apad_ref,) = rest[n_out_refs:]
    crops, pixels, channels = x_ref.shape
    rows = channels // n_in if n_out_refs == 2 else channels
    zero_borders(apad_ref, side)

    def read(c, k):
        return x_ref[c, :, k].astype(F32)

    act_shifted(apad_ref, read, stats_ref, norm_ref, 0, crops, channels, side)
    grad = jnp.concatenate([dconv_ref[c] for c in range(crops)], axis=0)
    conv_back_weight(
        apad_ref,
        crops,
        grad,
        side,
        pixels,
        lambda tap, v: put_blocks(place_ref, outs, n_in, n_out, tap * rows, v),
    )


def first_image_kernel(
    side,
    n_part,
    place_ref,
    x_ref,
    stats_ref,
    norm_ref,
    dconv_ref,
    dsum_ref,
    w_hbm,
    *rest,
):
    part_refs = rest[:n_part]
    ngrad_ref, w_ref, dpad_ref, dact_ref, image_ref, sem = rest[n_part:]
    crops, pixels, channels = x_ref.shape
    copy = pltpu.make_async_copy(w_hbm.at[0], w_ref, sem.at[0])
    copy.start()
    zero_borders(dpad_ref, side)
    for c in range(crops):
        for k in chunks(channels):
            put_shifted(dpad_ref, c, k, dconv_ref[c, :, k].astype(F32), side)
    copy.wait()
    for c in range(crops):
        dact_ref[c] = conv_back_image(dpad_ref, c, w_ref, side, pixels)

    def read(c, k):
        return x_ref[c, :, k].astype(F32)

    def store(c, k, value):
        image_ref[c, :, k] = (value + dsum_ref[c, :, k].astype(F32)).astype(BF)

    ngrad_ref[...] = jnp.zeros(ngrad_ref.shape, F32)
    act_back(read, dact_ref, stats_ref, norm_ref, 0, crops, pixels, channels, ngrad_ref, store)
    span = pixels // n_part
    for k in range(n_part):
        if n_part == 1:
            part_refs[k][...] = image_ref[...]
        else:
            at = pl.multiple_of((place_ref[0] ^ k) * span, span)
            for c in range(crops):
                part_refs[k][c] = image_ref[c, pl.ds(at, span), :]


def conv_cost(crops, pixels, channels, convs):
    return pl.CostEstimate(
        flops=convs * 18 * crops * pixels * channels * channels,
        bytes_accessed=12 * MIB,
        transcendentals=crops * pixels * channels,
    )


def grad_shapes(halves, n_in, n_out, channels, units):
    if not halves:
        return [jax.ShapeDtypeStruct((units[0] * channels, channels), BF)]
    rows = channels // n_in
    shape = (n_out // 2, n_in, units[0] * rows + units[1], channels // n_out)
    return [jax.ShapeDtypeStruct(shape, BF)] * 2


def second_call(place, dlat, red, sel, dn, pj, conv, stats, norm, w, side, halves, n_in, n_out):
    crops, pixels, channels = conv.shape
    if halves:
        fold = channels // n_in * pj.shape[1] // channels
        grads = grad_shapes(True, n_in, n_out, channels, (13, fold))
    else:
        grads = grad_shapes(False, n_in, n_out, channels, (14, 0))
    pad = (crops, 3, pixels + 2 * side, channels)
    return pl.pallas_call(
        functools.partial(second_kernel, side, len(grads), n_in, n_out),
        out_shape=grads
        + [
            jax.ShapeDtypeStruct(conv.shape, BF),
            jax.ShapeDtypeStruct(conv.shape, BF),
            jax.ShapeDtypeStruct((8, channels), F32),
        ],
        in_specs=[smem()] + [vmem()] * 8 + [hbm()],
        out_specs=[vmem()] * (len(grads) + 3),
        scratch_shapes=[
            pltpu.VMEM(w.shape[1:], BF),
            pltpu.VMEM(pad, BF),
            pltpu.VMEM(pad, BF),
            pltpu.VMEM(conv.shape, F32),
            pltpu.SemaphoreType.DMA((1,)),
        ],
        compiler_params=pltpu.CompilerParams(vmem_limit_bytes=44 * MIB),
        cost_estimate=conv_cost(crops, pixels, channels, 2),
        name="second_backward",
    )(place, dlat, red, sel, dn, pj, conv, stats, norm, w)


def first_weight_call(place, x, stats, norm, dconv, side, halves, n_in, n_out):
    crops, pixels, channels = x.shape
    grads = grad_shapes(halves, n_in, n_out, channels, (9, 0))
    return pl.pallas_call(
        functools.partial(first_weight_kernel, side, len(grads), n_in, n_out),
        out_shape=grads,
        in_specs=[smem()] + [vmem()] * 4,
        out_specs=[vmem()] * len(grads),
        scratch_shapes=[pltpu.VMEM((crops, 3, pixels + 2 * side, channels), BF)],
        compiler_params=pltpu.CompilerParams(vmem_limit_bytes=44 * MIB),
        cost_estimate=conv_cost(crops, pixels, channels, 1),
        name="first_weight_backward",
    )(place, x, stats, norm, dconv)


def first_image_call(place, x, stats, norm, dconv, dsum, w, side, n_part):
    crops, pixels, channels = x.shape
    return pl.pallas_call(
        functools.partial(first_image_kernel, side, n_part),
        out_shape=[jax.ShapeDtypeStruct((crops, pixels // n_part, channels), BF)] * n_part
        + [jax.ShapeDtypeStruct((8, channels), F32)],
        in_specs=[smem()] + [vmem()] * 5 + [hbm()],
        out_specs=[vmem()] * (n_part + 1),
        scratch_shapes=[
            pltpu.VMEM(w.shape[1:], BF),
            pltpu.VMEM((crops, 3, pixels + 2 * side, channels), BF),
            pltpu.VMEM(x.shape, F32),
            pltpu.VMEM(x.shape, BF),
            pltpu.SemaphoreType.DMA((1,)),
        ],
        compiler_params=pltpu.CompilerParams(vmem_limit_bytes=44 * MIB),
        cost_estimate=conv_cost(crops, pixels, channels, 1),
        name="first_image_backward",
    )(place, x, stats, norm, dconv, dsum, w)


def swap(array, axis, bit):
    count = lax.axis_size(axis)
    return lax.ppermute(array, axis, [(i, i ^ bit) for i in range(count)])


def add_low(first, second):
    return (first.astype(F32) + second.astype(F32)).astype(BF)


ORDERS = (("x", "y", "z1", "z2"), ("y", "z1", "x", "z2"), ("z1", "x", "y", "z2"))
LINKS = {"x": ("code", 2), "y": ("dp", 1), "z1": ("dp", 2), "z2": ("dp", 4)}


def halve_all(part, order, dims):
    dims = list(dims)
    for name in order:
        if name not in dims:
            continue
        at = dims.index(name)
        axis, bit = LINKS[name]
        mine = lax.index_in_dim(part, 0, at, keepdims=False)
        theirs = lax.index_in_dim(part, 1, at, keepdims=False)
        part = add_low(mine, swap(theirs, axis, bit))
        dims.pop(at)
    return part


def thirds(total, unit):
    units = total // unit
    cuts = [0, (units + 2) // 3 * unit, (units + 2) // 3 * unit + (units + 1) // 3 * unit, total]
    return [(cuts[k], cuts[k + 1]) for k in range(3)]


def nesterov_step(master, moment, average, grad, rate):
    moment_new = MOMENTUM * moment + grad
    master_new = master - rate * (grad + MOMENTUM * moment_new)
    return (moment_new, master_new, AVERAGE_DECAY * average + (1.0 - AVERAGE_DECAY) * master_new)


def body(
    crops_in,
    crop_weight,
    cotangent,
    conv_copy,
    down_copy,
    proj_copy,
    norm_copy,
    codebook,
    conv_master,
    conv_moment,
    conv_average,
    down_master,
    down_moment,
    down_average,
    proj_master,
    proj_moment,
    proj_average,
    norm_master,
    norm_moment,
    norm_average,
    code_master,
    code_moment,
    code_average,
    repl_code,
    repl_src,
):
    dp_count = lax.axis_size("dp")
    code_count = lax.axis_size("code")
    dp_at = lax.axis_index("dp")
    code_at = lax.axis_index("code")
    halves = dp_count == 8 and code_count == 4
    place = jnp.stack([dp_at, code_at]).astype(jnp.int32)

    local = lax.all_to_all(crops_in, "dp", split_axis=1, concat_axis=2, tiled=True)[0]
    crop_dev, pixels, channels = local.shape
    side = math.isqrt(pixels)
    lat = pixels // 4
    tokens = crop_dev * lat
    width = proj_copy.shape[1]
    code_dev = codebook.shape[0]
    codes_all = code_dev * code_count

    codes_wide = codebook.astype(F32)
    norms = BETA * jnp.sum(codes_wide * codes_wide, axis=1)
    if halves:
        shards, norm_rows = [codebook], [norms]
        for bit in (1, 2, 3):
            shards.append(swap(codebook, "code", bit))
            norm_rows.append(swap(norms, "code", bit))
        norms_all = jnp.concatenate(norm_rows)
    else:
        every = lax.all_gather(codebook, "code", axis=0)
        shards = [every[k] for k in range(code_count)]
        norms_all = lax.all_gather(norms, "code", axis=0, tiled=True)

    w = conv_copy.transpose(1, 2, 0, 3)
    dn = down_copy.transpose(1, 0, 2)
    gains = norm_copy.T.astype(F32)
    conv1, stats, sel, reduced, latent = forward_call(local, gains, w, dn, proj_copy, side)

    weight_col = jnp.broadcast_to(
        crop_weight.astype(F32).reshape(crop_dev, 1), (crop_dev, lat)
    ).reshape(tokens, 1)
    n_row = dp_count if halves else 1
    place_q = place if halves else jnp.zeros_like(place)
    quantized, dlat, rows, extra, code_grads = quant_call(
        place_q,
        latent,
        norms_all.reshape(1, codes_all),
        weight_col,
        cotangent.reshape(tokens, width),
        shards,
        n_row,
    )

    second = second_call(
        place, dlat, reduced, sel, dn, proj_copy, conv1, stats, gains, w, side, halves, dp_count,
        code_count,
    )
    grads_second, (dsum, dconv, ngrad_second) = second[:-3], second[-3:]
    grads_first = first_weight_call(
        place, local, stats, gains, dconv, side, halves, dp_count, code_count
    )
    image = first_image_call(
        place, local, stats, gains, dconv, dsum, w, side, dp_count if halves else 1
    )
    image_parts, ngrad_first = image[:-1], image[-1]

    crops_set = crop_dev * dp_count
    flat_src = repl_src.reshape(-1)
    crop_id = flat_src // lat % crops_set
    owner = (crop_id // crop_dev == dp_at) & (flat_src // (crops_set * lat) == code_at)
    row_id = crop_id % crop_dev * lat + flat_src % lat
    depth_id = jnp.repeat(jnp.arange(DEPTH, dtype=jnp.int32), repl_src.shape[1])
    flat_rows = rows.reshape(DEPTH * tokens, width)
    pick = (
        jnp.where(owner, depth_id * tokens + row_id, -1)[:, None]
        == jnp.arange(DEPTH * tokens, dtype=jnp.int32)[None, :]
    ).astype(BF)
    source = mm(flat_rows, pick, (((0,), (1,)), ((), ()))).astype(BF)

    norm_grad = jnp.concatenate([ngrad_first[0:2], ngrad_second[0:2]], axis=0)

    if halves:
        def by_bits(array, lead):
            return array.reshape(array.shape[:lead] + (2, 2, 2) + array.shape[lead + 1 :])

        keep_own = add_low(code_grads[0], swap(code_grads[1], "code", 1))
        keep_far = add_low(code_grads[2], swap(code_grads[3], "code", 1))
        pieces = []
        for k, (low, high) in enumerate(thirds(code_dev, 128)):
            part = jnp.stack([keep_own[:, :, low:high], keep_far[:, :, low:high]])
            part = part.reshape((2, 2, 2, 2) + part.shape[2:])
            pieces.append(halve_all(part, ORDERS[k], ("x", "z2", "z1", "y")))
        code_grad = jnp.concatenate(pieces, axis=1).astype(F32)

        rows_x = extra.reshape(2, code_count, code_dev)
        near = rows_x[:, 0] + swap(rows_x[:, 1], "code", 1)
        far = rows_x[:, 2] + swap(rows_x[:, 3], "code", 1)
        sums = near + swap(far, "code", 2)
        for bit in (1, 2, 4):
            sums = sums + swap(sums, "dp", bit)

        start = dp_at * (width // dp_count)
        block = source.reshape(2, 2, 2, width // dp_count, source.shape[1])
        bits = [(dp_at >> 2) & 1, (dp_at >> 1) & 1, dp_at & 1]
        for bit, at in zip((4, 2, 1), bits):
            mine = lax.dynamic_index_in_dim(block, at, 0, keepdims=False)
            theirs = lax.dynamic_index_in_dim(block, 1 - at, 0, keepdims=False)
            block = add_low(mine, swap(theirs, "dp", bit))
        for bit in (1, 2):
            block = add_low(block, swap(block, "code", bit))
        source_rows = block

        def matrix(keep, send):
            total = add_low(keep, swap(send, "code", 1))
            total = total.reshape((2, 2, 2, 2) + total.shape[2:])
            pieces = []
            for k, (low, high) in enumerate(thirds(total.shape[4], 16)):
                pieces.append(
                    halve_all(total[:, :, :, :, low:high], ORDERS[k], ("x", "z2", "z1", "y"))
                )
            return jnp.concatenate(pieces, axis=0).astype(F32)

        rows_in = channels // dp_count
        out_dev = channels // code_count
        mat_second = matrix(*grads_second)
        mat_first = matrix(*grads_first)
        conv_part = jnp.stack(
            [
                mat_first.reshape(9, rows_in, out_dev),
                mat_second[: 9 * rows_in].reshape(9, rows_in, out_dev),
            ]
        ).transpose(2, 0, 1, 3)
        down_part = (
            mat_second[9 * rows_in : 13 * rows_in].reshape(4, rows_in, out_dev).transpose(1, 0, 2)
        )
        fold = mat_second[13 * rows_in :]
        proj_part = jnp.concatenate([fold[:, : out_dev // 2], fold[:, out_dev // 2 :]], axis=0)

        total = norm_grad
        for axis, bit in (("code", 1), ("code", 2), ("dp", 1), ("dp", 2), ("dp", 4)):
            total = total + swap(total, axis, bit)
        norm_grad = total

        parts = [image_parts[0]] + [swap(image_parts[k], "dp", k) for k in range(1, dp_count)]
        input_back = jnp.zeros((crop_dev * dp_count, pixels // dp_count, channels), F32)
        for k, part in enumerate(parts):
            input_back = lax.dynamic_update_slice(
                input_back, part.astype(F32), ((dp_at ^ k) * crop_dev, 0, 0)
            )
        input_back = input_back[None]
    else:
        flat = code_grads.reshape(code_count, width, code_dev)
        flat = lax.psum_scatter(flat, "code", scatter_dimension=0, tiled=True)[0]
        code_grad = lax.psum_scatter(flat, "dp", scatter_dimension=0, tiled=True).astype(F32)
        sums = lax.psum_scatter(extra, "code", scatter_dimension=1, tiled=True)
        sums = lax.psum(sums, "dp")
        source_rows = lax.psum_scatter(source, "dp", scatter_dimension=0, tiled=True)
        source_rows = lax.psum(source_rows, "code")

        def matrix(array, scatter):
            array = lax.psum_scatter(array, "dp", scatter_dimension=0, tiled=True)
            return lax.psum_scatter(array, "code", scatter_dimension=scatter, tiled=True).astype(F32)

        conv_flat = jnp.stack(
            [
                grads_first[0].reshape(9, channels, channels),
                grads_second[0][: 9 * channels].reshape(9, channels, channels),
            ]
        ).transpose(2, 0, 1, 3)
        conv_part = matrix(conv_flat, 3)
        down_flat = grads_second[0][9 * channels : 13 * channels]
        down_part = matrix(down_flat.reshape(4, channels, channels).transpose(1, 0, 2), 2)
        proj_part = matrix(grads_second[0][13 * channels :, :width], 1)
        norm_grad = lax.psum(norm_grad, ("dp", "code"))
        input_back = lax.all_to_all(
            image_parts[0][None], "dp", split_axis=2, concat_axis=1, tiled=True
        ).astype(F32)

    pixels_all = crop_dev * pixels * dp_count * code_count
    weight_rate = WEIGHT_RATE / math.sqrt(pixels_all)
    norm_rate = NORM_RATE / math.sqrt(pixels_all)
    crops_all = crop_dev * dp_count * code_count
    mean_count = DEPTH * lat * crops_all / codes_all
    code_rate = CODE_RATE / math.sqrt(mean_count)
    conv_out = nesterov_step(conv_master, conv_moment, conv_average, conv_part, weight_rate)
    down_out = nesterov_step(down_master, down_moment, down_average, down_part, weight_rate)
    proj_out = nesterov_step(proj_master, proj_moment, proj_average, proj_part, weight_rate)
    norm_out = nesterov_step(norm_master, norm_moment, norm_average, norm_grad.T, norm_rate)

    counts_all, slope_sum = sums[0], sums[1]
    share = mean_count / (mean_count + counts_all)
    code_load = counts_all / mean_count
    cols = width // dp_count
    own_codes = lax.dynamic_slice_in_dim(codebook, dp_at * cols, cols, 1).T.astype(F32)
    code_grad = code_grad - own_codes * slope_sum[None, :]
    code_moment_new = MOMENTUM * code_moment.T + code_grad
    stepped = code_master.T - code_rate * (code_grad + MOMENTUM * code_moment_new)
    select = (
        repl_code.reshape(-1)[:, None] - code_at * code_dev
        == jnp.arange(code_dev, dtype=jnp.int32)[None, :]
    )
    chosen = jnp.sum(select.astype(F32), axis=0)
    renewed = mm(source_rows, select.astype(BF))
    code_master_new = stepped + (chosen * share)[None, :] * (renewed - stepped)
    code_average_new = AVERAGE_DECAY * code_average.T + (1.0 - AVERAGE_DECAY) * code_master_new
    return (
        quantized.reshape(1, crop_dev, lat, width),
        input_back,
        *conv_out,
        *down_out,
        *proj_out,
        *norm_out,
        code_moment_new.T,
        code_master_new.T,
        code_average_new.T,
        code_load,
    )


def solution(mesh):
    in_specs = (
        P("code", None, "dp", None),
        P("code", "dp"),
        P("code", "dp", None, None),
        P(),
        P(),
        P(),
        P(),
        P("code", None),
        P("dp", None, None, "code"),
        P("dp", None, None, "code"),
        P("dp", None, None, "code"),
        P("dp", None, "code"),
        P("dp", None, "code"),
        P("dp", None, "code"),
        P("dp", "code"),
        P("dp", "code"),
        P("dp", "code"),
        P(),
        P(),
        P(),
        P("code", "dp"),
        P("code", "dp"),
        P("code", "dp"),
        P(),
        P(),
    )
    out_specs = (
        P("code", "dp", None, None),
        P("code", None, "dp", None),
        P("dp", None, None, "code"),
        P("dp", None, None, "code"),
        P("dp", None, None, "code"),
        P("dp", None, "code"),
        P("dp", None, "code"),
        P("dp", None, "code"),
        P("dp", "code"),
        P("dp", "code"),
        P("dp", "code"),
        P(),
        P(),
        P(),
        P("code", "dp"),
        P("code", "dp"),
        P("code", "dp"),
        P("code"),
    )
    return jax.shard_map(body, mesh=mesh, in_specs=in_specs, out_specs=out_specs, check_vma=False)
```

```python
import functools
import math

import jax
import jax.numpy as jnp
from jax import lax
from jax.experimental import pallas as pl
from jax.experimental.pallas import tpu as pltpu
from jax.sharding import PartitionSpec as P

GROUPS = 32
DEPTH = 4
BETA = 0.0625
EPSILON = 1e-05
MOMENTUM = 0.5
AVERAGE_DECAY = 0.5
COMMIT = 0.25
WEIGHT_RATE = 0.05
NORM_RATE = 0.5
CODE_RATE = 0.5

BF = jnp.bfloat16
F32 = jnp.float32
NT = (((1,), (1,)), ((), ()))
NN = (((1,), (0,)), ((), ()))
TN = (((0,), (0,)), ((), ()))
MIB = 1 << 20


def mm(a, b, dims=NN):
    return lax.dot_general(a, b, dims, preferred_element_type=F32)


def vmem():
    return pl.BlockSpec(memory_space=pltpu.VMEM)


def smem():
    return pl.BlockSpec(memory_space=pltpu.SMEM)


def hbm():
    return pl.BlockSpec(memory_space=pl.ANY)


def group_sum(rows, per_group):
    lanes = rows.shape[1]
    at = lax.broadcasted_iota(jnp.int32, rows.shape, 1)
    step = 1
    while step < per_group:
        up = pltpu.roll(rows, step, 1)
        down = pltpu.roll(rows, lanes - step, 1)
        rows = rows + jnp.where((at & step) != 0, up, down)
        step *= 2
    return rows


def col_sum(values):
    rows, lanes = values.shape
    return jnp.sum(jnp.sum(values.reshape(rows // 8, 8, lanes), axis=0), axis=0, keepdims=True)


def put_shifted(pad_ref, crop, lanes, values, side):
    pixels = values.shape[0]
    col = lax.broadcasted_iota(jnp.int32, values.shape, 0) % side
    left = jnp.where(col == 0, 0.0, pltpu.roll(values, 1, 0))
    right = jnp.where(col == side - 1, 0.0, pltpu.roll(values, pixels - 1, 0))
    for shift, grid in enumerate((left, values, right)):
        pad_ref[crop, shift, side : side + pixels, lanes] = grid.astype(BF)


def zero_borders(pad_ref, side):
    rows = pad_ref.shape[2]
    edge = jnp.zeros((side, pad_ref.shape[3]), BF)
    for crop in range(pad_ref.shape[0]):
        for shift in range(3):
            pad_ref[crop, shift, 0:side, :] = edge
            pad_ref[crop, shift, rows - side : rows, :] = edge


def pixel_order(pixels, side):
    half = side // 2
    lat = half * half
    row = lax.broadcasted_iota(jnp.int32, (pixels, pixels), 0)
    col = lax.broadcasted_iota(jnp.int32, (pixels, pixels), 1)
    tap, pos = row // lat, row % lat
    at = (2 * (pos // half) + tap // 2) * side + 2 * (pos % half) + tap % 2
    return jnp.where(at == col, 1.0, 0.0).astype(BF)


def chunks(channels):
    return [slice(k, k + 128) for k in range(0, channels, 128)]


def norm_stats(read, crops, pixels, channels, per_group):
    count = float(pixels * per_group)
    result = []
    sums = [
        jnp.concatenate([col_sum(read(c, k)) for k in chunks(channels)], axis=1)
        for c in range(crops)
    ]
    means = [group_sum(s, per_group) * (1.0 / count) for s in sums]
    for c in range(crops):
        parts = []
        for k in chunks(channels):
            d = read(c, k) - means[c][:, k]
            parts.append(col_sum(d * d))
        spread = group_sum(jnp.concatenate(parts, axis=1), per_group) * (1.0 / count)
        result.append((means[c], lax.rsqrt(spread + EPSILON)))
    return result


def conv_apply(pad_ref, crop, w_ref, side, pixels):
    total = None
    for b in range(3):
        rows = jnp.concatenate(
            [pad_ref[crop, b, side * a : side * a + pixels, :] for a in range(3)], axis=1
        )
        part = None
        weight = jnp.concatenate([w_ref[3 * a + b] for a in range(3)], axis=0)
        part = mm(rows, weight)
        total = part if total is None else total + part
    return total


def forward_kernel(
    side,
    x_ref,
    norm_ref,
    w_hbm,
    dn_ref,
    pj_ref,
    conv_ref,
    stats_ref,
    sel_ref,
    red_ref,
    lat_ref,
    w_ref,
    pad_ref,
    sum_ref,
    sem,
):
    crops, pixels, channels = x_ref.shape
    per_group = channels // GROUPS
    copies = [pltpu.make_async_copy(w_hbm.at[k], w_ref.at[k], sem.at[k]) for k in range(2)]
    for copy in copies:
        copy.start()
    zero_borders(pad_ref, side)
    for stage in range(2):
        if stage == 0:

            def read(c, k):
                return x_ref[c, :, k].astype(F32)

        else:

            def read(c, k):
                return conv_ref[c, :, k]

        stats = norm_stats(read, crops, pixels, channels, per_group)
        for c in range(crops):
            mean, inverse = stats[c]
            stats_ref[c, 2 * stage : 2 * stage + 1, :] = mean
            stats_ref[c, 2 * stage + 1 : 2 * stage + 2, :] = inverse
            for k in chunks(channels):
                normed = (read(c, k) - mean[:, k]) * inverse[:, k]
                out = normed * norm_ref[2 * stage : 2 * stage + 1, k]
                out = out + norm_ref[2 * stage + 1 : 2 * stage + 2, k]
                put_shifted(pad_ref, c, k, out * jax.nn.sigmoid(out), side)
        copies[stage].wait()
        for c in range(crops):
            total = conv_apply(pad_ref, c, w_ref.at[stage], side, pixels)
            if stage == 0:
                conv_ref[c] = total
            else:
                sum_ref[c] = (x_ref[c].astype(F32) + total).astype(BF)
    order = pixel_order(pixels, side)
    lat = pixels // 4
    for c in range(crops):
        picked = mm(order, sum_ref[c]).astype(BF)
        for tap in range(4):
            sel_ref[tap, c * lat : (c + 1) * lat, :] = picked[tap * lat : (tap + 1) * lat]
    reduced = mm(sel_ref[0], dn_ref[0])
    for tap in range(1, 4):
        reduced = reduced + mm(sel_ref[tap], dn_ref[tap])
    reduced = reduced.astype(BF)
    red_ref[...] = reduced
    lat_ref[...] = mm(reduced, pj_ref[...]).astype(BF)


def forward_call(x, norm, w, dn, pj, side):
    crops, pixels, channels = x.shape
    tokens = crops * pixels // 4
    flops = 4 * crops * pixels * channels * channels * 9
    return pl.pallas_call(
        functools.partial(forward_kernel, side),
        out_shape=[
            jax.ShapeDtypeStruct((crops, pixels, channels), F32),
            jax.ShapeDtypeStruct((crops, 8, channels), F32),
            jax.ShapeDtypeStruct((4, tokens, channels), BF),
            jax.ShapeDtypeStruct((tokens, channels), BF),
            jax.ShapeDtypeStruct((tokens, pj.shape[1]), BF),
        ],
        in_specs=[vmem(), vmem(), hbm(), vmem(), vmem()],
        out_specs=[vmem()] * 5,
        scratch_shapes=[
            pltpu.VMEM(w.shape, BF),
            pltpu.VMEM((crops, 3, pixels + 2 * side, channels), BF),
            pltpu.VMEM((crops, pixels, channels), BF),
            pltpu.SemaphoreType.DMA((2,)),
        ],
        compiler_params=pltpu.CompilerParams(vmem_limit_bytes=44 * MIB),
        cost_estimate=pl.CostEstimate(
            flops=2 * flops, bytes_accessed=16 * MIB, transcendentals=crops * pixels * channels * 2
        ),
        name="residual_forward",
    )(x, norm, w, dn, pj)


TILE = 1024
SUB = 1024
SPAN = 4096


def quant_kernel(n_shard, halves, n_piece, place_ref, lat_ref, weight_ref, cot_ref, pick_ref, *rest):
    shard_hbm = rest[:n_piece]
    n_out = 6 if halves else 5
    q_ref, g_ref, rows_ref, extra_ref = rest[n_piece : n_piece + 4]
    grad_hbm = rest[n_piece + 4 : n_piece + n_out]
    (
        code_ref,
        codet_ref,
        score_ref,
        stack_ref,
        res_ref,
        q_level_ref,
        fac_ref,
        side_ref,
        acc_ref,
        count_ref,
        norms_ref,
        carry_ref,
        stage_ref,
        more_ref,
        in_sem,
        out_sem,
        more_sem,
    ) = rest[n_piece + n_out :]
    tokens, width = lat_ref.shape
    codes = code_ref.shape[0]
    shard = codes // n_shard
    part = codes // 2
    tile = min(TILE, part)
    near = place_ref[0] % 2

    starts = []
    if halves:
        half, quarter = shard // 2, shard // 4
        starts = [0, shard]
        for base in (2 * shard, 3 * shard):
            for side in (near, 1 - near):
                for k in range(2):
                    starts.append(base + side * half + k * quarter)
    else:
        starts = [k * shard for k in range(n_shard)]
    copies = [
        pltpu.make_async_copy(
            shard_hbm[k],
            code_ref.at[pl.ds(pl.multiple_of(starts[k], 256), shard_hbm[k].shape[0]), :],
            in_sem.at[k],
        )
        for k in range(n_piece)
    ]
    for copy in copies:
        copy.start()

    def fold(values, combine):
        out = values[:, :128]
        for k in range(128, values.shape[1], 128):
            out = combine(out, values[:, k : k + 128])
        return out

    def level_forward(level, first):
        residual = res_ref[level]
        low = residual.astype(BF)
        rows_ref[level] = low
        scaled = low * jnp.asarray(2.0 * BETA, BF)
        at_row = pl.multiple_of(level * tokens, tokens)
        peaks, sums, picks = [], [], []
        for h in range(2):
            best = jnp.full((tokens, 128), -jnp.inf, F32)
            for k in range(part // tile):
                at = h * part + k * tile
                lanes = slice(at, at + tile)
                if first:
                    if halves:
                        if at % shard == 0:
                            group = at // shard
                            for piece in ([group] if group < 2 else range(4 * group - 6, 4 * group - 2)):
                                copies[piece].wait()
                    else:
                        if at % shard == 0:
                            copies[at // shard].wait()
                    for j in range(at, at + tile, 512):
                        turned = code_ref[j : j + 512, :].T
                        codet_ref[:, j : j + 512] = turned
                        wide = turned.astype(F32)
                        norms_ref[:, j : j + 512] = BETA * col_sum(wide * wide)
                s = mm(scaled, codet_ref[:, lanes]) - norms_ref[:, lanes]
                score_ref[:, k * tile : (k + 1) * tile] = s
                best = jnp.maximum(best, fold(s, jnp.maximum))
            peak = jnp.max(best, axis=1, keepdims=True)
            acc_ref[h] = jnp.zeros((tokens, width), F32)

            def power(i, total):
                for k in range(SPAN // tile):
                    at = pl.multiple_of(i * SPAN + k * tile, tile)
                    lanes = pl.ds(pl.multiple_of(h * part + at, tile), tile)
                    p = jnp.exp(score_ref[:, pl.ds(at, tile)] - peak)
                    low_p = p.astype(BF)
                    stack_ref[pl.ds(at_row, tokens), lanes] = low_p
                    acc_ref[h] += mm(low_p, code_ref[lanes, :])
                    total = total + fold(p, jnp.add)
                return total

            total = lax.fori_loop(0, part // SPAN, power, jnp.zeros((tokens, 128), F32))
            peaks.append(peak)
            sums.append(jnp.sum(total, axis=1, keepdims=True))
        top = jnp.maximum(peaks[0], peaks[1])
        scales = [jnp.exp(peak - top) for peak in peaks]
        inverse = 1.0 / (sums[0] * scales[0] + sums[1] * scales[1])
        factors = [scale * inverse for scale in scales]
        for h in range(2):
            fac_ref[level, h] = jnp.broadcast_to(factors[h], (tokens, 128))
        picked = acc_ref[0] * factors[0] + acc_ref[1] * factors[1]
        q_level_ref[level] = picked
        res_ref[level + 1] = residual - picked

    res_ref[0] = lat_ref[...].astype(F32)
    level_forward(0, True)

    def later(level, nothing):
        level_forward(level, False)
        return nothing

    lax.fori_loop(1, DEPTH, later, 0)
    q_ref[...] = (q_level_ref[0] + q_level_ref[1]) + (q_level_ref[2] + q_level_ref[3])

    weight = weight_ref[...]
    count_ref[...] = jnp.zeros(count_ref.shape, F32)
    carry_ref[...] = 2.0 * COMMIT * weight * res_ref[DEPTH]

    def level_back(step, nothing):
        level = DEPTH - 1 - step
        carry = carry_ref[...]
        grad = cot_ref[...].astype(F32) - carry
        dot = jnp.sum(grad * q_level_ref[level], axis=1, keepdims=True)
        ex_row = pl.multiple_of(level * tokens, tokens)
        in_row = pl.multiple_of((DEPTH + level) * tokens, tokens)
        turned_rows = grad_t(rows_ref[level])
        for h in range(2):
            factor = fac_ref[level, h][:, 0:1]
            down = (grad * factor).astype(BF)
            small = down * jnp.asarray(2.0 * BETA, BF)
            total_grad = dot * factor * (-2.0 * BETA)
            share = weight * factor
            side_ref[h, :, pl.ds(ex_row, tokens)] = grad_t(down)
            side_ref[h, :, pl.ds(in_row, tokens)] = turned_rows
            for k in range(part // tile):
                lanes = slice(h * part + k * tile, h * part + (k + 1) * tile)
                p = stack_ref[pl.ds(ex_row, tokens), lanes].astype(F32)
                ds = (mm(small, codet_ref[:, lanes]) + total_grad) * p
                inner = ds.astype(BF)
                stack_ref[pl.ds(in_row, tokens), lanes] = inner
                value = mm(inner, code_ref[lanes, :])
                if h == 0 and k == 0:
                    acc_ref[0] = value
                else:
                    acc_ref[0] += value
                weighted = (p * share).reshape(tokens // 8, 8, tile)
                count_ref[0, :, lanes] += jnp.sum(weighted, axis=0)
                count_ref[1, :, lanes] += jnp.sum(ds.reshape(tokens // 8, 8, tile), axis=0)
        pull = jnp.where(level > 0, 2.0 * COMMIT, 0.0)
        carry_ref[...] = carry + acc_ref[0] + pull * weight * res_ref[level]
        return nothing

    lax.fori_loop(0, DEPTH, level_back, 0)
    g_ref[...] = carry_ref[...].astype(BF)
    extra_ref[0:1, :] = jnp.sum(count_ref[0], axis=0, keepdims=True)
    extra_ref[1:2, :] = jnp.sum(count_ref[1], axis=0, keepdims=True)

    place = place_ref[0]
    pending = []
    n_row = stage_ref.shape[1] if halves else 1
    block = width // n_row
    if halves:
        flat = jnp.concatenate([rows_ref[level] for level in range(DEPTH)], axis=0)
        source = mm(flat, pick_ref[...], TN).astype(BF)
        spans = source.shape[1] // 128
        for k in range(n_shard):
            lines = []
            for row in range(2):
                for at in range(k * shard, (k + 1) * shard, 128):
                    lines.append(extra_ref[row : row + 1, at : at + 128])
            lines = jnp.concatenate(lines, axis=0).astype(BF)
            for r in range(n_row):
                for span in range(spans):
                    more_ref[k, r ^ place, span * block : (span + 1) * block, :] = source[
                        r * block : (r + 1) * block, span * 128 : (span + 1) * 128
                    ]
                more_ref[k, r ^ place, spans * block :, :] = lines
            rows = more_ref.shape[2]
            target = grad_hbm[k % 2].at[k // 2, :, pl.ds(shard // 128 * block, rows), :]
            copy = pltpu.make_async_copy(more_ref.at[k], target, more_sem.at[k])
            copy.start()
            pending.append(copy)
    slots = [None, None]
    for k in range(n_shard):
        for j in range(shard // min(SUB, shard)):
            sub = min(SUB, shard)
            at = k * shard + j * sub
            slot = (at // sub) % 2
            value = mm(side_ref[at // part], stack_ref[:, at : at + sub]).astype(BF)
            if slots[slot] is not None:
                slots[slot].wait()
            if halves:
                for r in range(n_row):
                    for t in range(sub // 128):
                        stage_ref[slot, r ^ place, t * block : (t + 1) * block, :] = value[
                            r * block : (r + 1) * block, t * 128 : (t + 1) * 128
                        ]
                rows = sub // 128 * block
                target = grad_hbm[k % 2].at[k // 2, :, pl.ds(j * rows, rows), :]
            else:
                stage_ref[slot] = value
                target = grad_hbm[0].at[k, :, pl.ds(j * sub, sub)]
            slots[slot] = pltpu.make_async_copy(stage_ref.at[slot], target, out_sem.at[slot])
            slots[slot].start()
    for copy in slots + pending:
        copy.wait()


def grad_t(values):
    return values.astype(F32).T.astype(BF)


def quant_call(place, latent, weight, cot, pick, pieces, halves, n_shard, n_row):
    tokens, width = latent.shape
    codes = sum(piece.shape[0] for piece in pieces)
    shard = codes // n_shard
    n_piece = len(pieces)
    sub = min(SUB, shard)
    block = width // n_row
    more = (n_shard, n_row, pick.shape[1] // 128 * block + 2 * shard // 128, 128)
    if halves:
        rows = shard // 128 * block + more[2]
        grads = [jax.ShapeDtypeStruct((n_shard // 2, n_row, rows, 128), BF)] * 2
        stage = (2, n_row, sub // 128 * block, 128)
    else:
        grads = [jax.ShapeDtypeStruct((n_shard, width, shard), BF)]
        stage = (2, width, sub)
        more = (1, 1, 16, 128)
    outs = [
        jax.ShapeDtypeStruct((tokens, width), F32),
        jax.ShapeDtypeStruct((tokens, width), BF),
        jax.ShapeDtypeStruct((DEPTH, tokens, width), BF),
        jax.ShapeDtypeStruct((2, codes), F32),
    ] + grads
    return pl.pallas_call(
        functools.partial(quant_kernel, n_shard, halves, n_piece),
        out_shape=outs,
        in_specs=[smem(), vmem(), vmem(), vmem(), vmem()] + [hbm()] * n_piece,
        out_specs=[vmem()] * 4 + [hbm()] * len(grads),
        scratch_shapes=[
            pltpu.VMEM((codes, width), BF),
            pltpu.VMEM((width, codes), BF),
            pltpu.VMEM((tokens, codes // 2), F32),
            pltpu.VMEM((2 * DEPTH * tokens, codes), BF),
            pltpu.VMEM((DEPTH + 1, tokens, width), F32),
            pltpu.VMEM((DEPTH, tokens, width), F32),
            pltpu.VMEM((DEPTH, 2, tokens, 128), F32),
            pltpu.VMEM((2, width, 2 * DEPTH * tokens), BF),
            pltpu.VMEM((2, tokens, width), F32),
            pltpu.VMEM((2, 8, codes), F32),
            pltpu.VMEM((1, codes), F32),
            pltpu.VMEM((tokens, width), F32),
            pltpu.VMEM(stage, BF),
            pltpu.VMEM(more, BF),
            pltpu.SemaphoreType.DMA((n_piece,)),
            pltpu.SemaphoreType.DMA((2,)),
            pltpu.SemaphoreType.DMA((n_shard,)),
        ],
        compiler_params=pltpu.CompilerParams(vmem_limit_bytes=63 * MIB),
        cost_estimate=pl.CostEstimate(
            flops=48 * tokens * width * codes,
            bytes_accessed=18 * MIB,
            transcendentals=DEPTH * tokens * codes,
        ),
        name="soft_quantize",
    )(place, latent, weight, cot, pick, *pieces)


def slope(values):
    sigma = jax.nn.sigmoid(values)
    return sigma * (1.0 + values * (1.0 - sigma))


def put_blocks(place_ref, outs, n_in, n_out, row, value):
    if len(outs) == 1:
        outs[0][row : row + value.shape[0], :] = value.astype(BF)
        return
    rows = value.shape[0] // n_in
    odd = place_ref[1] % 2 == 1
    line = place_ref[1] // 2
    low = value.astype(BF)
    for pair in range(n_out // 2):
        even = low[:, 256 * pair : 256 * pair + 128]
        other = low[:, 256 * pair + 128 : 256 * pair + 256]
        keep = jnp.where(odd, other, even)
        send = jnp.where(odd, even, other)
        for i in range(n_in):
            at = slice(i * rows, (i + 1) * rows)
            outs[0][pair ^ line, i ^ place_ref[0], row : row + rows, :] = keep[at]
            outs[1][pair ^ line, i ^ place_ref[0], row : row + rows, :] = send[at]


def put_proj(place_ref, outs, n_in, n_out, row, value):
    if len(outs) == 1:
        outs[0][row : row + value.shape[0], 0 : value.shape[1]] = value.astype(BF)
        outs[0][row : row + value.shape[0], value.shape[1] :] = jnp.zeros(value.shape, BF)
        return
    channels, width = value.shape
    rows = channels // n_in
    cols = width // n_out
    folded = []
    for i in range(n_in):
        top = value[i * rows : i * rows + rows // 2]
        low = value[i * rows + rows // 2 : (i + 1) * rows]
        folded.append(
            jnp.concatenate(
                [
                    part[:, c * cols : (c + 1) * cols]
                    for c in range(n_out)
                    for part in (top, low)
                ],
                axis=1,
            )
        )
    put_blocks(place_ref, outs, n_in, n_out, row, jnp.concatenate(folded, axis=0))


def put_rows(place_ref, outs, n_in, n_out, row, grads_ref):
    channels = grads_ref.shape[1]
    lines = [grads_ref[k : k + 1, at] for k in range(2) for at in chunks(channels)]
    lines.append(jnp.zeros((16 - len(lines), 128), F32))
    lines = jnp.concatenate(lines, axis=0).astype(BF)
    for out in outs:
        for pair in range(n_out // 2):
            for i in range(n_in):
                out[pair, i, row : row + 16, :] = lines


def norm_back(grad, normed, inverse, gain, per_group, count):
    dn = grad * gain
    first = group_sum(col_sum(dn), per_group) * (1.0 / count)
    second = group_sum(col_sum(dn * normed), per_group) * (1.0 / count)
    return inverse * (dn - first - normed * second)


def conv_back_image(pad_ref, crop, w_ref, side, pixels):
    total = None
    for tap in range(9):
        a, b = tap // 3, tap % 3
        rows = pad_ref[crop, 2 - b, side * (2 - a) : side * (2 - a) + pixels, :]
        part = mm(rows, w_ref[tap], NT)
        total = part if total is None else total + part
    return total


def conv_back_weight(pad_ref, crops, grad, side, pixels, store):
    for tap in range(9):
        a, b = tap // 3, tap % 3
        rows = jnp.concatenate(
            [pad_ref[c, b, side * a : side * a + pixels, :] for c in range(crops)], axis=0
        )
        store(tap, mm(rows, grad, TN))


def act_shifted(pad_ref, read, stats_ref, norm_ref, stage, crops, channels, side):
    for c in range(crops):
        for k in chunks(channels):
            normed = (read(c, k) - stats_ref[c, 2 * stage : 2 * stage + 1, k]) * stats_ref[
                c, 2 * stage + 1 : 2 * stage + 2, k
            ]
            out = normed * norm_ref[2 * stage : 2 * stage + 1, k]
            out = out + norm_ref[2 * stage + 1 : 2 * stage + 2, k]
            put_shifted(pad_ref, c, k, out * jax.nn.sigmoid(out), side)


def act_back(read, dact_ref, stats_ref, norm_ref, stage, crops, pixels, channels, grads_ref, store):
    per_group = channels // GROUPS
    count = float(pixels * per_group)
    for k in chunks(channels):
        gain_row = norm_ref[2 * stage : 2 * stage + 1, k]
        bias_row = norm_ref[2 * stage + 1 : 2 * stage + 2, k]
        grad_gain = jnp.zeros((1, 128), F32)
        grad_bias = jnp.zeros((1, 128), F32)
        for c in range(crops):
            inverse = stats_ref[c, 2 * stage + 1 : 2 * stage + 2, k]
            normed = (read(c, k) - stats_ref[c, 2 * stage : 2 * stage + 1, k]) * inverse
            dout = dact_ref[c, :, k] * slope(normed * gain_row + bias_row)
            grad_gain = grad_gain + col_sum(dout * normed)
            grad_bias = grad_bias + col_sum(dout)
            store(c, k, norm_back(dout, normed, inverse, gain_row, per_group, count))
        grads_ref[0:1, k] = grad_gain
        grads_ref[1:2, k] = grad_bias


def second_kernel(
    side,
    n_out_refs,
    n_in,
    n_out,
    place_ref,
    dlat_ref,
    red_ref,
    sel_ref,
    dn_ref,
    pj_ref,
    conv_ref,
    stats_ref,
    norm_ref,
    w_hbm,
    *rest,
):
    outs = rest[:n_out_refs]
    dsum_ref, dconv_ref, ngrad_ref, w_ref, apad_ref, dpad_ref, dact_ref, sem = rest[n_out_refs:]
    crops, pixels, channels = conv_ref.shape
    copy = pltpu.make_async_copy(w_hbm.at[1], w_ref, sem.at[0])
    copy.start()
    zero_borders(apad_ref, side)
    zero_borders(dpad_ref, side)
    rows = channels // n_in if n_out_refs == 2 else channels
    lat = pixels // 4

    def read(c, k):
        return conv_ref[c, :, k]

    dlat = dlat_ref[...]
    dred = mm(dlat, pj_ref[...], NT).astype(BF)
    order = pixel_order(pixels, side)
    pieces = [mm(dred, dn_ref[tap], NT).astype(BF) for tap in range(4)]
    for c in range(crops):
        mixed = jnp.concatenate([p[c * lat : (c + 1) * lat] for p in pieces], axis=0)
        dsum_ref[c] = mm(order, mixed, TN).astype(BF)
        for k in chunks(channels):
            put_shifted(dpad_ref, c, k, dsum_ref[c, :, k].astype(F32), side)
    copy.wait()
    for c in range(crops):
        dact_ref[c] = conv_back_image(dpad_ref, c, w_ref, side, pixels)

    def store(c, k, value):
        dconv_ref[c, :, k] = value.astype(BF)

    ngrad_ref[...] = jnp.zeros(ngrad_ref.shape, F32)
    act_back(read, dact_ref, stats_ref, norm_ref, 1, crops, pixels, channels, ngrad_ref, store)
    act_shifted(apad_ref, read, stats_ref, norm_ref, 1, crops, channels, side)
    grad = jnp.concatenate([dsum_ref[c] for c in range(crops)], axis=0)
    conv_back_weight(
        apad_ref,
        crops,
        grad,
        side,
        pixels,
        lambda tap, v: put_blocks(place_ref, outs, n_in, n_out, tap * rows, v),
    )
    for tap in range(4):
        put_blocks(place_ref, outs, n_in, n_out, (9 + tap) * rows, mm(sel_ref[tap], dred, TN))
    put_proj(place_ref, outs, n_in, n_out, 13 * rows, mm(red_ref[...], dlat, TN))
    if n_out_refs == 2:
        put_rows(place_ref, outs, n_in, n_out, outs[0].shape[2] - 16, ngrad_ref)


def first_kernel(
    side,
    n_out_refs,
    n_in,
    n_out,
    n_part,
    place_ref,
    x_ref,
    stats_ref,
    norm_ref,
    dconv_ref,
    dsum_ref,
    w_hbm,
    *rest,
):
    outs = rest[:n_out_refs]
    part_refs = rest[n_out_refs : n_out_refs + n_part]
    ngrad_ref, w_ref, pad_ref, dact_ref, image_ref, sem = rest[n_out_refs + n_part :]
    crops, pixels, channels = x_ref.shape
    rows = channels // n_in if n_out_refs == 2 else channels
    copy = pltpu.make_async_copy(w_hbm.at[0], w_ref, sem.at[0])
    copy.start()
    zero_borders(pad_ref, side)

    def read(c, k):
        return x_ref[c, :, k].astype(F32)

    def store(c, k, value):
        image_ref[c, :, k] = (value + dsum_ref[c, :, k].astype(F32)).astype(BF)

    act_shifted(pad_ref, read, stats_ref, norm_ref, 0, crops, channels, side)
    grad = jnp.concatenate([dconv_ref[c] for c in range(crops)], axis=0)
    conv_back_weight(
        pad_ref,
        crops,
        grad,
        side,
        pixels,
        lambda tap, v: put_blocks(place_ref, outs, n_in, n_out, tap * rows, v),
    )
    for c in range(crops):
        for k in chunks(channels):
            put_shifted(pad_ref, c, k, dconv_ref[c, :, k].astype(F32), side)
    copy.wait()
    for c in range(crops):
        dact_ref[c] = conv_back_image(pad_ref, c, w_ref, side, pixels)
    ngrad_ref[...] = jnp.zeros(ngrad_ref.shape, F32)
    act_back(read, dact_ref, stats_ref, norm_ref, 0, crops, pixels, channels, ngrad_ref, store)
    if n_out_refs == 2:
        put_rows(place_ref, outs, n_in, n_out, 9 * rows, ngrad_ref)
    span = pixels // n_part
    for k in range(n_part):
        if n_part == 1:
            part_refs[k][...] = image_ref[...]
        else:
            at = pl.multiple_of((place_ref[0] ^ k) * span, span)
            for c in range(crops):
                part_refs[k][c] = image_ref[c, pl.ds(at, span), :]


def conv_cost(crops, pixels, channels, convs):
    return pl.CostEstimate(
        flops=convs * 18 * crops * pixels * channels * channels,
        bytes_accessed=12 * MIB,
        transcendentals=crops * pixels * channels,
    )


def grad_shapes(halves, n_in, n_out, channels, units):
    if not halves:
        return [jax.ShapeDtypeStruct((units[0] * channels, channels), BF)]
    rows = channels // n_in
    shape = (n_out // 2, n_in, units[0] * rows + units[1], channels // n_out)
    return [jax.ShapeDtypeStruct(shape, BF)] * 2


def second_call(place, dlat, red, sel, dn, pj, conv, stats, norm, w, side, halves, n_in, n_out):
    crops, pixels, channels = conv.shape
    if halves:
        fold = channels // n_in * pj.shape[1] // channels
        grads = grad_shapes(True, n_in, n_out, channels, (13, fold + 16))
    else:
        grads = grad_shapes(False, n_in, n_out, channels, (14, 0))
    pad = (crops, 3, pixels + 2 * side, channels)
    return pl.pallas_call(
        functools.partial(second_kernel, side, len(grads), n_in, n_out),
        out_shape=grads
        + [
            jax.ShapeDtypeStruct(conv.shape, BF),
            jax.ShapeDtypeStruct(conv.shape, BF),
            jax.ShapeDtypeStruct((8, channels), F32),
        ],
        in_specs=[smem()] + [vmem()] * 8 + [hbm()],
        out_specs=[vmem()] * (len(grads) + 3),
        scratch_shapes=[
            pltpu.VMEM(w.shape[1:], BF),
            pltpu.VMEM(pad, BF),
            pltpu.VMEM(pad, BF),
            pltpu.VMEM(conv.shape, F32),
            pltpu.SemaphoreType.DMA((1,)),
        ],
        compiler_params=pltpu.CompilerParams(vmem_limit_bytes=44 * MIB),
        cost_estimate=conv_cost(crops, pixels, channels, 2),
        name="second_backward",
    )(place, dlat, red, sel, dn, pj, conv, stats, norm, w)


def first_call(place, x, stats, norm, dconv, dsum, w, side, halves, n_in, n_out):
    crops, pixels, channels = x.shape
    n_part = n_in if halves else 1
    grads = grad_shapes(halves, n_in, n_out, channels, (9, 16 if halves else 0))
    outs = (
        grads
        + [jax.ShapeDtypeStruct((crops, pixels // n_part, channels), BF)] * n_part
        + [jax.ShapeDtypeStruct((8, channels), F32)]
    )
    return pl.pallas_call(
        functools.partial(first_kernel, side, len(grads), n_in, n_out, n_part),
        out_shape=outs,
        in_specs=[smem()] + [vmem()] * 5 + [hbm()],
        out_specs=[vmem()] * len(outs),
        scratch_shapes=[
            pltpu.VMEM(w.shape[1:], BF),
            pltpu.VMEM((crops, 3, pixels + 2 * side, channels), BF),
            pltpu.VMEM(x.shape, F32),
            pltpu.VMEM(x.shape, BF),
            pltpu.SemaphoreType.DMA((1,)),
        ],
        compiler_params=pltpu.CompilerParams(vmem_limit_bytes=44 * MIB),
        cost_estimate=conv_cost(crops, pixels, channels, 2),
        name="first_backward",
    )(place, x, stats, norm, dconv, dsum, w)


def swap(array, axis, bit):
    count = lax.axis_size(axis)
    return lax.ppermute(array, axis, [(i, i ^ bit) for i in range(count)])


def add_low(first, second):
    return (first.astype(F32) + second.astype(F32)).astype(BF)


ORDERS = (("x", "y", "z1", "z2"), ("y", "z1", "x", "z2"), ("z1", "x", "y", "z2"))
LINKS = {"x": ("code", 2), "y": ("dp", 1), "z1": ("dp", 2), "z2": ("dp", 4)}
BITS = ("x", "z2", "z1", "y")


class Part:
    def __init__(self, array, order):
        self.array, self.order, self.dims = array, list(order), list(BITS)


def split_parts(total):
    total = total.reshape((2, 2, 2, 2) + total.shape[2:])
    units = total.shape[4] // 16
    cuts = [0, (units + 2) // 3 * 16, (units + 2) // 3 * 16 + (units + 1) // 3 * 16, units * 16]
    return [Part(total[..., cuts[k] : cuts[k + 1], :], ORDERS[k]) for k in range(3)]


def send_round(parts):
    sent = {}
    for part in parts:
        sent.setdefault(part.order[0], []).append(part)
    flights = []
    for name, group in sent.items():
        axis, bit = LINKS[name]
        theirs = [lax.index_in_dim(p.array, 1, p.dims.index(name), keepdims=False) for p in group]
        flat = jnp.concatenate([t.reshape(-1, t.shape[-1]) for t in theirs])
        flights.append((name, group, swap(flat, axis, bit)))
    return flights


def land_round(flights, arrived):
    for (name, group, _), flat in zip(flights, arrived):
        at = 0
        for part in group:
            mine = lax.index_in_dim(part.array, 0, part.dims.index(name), keepdims=False)
            rows = mine.size // mine.shape[-1]
            part.array = add_low(mine, flat[at : at + rows].reshape(mine.shape))
            part.dims.remove(name)
            part.order.pop(0)
            at += rows


def together(flights, *others):
    arrived = [flight[2] for flight in flights]
    tied = lax.optimization_barrier(tuple(arrived) + tuple(others))
    land_round(flights, tied[: len(arrived)])
    return tied[len(arrived) :]


def joined(parts):
    return jnp.concatenate([part.array for part in parts], axis=0).astype(F32)


def nesterov_step(master, moment, average, grad, rate):
    moment_new = MOMENTUM * moment + grad
    master_new = master - rate * (grad + MOMENTUM * moment_new)
    return (moment_new, master_new, AVERAGE_DECAY * average + (1.0 - AVERAGE_DECAY) * master_new)


def body(
    crops_in,
    crop_weight,
    cotangent,
    conv_copy,
    down_copy,
    proj_copy,
    norm_copy,
    codebook,
    conv_master,
    conv_moment,
    conv_average,
    down_master,
    down_moment,
    down_average,
    proj_master,
    proj_moment,
    proj_average,
    norm_master,
    norm_moment,
    norm_average,
    code_master,
    code_moment,
    code_average,
    repl_code,
    repl_src,
):
    dp_count = lax.axis_size("dp")
    code_count = lax.axis_size("code")
    dp_at = lax.axis_index("dp")
    code_at = lax.axis_index("code")
    halves = dp_count == 8 and code_count == 4
    place = jnp.stack([dp_at, code_at]).astype(jnp.int32)

    local = lax.all_to_all(crops_in, "dp", split_axis=1, concat_axis=2, tiled=True)[0]
    crop_dev, pixels, channels = local.shape
    side = math.isqrt(pixels)
    lat = pixels // 4
    tokens = crop_dev * lat
    width = proj_copy.shape[1]
    code_dev = codebook.shape[0]
    codes_all = code_dev * code_count

    if halves:
        half, quarter = code_dev // 2, code_dev // 4
        mine = lax.dynamic_slice_in_dim(codebook, (dp_at % 2) * half, half, 0)
        far = [swap(mine[:quarter], "code", 2), swap(mine[quarter:], "code", 2)]
        far = far + [swap(piece, "dp", 1) for piece in far]
        pieces = [codebook, swap(codebook, "code", 1)] + far
        pieces = pieces + [swap(piece, "code", 1) for piece in far]
    else:
        every = lax.all_gather(codebook, "code", axis=0)
        pieces = [every[k] for k in range(code_count)]

    crops_set = crop_dev * dp_count
    flat_src = repl_src.reshape(-1)
    crop_id = flat_src // lat % crops_set
    owner = (crop_id // crop_dev == dp_at) & (flat_src // (crops_set * lat) == code_at)
    row_id = crop_id % crop_dev * lat + flat_src % lat
    depth_id = jnp.repeat(jnp.arange(DEPTH, dtype=jnp.int32), repl_src.shape[1])
    pick = (
        jnp.where(owner, depth_id * tokens + row_id, -1)[None, :]
        == jnp.arange(DEPTH * tokens, dtype=jnp.int32)[:, None]
    ).astype(BF)

    w = conv_copy.transpose(1, 2, 0, 3)
    dn = down_copy.transpose(1, 0, 2)
    gains = norm_copy.T.astype(F32)
    conv1, stats, sel, reduced, latent = forward_call(local, gains, w, dn, proj_copy, side)

    weight_col = jnp.broadcast_to(
        crop_weight.astype(F32).reshape(crop_dev, 1), (crop_dev, lat)
    ).reshape(tokens, 1)
    n_row = dp_count if halves else 1
    quantized, dlat, rows, extra, *code_grads = quant_call(
        place,
        latent,
        weight_col,
        cotangent.reshape(tokens, width),
        pick,
        pieces,
        halves,
        code_count,
        n_row,
    )
    rows_in = channels // dp_count
    out_dev = channels // code_count

    def second_args(dlat):
        return second_call(
            place, dlat, reduced, sel, dn, proj_copy, conv1, stats, gains, w, side, halves,
            dp_count, code_count,
        )

    def first_args(dconv, dsum):
        return first_call(
            place, local, stats, gains, dconv, dsum, w, side, halves, dp_count, code_count
        )

    if halves:
        code_core = swap(code_grads[1], "code", 1)
        keep_two, send_two, dsum, dconv, _ = second_args(dlat)
        code_core, dconv, send_two = lax.optimization_barrier((code_core, dconv, send_two))
        codes = split_parts(add_low(code_grads[0], code_core))
        flights = send_round(codes)
        two_core = swap(send_two, "code", 1)
        keep_one, send_one, *image_parts, _ = first_args(dconv, dsum)
        two_core, send_one, *image_parts = together(flights, two_core, send_one, *image_parts)
        twos = split_parts(add_low(keep_two, two_core))
        one_core = swap(send_one, "code", 1)
        flights = send_round(codes + twos)
        images = {k: swap(image_parts[k], "dp", k) for k in (6, 7)}
        one_core, images[6], images[7] = together(flights, one_core, images[6], images[7])
        ones = split_parts(add_low(keep_one, one_core))
        flights = send_round(codes + twos + ones)
        images.update({k: swap(image_parts[k], "dp", k) for k in (4, 5)})
        images[4], images[5] = together(flights, images[4], images[5])
        flights = send_round(codes + twos + ones)
        images.update({k: swap(image_parts[k], "dp", k) for k in (3,)})
        (images[3],) = together(flights, images[3])
        flights = send_round(twos + ones)
        images.update({k: swap(image_parts[k], "dp", k) for k in (1, 2)})
        images[1], images[2] = together(flights, images[1], images[2])
        together(send_round(ones))

        code_total, two_total, one_total = joined(codes), joined(twos), joined(ones)
        cols = width // dp_count
        tiles = code_dev // 128
        span = tiles * cols
        code_grad = code_total[:span].reshape(tiles, cols, 128).transpose(1, 0, 2)
        code_grad = code_grad.reshape(cols, code_dev)
        spans = pick.shape[1] // 128
        source_rows = code_total[span : span + spans * cols].reshape(spans, cols, 128)
        source_rows = source_rows.transpose(1, 0, 2).reshape(cols, spans * 128).astype(BF)
        sums = code_total[span + spans * cols :].reshape(2, code_dev)

        conv_part = jnp.stack(
            [
                one_total[: 9 * rows_in].reshape(9, rows_in, out_dev),
                two_total[: 9 * rows_in].reshape(9, rows_in, out_dev),
            ]
        ).transpose(2, 0, 1, 3)
        down_part = (
            two_total[9 * rows_in : 13 * rows_in].reshape(4, rows_in, out_dev).transpose(1, 0, 2)
        )
        fold = two_total[13 * rows_in : -16]
        proj_part = jnp.concatenate([fold[:, : out_dev // 2], fold[:, out_dev // 2 :]], axis=0)
        lines = 2 * channels // 128
        norm_grad = jnp.concatenate(
            [
                one_total[9 * rows_in : 9 * rows_in + lines].reshape(2, channels),
                two_total[-16 : lines - 16].reshape(2, channels),
            ]
        )

        images[0] = image_parts[0]
        input_back = jnp.zeros((crop_dev * dp_count, pixels // dp_count, channels), F32)
        for k in range(dp_count):
            input_back = lax.dynamic_update_slice(
                input_back, images[k].astype(F32), ((dp_at ^ k) * crop_dev, 0, 0)
            )
        input_back = input_back[None]
    else:
        grads_second, dsum, dconv, ngrad_second = second_args(dlat)
        grads_first, image, ngrad_first = first_args(dconv, dsum)
        norm_grad = jnp.concatenate([ngrad_first[0:2], ngrad_second[0:2]], axis=0)
        flat = lax.psum_scatter(code_grads[0], "code", scatter_dimension=0, tiled=True)[0]
        code_grad = lax.psum_scatter(flat, "dp", scatter_dimension=0, tiled=True).astype(F32)
        sums = lax.psum_scatter(extra, "code", scatter_dimension=1, tiled=True)
        sums = lax.psum(sums, "dp")
        source = mm(rows.reshape(DEPTH * tokens, width), pick, TN).astype(BF)
        source_rows = lax.psum_scatter(source, "dp", scatter_dimension=0, tiled=True)
        source_rows = lax.psum(source_rows, "code")

        def matrix(array, scatter):
            array = lax.psum_scatter(array, "dp", scatter_dimension=0, tiled=True)
            return lax.psum_scatter(array, "code", scatter_dimension=scatter, tiled=True).astype(F32)

        conv_flat = jnp.stack(
            [
                grads_first.reshape(9, channels, channels),
                grads_second[: 9 * channels].reshape(9, channels, channels),
            ]
        ).transpose(2, 0, 1, 3)
        conv_part = matrix(conv_flat, 3)
        down_flat = grads_second[9 * channels : 13 * channels]
        down_part = matrix(down_flat.reshape(4, channels, channels).transpose(1, 0, 2), 2)
        proj_part = matrix(grads_second[13 * channels :, :width], 1)
        norm_grad = lax.psum(norm_grad, ("dp", "code"))
        input_back = lax.all_to_all(
            image[None], "dp", split_axis=2, concat_axis=1, tiled=True
        ).astype(F32)

    pixels_all = crop_dev * pixels * dp_count * code_count
    weight_rate = WEIGHT_RATE / math.sqrt(pixels_all)
    norm_rate = NORM_RATE / math.sqrt(pixels_all)
    crops_all = crop_dev * dp_count * code_count
    mean_count = DEPTH * lat * crops_all / codes_all
    code_rate = CODE_RATE / math.sqrt(mean_count)
    conv_out = nesterov_step(conv_master, conv_moment, conv_average, conv_part, weight_rate)
    down_out = nesterov_step(down_master, down_moment, down_average, down_part, weight_rate)
    proj_out = nesterov_step(proj_master, proj_moment, proj_average, proj_part, weight_rate)
    norm_out = nesterov_step(norm_master, norm_moment, norm_average, norm_grad.T, norm_rate)

    counts_all, slope_sum = sums[0], sums[1]
    share = mean_count / (mean_count + counts_all)
    code_load = counts_all / mean_count
    cols = width // dp_count
    own_codes = lax.dynamic_slice_in_dim(codebook, dp_at * cols, cols, 1).T.astype(F32)
    code_grad = code_grad - own_codes * slope_sum[None, :]
    code_moment_new = MOMENTUM * code_moment.T + code_grad
    stepped = code_master.T - code_rate * (code_grad + MOMENTUM * code_moment_new)
    select = (
        repl_code.reshape(-1)[:, None] - code_at * code_dev
        == jnp.arange(code_dev, dtype=jnp.int32)[None, :]
    )
    chosen = jnp.sum(select.astype(F32), axis=0)
    renewed = mm(source_rows, select.astype(BF))
    code_master_new = stepped + (chosen * share)[None, :] * (renewed - stepped)
    code_average_new = AVERAGE_DECAY * code_average.T + (1.0 - AVERAGE_DECAY) * code_master_new
    return (
        quantized.reshape(1, crop_dev, lat, width),
        input_back,
        *conv_out,
        *down_out,
        *proj_out,
        *norm_out,
        code_moment_new.T,
        code_master_new.T,
        code_average_new.T,
        code_load,
    )


def solution(mesh):
    in_specs = (
        P("code", None, "dp", None),
        P("code", "dp"),
        P("code", "dp", None, None),
        P(),
        P(),
        P(),
        P(),
        P("code", None),
        P("dp", None, None, "code"),
        P("dp", None, None, "code"),
        P("dp", None, None, "code"),
        P("dp", None, "code"),
        P("dp", None, "code"),
        P("dp", None, "code"),
        P("dp", "code"),
        P("dp", "code"),
        P("dp", "code"),
        P(),
        P(),
        P(),
        P("code", "dp"),
        P("code", "dp"),
        P("code", "dp"),
        P(),
        P(),
    )
    out_specs = (
        P("code", "dp", None, None),
        P("code", None, "dp", None),
        P("dp", None, None, "code"),
        P("dp", None, None, "code"),
        P("dp", None, None, "code"),
        P("dp", None, "code"),
        P("dp", None, "code"),
        P("dp", None, "code"),
        P("dp", "code"),
        P("dp", "code"),
        P("dp", "code"),
        P(),
        P(),
        P(),
        P("code", "dp"),
        P("code", "dp"),
        P("code", "dp"),
        P("code"),
    )
    return jax.shard_map(body, mesh=mesh, in_specs=in_specs, out_specs=out_specs, check_vma=False)
```

```python
import functools
import math

import jax
import jax.numpy as jnp
from jax import lax
from jax.experimental import pallas as pl
from jax.experimental.pallas import tpu as pltpu
from jax.sharding import PartitionSpec as P

GROUPS = 32
DEPTH = 4
BETA = 0.0625
EPSILON = 1e-05
MOMENTUM = 0.5
AVERAGE_DECAY = 0.5
COMMIT = 0.25
WEIGHT_RATE = 0.05
NORM_RATE = 0.5
CODE_RATE = 0.5

BF = jnp.bfloat16
F32 = jnp.float32
NT = (((1,), (1,)), ((), ()))
NN = (((1,), (0,)), ((), ()))
TN = (((0,), (0,)), ((), ()))
MIB = 1 << 20
LIMIT = 62 * MIB
SMALL_COST = pl.CostEstimate(flops=1 << 20, bytes_accessed=1 << 16, transcendentals=0)


def mm(a, b, dims=NN):
    return lax.dot_general(a, b, dims, preferred_element_type=F32)


def vmem():
    return pl.BlockSpec(memory_space=pltpu.VMEM)


def smem():
    return pl.BlockSpec(memory_space=pltpu.SMEM)


def anywhere():
    return pl.BlockSpec(memory_space=pl.ANY)


def hbm():
    return pl.BlockSpec(memory_space=pltpu.HBM)


def group_sum(rows, per_group):
    lanes = rows.shape[1]
    at = lax.broadcasted_iota(jnp.int32, rows.shape, 1)
    step = 1
    while step < per_group:
        up = pltpu.roll(rows, step, 1)
        down = pltpu.roll(rows, lanes - step, 1)
        rows = rows + jnp.where((at & step) != 0, up, down)
        step *= 2
    return rows


def col_sum(values):
    rows, lanes = values.shape
    return jnp.sum(jnp.sum(values.reshape(rows // 8, 8, lanes), axis=0), axis=0, keepdims=True)


def put_shifted(pad_ref, crop, lanes, values, side):
    pixels = values.shape[0]
    col = lax.broadcasted_iota(jnp.int32, values.shape, 0) % side
    left = jnp.where(col == 0, 0.0, pltpu.roll(values, 1, 0))
    right = jnp.where(col == side - 1, 0.0, pltpu.roll(values, pixels - 1, 0))
    for shift, grid in enumerate((left, values, right)):
        pad_ref[crop, shift, side : side + pixels, lanes] = grid.astype(BF)


def zero_borders(pad_ref, side):
    rows = pad_ref.shape[2]
    edge = jnp.zeros((side, pad_ref.shape[3]), BF)
    for crop in range(pad_ref.shape[0]):
        for shift in range(3):
            pad_ref[crop, shift, 0:side, :] = edge
            pad_ref[crop, shift, rows - side : rows, :] = edge


def pixel_order(pixels, side):
    half = side // 2
    lat = half * half
    row = lax.broadcasted_iota(jnp.int32, (pixels, pixels), 0)
    col = lax.broadcasted_iota(jnp.int32, (pixels, pixels), 1)
    tap, pos = row // lat, row % lat
    at = (2 * (pos // half) + tap // 2) * side + 2 * (pos % half) + tap % 2
    return jnp.where(at == col, 1.0, 0.0).astype(BF)


def chunks(channels):
    return [slice(k, k + 128) for k in range(0, channels, 128)]


def norm_stats(read, crops, pixels, channels, per_group):
    count = float(pixels * per_group)
    result = []
    sums = [
        jnp.concatenate([col_sum(read(c, k)) for k in chunks(channels)], axis=1)
        for c in range(crops)
    ]
    means = [group_sum(s, per_group) * (1.0 / count) for s in sums]
    for c in range(crops):
        parts = []
        for k in chunks(channels):
            d = read(c, k) - means[c][:, k]
            parts.append(col_sum(d * d))
        spread = group_sum(jnp.concatenate(parts, axis=1), per_group) * (1.0 / count)
        result.append((means[c], lax.rsqrt(spread + EPSILON)))
    return result


def conv_apply(pad_ref, crop, w_ref, side, pixels):
    total = None
    for b in range(3):
        rows = jnp.concatenate(
            [pad_ref[crop, b, side * a : side * a + pixels, :] for a in range(3)], axis=1
        )
        part = None
        weight = jnp.concatenate([w_ref[3 * a + b] for a in range(3)], axis=0)
        part = mm(rows, weight)
        total = part if total is None else total + part
    return total


def forward_kernel(
    side,
    x_ref,
    norm_ref,
    w_hbm,
    dn_hbm,
    pj_ref,
    conv_hbm,
    stats_ref,
    save_hbm,
    lat_ref,
    w_ref,
    dn_ref,
    pad_ref,
    sum_ref,
    conv_ref,
    sel_ref,
    sem,
):
    crops, pixels, channels = x_ref.shape
    per_group = channels // GROUPS
    lat = pixels // 4
    tokens = crops * lat
    copies = [pltpu.make_async_copy(w_hbm.at[k], w_ref.at[k], sem.at[k]) for k in range(2)]
    dn_copy = pltpu.make_async_copy(dn_hbm, dn_ref, sem.at[2])
    for copy in copies + [dn_copy]:
        copy.start()
    conv_save = pltpu.make_async_copy(conv_ref, conv_hbm, sem.at[3])
    zero_borders(pad_ref, side)
    for stage in range(2):
        if stage == 0:

            def read(c, k):
                return x_ref[c, :, k].astype(F32)

        else:

            def read(c, k):
                return conv_ref[c, :, k]

        stats = norm_stats(read, crops, pixels, channels, per_group)
        for c in range(crops):
            mean, inverse = stats[c]
            stats_ref[c, 2 * stage : 2 * stage + 1, :] = mean
            stats_ref[c, 2 * stage + 1 : 2 * stage + 2, :] = inverse
            for k in chunks(channels):
                normed = (read(c, k) - mean[:, k]) * inverse[:, k]
                out = normed * norm_ref[2 * stage : 2 * stage + 1, k]
                out = out + norm_ref[2 * stage + 1 : 2 * stage + 2, k]
                put_shifted(pad_ref, c, k, out * jax.nn.sigmoid(out), side)
        acts = [
            pltpu.make_async_copy(
                pad_ref.at[c, 1, pl.ds(side, pixels), :],
                save_hbm.at[pl.ds((stage * crops + c) * pixels, pixels), :],
                sem.at[4 + c],
            )
            for c in range(crops)
        ]
        for act in acts:
            act.start()
        copies[stage].wait()
        for c in range(crops):
            total = conv_apply(pad_ref, c, w_ref.at[stage], side, pixels)
            if stage == 0:
                conv_ref[c] = total
            else:
                sum_ref[c] = (x_ref[c].astype(F32) + total).astype(BF)
        for act in acts:
            act.wait()
        if stage == 0:
            conv_save.start()
    order = pixel_order(pixels, side)
    for c in range(crops):
        picked = mm(order, sum_ref[c]).astype(BF)
        for tap in range(4):
            at = tap * tokens + c * lat
            sel_ref[at : at + lat, :] = picked[tap * lat : (tap + 1) * lat]
    dn_copy.wait()
    reduced = mm(sel_ref[0:tokens], dn_ref[0])
    for tap in range(1, 4):
        reduced = reduced + mm(sel_ref[tap * tokens : (tap + 1) * tokens], dn_ref[tap])
    reduced = reduced.astype(BF)
    sel_ref[4 * tokens : 5 * tokens, :] = reduced
    sel_save = pltpu.make_async_copy(
        sel_ref, save_hbm.at[pl.ds(2 * crops * pixels, 5 * tokens), :], sem.at[4 + crops]
    )
    sel_save.start()
    lat_ref[...] = mm(reduced, pj_ref[...]).astype(BF)
    conv_save.wait()
    sel_save.wait()


def forward_call(x, norm, w, dn, pj, side):
    crops, pixels, channels = x.shape
    tokens = crops * pixels // 4
    return pl.pallas_call(
        functools.partial(forward_kernel, side),
        out_shape=[
            jax.ShapeDtypeStruct((crops, pixels, channels), F32),
            jax.ShapeDtypeStruct((crops, 8, channels), F32),
            jax.ShapeDtypeStruct((2 * crops * pixels + 5 * tokens, channels), BF),
            jax.ShapeDtypeStruct((tokens, pj.shape[1]), BF),
        ],
        in_specs=[vmem(), vmem(), hbm(), hbm(), vmem()],
        out_specs=[hbm(), vmem(), hbm(), vmem()],
        scratch_shapes=[
            pltpu.VMEM(w.shape, BF),
            pltpu.VMEM(dn.shape, BF),
            pltpu.VMEM((crops, 3, pixels + 2 * side, channels), BF),
            pltpu.VMEM((crops, pixels, channels), BF),
            pltpu.VMEM((crops, pixels, channels), F32),
            pltpu.VMEM((5 * tokens, channels), BF),
            pltpu.SemaphoreType.DMA((5 + crops,)),
        ],
        compiler_params=pltpu.CompilerParams(vmem_limit_bytes=LIMIT),
        cost_estimate=SMALL_COST,
        name="residual_forward",
    )(x, norm, w, dn, pj)


TILE = 1024
SUB = 1024
SPAN = 4096


def quant_kernel(n_shard, halves, n_piece, place_ref, lat_ref, weight_ref, cot_ref, pick_ref, *rest):
    shard_hbm = rest[:n_piece]
    n_out = 6 if halves else 5
    q_ref, g_ref, rows_ref, extra_ref = rest[n_piece : n_piece + 4]
    grad_hbm = rest[n_piece + 4 : n_piece + n_out]
    (
        code_ref,
        codet_ref,
        score_ref,
        stack_ref,
        res_ref,
        q_level_ref,
        fac_ref,
        side_ref,
        acc_ref,
        count_ref,
        norms_ref,
        carry_ref,
        stage_ref,
        more_ref,
        in_sem,
        out_sem,
        more_sem,
    ) = rest[n_piece + n_out :]
    tokens, width = lat_ref.shape
    codes = code_ref.shape[0]
    shard = codes // n_shard
    part = codes // 2
    tile = min(TILE, part)

    if halves:
        quarter = shard // 4
        corner = (place_ref[0] & 1) * 2 + ((place_ref[0] >> 1) & 1)
        starts = [0, shard]
        for base in (2 * shard, 3 * shard):
            starts += [base + (corner ^ k) * quarter for k in (0, 2, 1, 3)]
            starts.append(starts[-1] + quarter // 2)
    else:
        starts = [k * shard for k in range(n_shard)]
    copies = [
        pltpu.make_async_copy(
            shard_hbm[k],
            code_ref.at[pl.ds(pl.multiple_of(starts[k], 256), shard_hbm[k].shape[0]), :],
            in_sem.at[k],
        )
        for k in range(n_piece)
    ]
    for copy in copies:
        copy.start()

    def fold(values, combine):
        out = values[:, :128]
        for k in range(128, values.shape[1], 128):
            out = combine(out, values[:, k : k + 128])
        return out

    def level_forward(level, first):
        residual = res_ref[level]
        low = residual.astype(BF)
        rows_ref[level] = low
        scaled = low * jnp.asarray(2.0 * BETA, BF)
        at_row = pl.multiple_of(level * tokens, tokens)
        peaks, sums, picks = [], [], []
        for h in range(2):
            best = jnp.full((tokens, 128), -jnp.inf, F32)
            for k in range(part // tile):
                at = h * part + k * tile
                lanes = slice(at, at + tile)
                if first:
                    if halves:
                        if at % shard == 0:
                            group = at // shard
                            for piece in ([group] if group < 2 else range(5 * group - 8, 5 * group - 3)):
                                copies[piece].wait()
                    else:
                        if at % shard == 0:
                            copies[at // shard].wait()
                    for j in range(at, at + tile, 512):
                        turned = code_ref[j : j + 512, :].T
                        codet_ref[:, j : j + 512] = turned
                        wide = turned.astype(F32)
                        norms_ref[:, j : j + 512] = BETA * col_sum(wide * wide)
                s = mm(scaled, codet_ref[:, lanes]) - norms_ref[:, lanes]
                score_ref[:, k * tile : (k + 1) * tile] = s
                best = jnp.maximum(best, fold(s, jnp.maximum))
            peak = jnp.max(best, axis=1, keepdims=True)
            acc_ref[h] = jnp.zeros((tokens, width), F32)

            def power(i, total):
                for k in range(SPAN // tile):
                    at = pl.multiple_of(i * SPAN + k * tile, tile)
                    lanes = pl.ds(pl.multiple_of(h * part + at, tile), tile)
                    p = jnp.exp(score_ref[:, pl.ds(at, tile)] - peak)
                    low_p = p.astype(BF)
                    stack_ref[pl.ds(at_row, tokens), lanes] = low_p
                    acc_ref[h] += mm(low_p, code_ref[lanes, :])
                    total = total + fold(p, jnp.add)
                return total

            total = lax.fori_loop(0, part // SPAN, power, jnp.zeros((tokens, 128), F32))
            peaks.append(peak)
            sums.append(jnp.sum(total, axis=1, keepdims=True))
        top = jnp.maximum(peaks[0], peaks[1])
        scales = [jnp.exp(peak - top) for peak in peaks]
        inverse = 1.0 / (sums[0] * scales[0] + sums[1] * scales[1])
        factors = [scale * inverse for scale in scales]
        for h in range(2):
            fac_ref[level, h] = jnp.broadcast_to(factors[h], (tokens, 128))
        picked = acc_ref[0] * factors[0] + acc_ref[1] * factors[1]
        q_level_ref[level] = picked
        res_ref[level + 1] = residual - picked

    res_ref[0] = lat_ref[...].astype(F32)
    level_forward(0, True)

    def later(level, nothing):
        level_forward(level, False)
        return nothing

    lax.fori_loop(1, DEPTH, later, 0)
    q_ref[...] = (q_level_ref[0] + q_level_ref[1]) + (q_level_ref[2] + q_level_ref[3])

    weight = weight_ref[...]
    count_ref[...] = jnp.zeros(count_ref.shape, F32)
    carry_ref[...] = 2.0 * COMMIT * weight * res_ref[DEPTH]

    def level_back(step, nothing):
        level = DEPTH - 1 - step
        carry = carry_ref[...]
        grad = cot_ref[...].astype(F32) - carry
        dot = jnp.sum(grad * q_level_ref[level], axis=1, keepdims=True)
        ex_row = pl.multiple_of(level * tokens, tokens)
        in_row = pl.multiple_of((DEPTH + level) * tokens, tokens)
        turned_rows = grad_t(rows_ref[level])
        for h in range(2):
            factor = fac_ref[level, h][:, 0:1]
            down = (grad * factor).astype(BF)
            small = down * jnp.asarray(2.0 * BETA, BF)
            total_grad = dot * factor * (-2.0 * BETA)
            share = weight * factor
            side_ref[h, :, pl.ds(ex_row, tokens)] = grad_t(down)
            side_ref[h, :, pl.ds(in_row, tokens)] = turned_rows
            for k in range(part // tile):
                lanes = slice(h * part + k * tile, h * part + (k + 1) * tile)
                p = stack_ref[pl.ds(ex_row, tokens), lanes].astype(F32)
                ds = (mm(small, codet_ref[:, lanes]) + total_grad) * p
                inner = ds.astype(BF)
                stack_ref[pl.ds(in_row, tokens), lanes] = inner
                value = mm(inner, code_ref[lanes, :])
                if h == 0 and k == 0:
                    acc_ref[0] = value
                else:
                    acc_ref[0] += value
                weighted = (p * share).reshape(tokens // 8, 8, tile)
                count_ref[0, :, lanes] += jnp.sum(weighted, axis=0)
                count_ref[1, :, lanes] += jnp.sum(ds.reshape(tokens // 8, 8, tile), axis=0)
        pull = jnp.where(level > 0, 2.0 * COMMIT, 0.0)
        carry_ref[...] = carry + acc_ref[0] + pull * weight * res_ref[level]
        return nothing

    lax.fori_loop(0, DEPTH, level_back, 0)
    g_ref[...] = carry_ref[...].astype(BF)
    extra_ref[0:1, :] = jnp.sum(count_ref[0], axis=0, keepdims=True)
    extra_ref[1:2, :] = jnp.sum(count_ref[1], axis=0, keepdims=True)

    place = place_ref[0]
    pending = []
    n_row = stage_ref.shape[1] if halves else 1
    block = width // n_row
    if halves:
        flat = jnp.concatenate([rows_ref[level] for level in range(DEPTH)], axis=0)
        source = mm(flat, pick_ref[...], TN).astype(BF)
        spans = source.shape[1] // 128
        for k in range(n_shard):
            lines = []
            for row in range(2):
                for at in range(k * shard, (k + 1) * shard, 128):
                    lines.append(extra_ref[row : row + 1, at : at + 128])
            lines = jnp.concatenate(lines, axis=0).astype(BF)
            for r in range(n_row):
                for span in range(spans):
                    more_ref[k, r ^ place, span * block : (span + 1) * block, :] = source[
                        r * block : (r + 1) * block, span * 128 : (span + 1) * 128
                    ]
                more_ref[k, r ^ place, spans * block :, :] = lines
            rows = more_ref.shape[2]
            target = grad_hbm[k % 2].at[k // 2, :, pl.ds(shard // 128 * block, rows), :]
            copy = pltpu.make_async_copy(more_ref.at[k], target, more_sem.at[k])
            copy.start()
            pending.append(copy)
    slots = [None, None]
    for k in range(n_shard):
        for j in range(shard // min(SUB, shard)):
            sub = min(SUB, shard)
            at = k * shard + j * sub
            slot = (at // sub) % 2
            value = mm(side_ref[at // part], stack_ref[:, at : at + sub]).astype(BF)
            if slots[slot] is not None:
                slots[slot].wait()
            if halves:
                for r in range(n_row):
                    for t in range(sub // 128):
                        stage_ref[slot, r ^ place, t * block : (t + 1) * block, :] = value[
                            r * block : (r + 1) * block, t * 128 : (t + 1) * 128
                        ]
                rows = sub // 128 * block
                target = grad_hbm[k % 2].at[k // 2, :, pl.ds(j * rows, rows), :]
            else:
                stage_ref[slot] = value
                target = grad_hbm[0].at[k, :, pl.ds(j * sub, sub)]
            slots[slot] = pltpu.make_async_copy(stage_ref.at[slot], target, out_sem.at[slot])
            slots[slot].start()
    for copy in slots + pending:
        copy.wait()


def grad_t(values):
    return values.astype(F32).T.astype(BF)


def quant_call(place, latent, weight, cot, pick, pieces, halves, n_shard, n_row):
    tokens, width = latent.shape
    codes = sum(piece.shape[0] for piece in pieces)
    shard = codes // n_shard
    n_piece = len(pieces)
    sub = min(SUB, shard)
    block = width // n_row
    more = (n_shard, n_row, pick.shape[1] // 128 * block + 2 * shard // 128, 128)
    if halves:
        rows = shard // 128 * block + more[2]
        grads = [jax.ShapeDtypeStruct((n_shard // 2, n_row, rows, 128), BF)] * 2
        stage = (2, n_row, sub // 128 * block, 128)
    else:
        grads = [jax.ShapeDtypeStruct((n_shard, width, shard), BF)]
        stage = (2, width, sub)
        more = (1, 1, 16, 128)
    outs = [
        jax.ShapeDtypeStruct((tokens, width), F32),
        jax.ShapeDtypeStruct((tokens, width), BF),
        jax.ShapeDtypeStruct((DEPTH, tokens, width), BF),
        jax.ShapeDtypeStruct((2, codes), F32),
    ] + grads
    return pl.pallas_call(
        functools.partial(quant_kernel, n_shard, halves, n_piece),
        out_shape=outs,
        in_specs=[smem(), vmem(), vmem(), vmem(), vmem()] + [hbm()] * n_piece,
        out_specs=[vmem()] * 4 + [hbm()] * len(grads),
        scratch_shapes=[
            pltpu.VMEM((codes, width), BF),
            pltpu.VMEM((width, codes), BF),
            pltpu.VMEM((tokens, codes // 2), F32),
            pltpu.VMEM((2 * DEPTH * tokens, codes), BF),
            pltpu.VMEM((DEPTH + 1, tokens, width), F32),
            pltpu.VMEM((DEPTH, tokens, width), F32),
            pltpu.VMEM((DEPTH, 2, tokens, 128), F32),
            pltpu.VMEM((2, width, 2 * DEPTH * tokens), BF),
            pltpu.VMEM((2, tokens, width), F32),
            pltpu.VMEM((2, 8, codes), F32),
            pltpu.VMEM((1, codes), F32),
            pltpu.VMEM((tokens, width), F32),
            pltpu.VMEM(stage, BF),
            pltpu.VMEM(more, BF),
            pltpu.SemaphoreType.DMA((n_piece,)),
            pltpu.SemaphoreType.DMA((2,)),
            pltpu.SemaphoreType.DMA((n_shard,)),
        ],
        compiler_params=pltpu.CompilerParams(vmem_limit_bytes=63 * MIB),
        cost_estimate=pl.CostEstimate(
            flops=48 * tokens * width * codes,
            bytes_accessed=18 * MIB,
            transcendentals=DEPTH * tokens * codes,
        ),
        name="soft_quantize",
    )(place, latent, weight, cot, pick, *pieces)


def slope(values):
    sigma = jax.nn.sigmoid(values)
    return sigma * (1.0 + values * (1.0 - sigma))


def norm_back(grad, normed, inverse, gain, per_group, count):
    dn = grad * gain
    first = group_sum(col_sum(dn), per_group) * (1.0 / count)
    second = group_sum(col_sum(dn * normed), per_group) * (1.0 / count)
    return inverse * (dn - first - normed * second)


def conv_back_image(pad_ref, crop, w_ref, side, pixels):
    total = None
    for tap in range(9):
        a, b = tap // 3, tap % 3
        rows = pad_ref[crop, 2 - b, side * (2 - a) : side * (2 - a) + pixels, :]
        part = mm(rows, w_ref[tap], NT)
        total = part if total is None else total + part
    return total


def act_back(read, dact_ref, stats_ref, norm_ref, stage, crops, pixels, channels, grads_ref, store):
    per_group = channels // GROUPS
    count = float(pixels * per_group)
    for k in chunks(channels):
        gain_row = norm_ref[2 * stage : 2 * stage + 1, k]
        bias_row = norm_ref[2 * stage + 1 : 2 * stage + 2, k]
        grad_gain = jnp.zeros((1, 128), F32)
        grad_bias = jnp.zeros((1, 128), F32)
        for c in range(crops):
            inverse = stats_ref[c, 2 * stage + 1 : 2 * stage + 2, k]
            normed = (read(c, k) - stats_ref[c, 2 * stage : 2 * stage + 1, k]) * inverse
            dout = dact_ref[c, :, k] * slope(normed * gain_row + bias_row)
            grad_gain = grad_gain + col_sum(dout * normed)
            grad_bias = grad_bias + col_sum(dout)
            store(c, k, norm_back(dout, normed, inverse, gain_row, per_group, count))
        grads_ref[0:1, k] = grad_gain
        grads_ref[1:2, k] = grad_bias


def second_kernel(
    side,
    dlat_ref,
    pj_ref,
    stats_ref,
    norm_ref,
    dn_hbm,
    conv_hbm,
    w_hbm,
    low_ref,
    dn_ref,
    conv_ref,
    w_ref,
    pad_ref,
    dact_ref,
    ngrad_ref,
    sem,
):
    crops, pixels, channels = conv_ref.shape
    lat = pixels // 4
    tokens, width = dlat_ref.shape
    pairs = ((dn_hbm, dn_ref), (w_hbm.at[1], w_ref), (conv_hbm, conv_ref))
    copies = [pltpu.make_async_copy(*pair, sem.at[k]) for k, pair in enumerate(pairs)]
    for copy in copies:
        copy.start()
    zero_borders(pad_ref, side)
    dlat = dlat_ref[...]
    dred = mm(dlat, pj_ref[...], NT).astype(BF)
    base = 2 * crops * pixels
    low_ref[base : base + tokens, :] = dred
    low_ref[base + tokens : base + 2 * tokens, 0:width] = dlat
    low_ref[base + tokens : base + 2 * tokens, width:] = jnp.zeros((tokens, channels - width), BF)
    order = pixel_order(pixels, side)
    copies[0].wait()
    pieces = [mm(dred, dn_ref[tap], NT).astype(BF) for tap in range(4)]
    for c in range(crops):
        mixed = jnp.concatenate([p[c * lat : (c + 1) * lat] for p in pieces], axis=0)
        low_ref[c * pixels : (c + 1) * pixels, :] = mm(order, mixed, TN).astype(BF)
        for k in chunks(channels):
            rows = low_ref[c * pixels : (c + 1) * pixels, k].astype(F32)
            put_shifted(pad_ref, c, k, rows, side)
    for copy in copies[1:]:
        copy.wait()
    for c in range(crops):
        dact_ref[c] = conv_back_image(pad_ref, c, w_ref, side, pixels)

    def read(c, k):
        return conv_ref[c, :, k]

    def store(c, k, value):
        at = (crops + c) * pixels
        low_ref[at : at + pixels, k] = value.astype(BF)

    act_back(read, dact_ref, stats_ref, norm_ref, 1, crops, pixels, channels, ngrad_ref, store)
    ngrad_ref[2:8, :] = jnp.zeros((6, channels), F32)
    lines = jnp.concatenate([ngrad_ref[...], jnp.zeros((8, channels), F32)], axis=0)
    low_ref[base + 2 * tokens : base + 2 * tokens + 16, :] = lines.astype(BF)


def second_call(dlat, pj, stats, norm, dn, conv, w, side):
    crops, pixels, channels = conv.shape
    tokens = dlat.shape[0]
    return pl.pallas_call(
        functools.partial(second_kernel, side),
        out_shape=jax.ShapeDtypeStruct((2 * crops * pixels + 2 * tokens + 16, channels), BF),
        in_specs=[vmem()] * 4 + [hbm()] * 3,
        out_specs=vmem(),
        scratch_shapes=[
            pltpu.VMEM(dn.shape, BF),
            pltpu.VMEM(conv.shape, F32),
            pltpu.VMEM(w.shape[1:], BF),
            pltpu.VMEM((crops, 3, pixels + 2 * side, channels), BF),
            pltpu.VMEM(conv.shape, F32),
            pltpu.VMEM((8, channels), F32),
            pltpu.SemaphoreType.DMA((3,)),
        ],
        compiler_params=pltpu.CompilerParams(vmem_limit_bytes=LIMIT),
        cost_estimate=SMALL_COST,
        name="second_backward",
    )(dlat, pj, stats, norm, dn, conv, w)


def first_kernel(
    side, x_ref, stats_ref, norm_ref, low_ref, w_hbm, image_ref, ngrad_ref, w_ref, pad_ref, dact_ref, sem
):
    crops, pixels, channels = x_ref.shape
    copy = pltpu.make_async_copy(w_hbm.at[0], w_ref, sem.at[0])
    copy.start()
    zero_borders(pad_ref, side)

    def read(c, k):
        return x_ref[c, :, k].astype(F32)

    def store(c, k, value):
        rows = low_ref[c * pixels : (c + 1) * pixels, k].astype(F32)
        image_ref[c, :, k] = (value + rows).astype(BF)

    for c in range(crops):
        at = (crops + c) * pixels
        for k in chunks(channels):
            put_shifted(pad_ref, c, k, low_ref[at : at + pixels, k].astype(F32), side)
    copy.wait()
    for c in range(crops):
        dact_ref[c] = conv_back_image(pad_ref, c, w_ref, side, pixels)
    act_back(read, dact_ref, stats_ref, norm_ref, 0, crops, pixels, channels, ngrad_ref, store)
    ngrad_ref[2:8, :] = jnp.zeros((6, channels), F32)


def first_call(x, stats, norm, low, w, side):
    crops, pixels, channels = x.shape
    return pl.pallas_call(
        functools.partial(first_kernel, side),
        out_shape=[
            jax.ShapeDtypeStruct((crops, pixels, channels), BF),
            jax.ShapeDtypeStruct((8, channels), F32),
        ],
        in_specs=[vmem()] * 4 + [hbm()],
        out_specs=[vmem()] * 2,
        scratch_shapes=[
            pltpu.VMEM(w.shape[1:], BF),
            pltpu.VMEM((crops, 3, pixels + 2 * side, channels), BF),
            pltpu.VMEM(x.shape, F32),
            pltpu.SemaphoreType.DMA((1,)),
        ],
        compiler_params=pltpu.CompilerParams(vmem_limit_bytes=LIMIT),
        cost_estimate=SMALL_COST,
        name="first_backward",
    )(x, stats, norm, low, w)


BLOCK = 64
TAIL = 48


def matrix_kernel(side, crops, pixels, width, plan, n_set, place_ref, *refs):
    sources, refs = refs[: 3 * n_set], refs[3 * n_set :]
    n_out = 2 * len(plan) if plan else 1
    targets, refs = refs[:n_out], refs[n_out:]
    saves, refs = refs[:n_set], refs[n_set:]
    lows, refs = refs[:n_set], refs[n_set:]
    norms, refs = refs[:n_set], refs[n_set:]
    outs, (pad_ref, in_sem, out_sem) = refs[:n_out], refs[n_out:]
    channels = pad_ref.shape[3]
    locals_ = list(saves) + list(lows) + list(norms)
    image = crops * pixels
    loads = []
    for save_at, low_at in ((image, 0), (2 * image, 2 * image), (0, image)):
        group = []
        for k in range(2 * n_set):
            at = save_at if k < n_set else low_at
            count = image if at < 2 * image else sources[k].shape[0] - 2 * image
            rows = pl.ds(at, count)
            group.append(
                pltpu.make_async_copy(
                    sources[k].at[rows, :], locals_[k].at[rows, :], in_sem.at[len(loads), k]
                )
            )
        loads.append(group)
    for k in range(2 * n_set, 3 * n_set):
        loads[1].append(pltpu.make_async_copy(sources[k], locals_[k], in_sem.at[1, k]))
    for group in loads:
        for load in group:
            load.start()
    stores = [
        pltpu.make_async_copy(outs[k], targets[k].at[pl.ds(0, outs[k].shape[0])], out_sem.at[k])
        for k in range(n_out)
    ]
    done = {}
    tokens = crops * pixels // 4
    odd = place_ref[1] % 2 == 1
    line = place_ref[1] // 2 % 2
    dp = place_ref[0]
    zero_borders(pad_ref, side)

    def arrive(group):
        for load in loads[group]:
            load.wait()

    def half(values):
        if not plan:
            return values
        parts = []
        for k in range(0, values.shape[1], 256):
            parts.append(jnp.where(odd, values[:, k + 128 : k + 256], values[:, k : k + 128]))
        return jnp.concatenate(parts, axis=1)

    def low_rows(at, count):
        return jnp.concatenate([half(low[at : at + count, :]) for low in lows], axis=0)

    def squeeze(index, bit):
        return (index >> (bit + 1) << bit) | (index & ((1 << bit) - 1))

    def place_rows(part, row, count, value):
        keep_ref, send_ref = outs[2 * part], outs[2 * part + 1]
        rows = keep_ref.shape[1]
        name = plan[part][1].split()[0]

        def put(lead, keep, send):
            keep_ref[lead, row : row + count, :] = keep
            send_ref[pl.ds(pl.multiple_of(lead * rows + row, 16), count), :] = send

        if name == "x":
            far = line == 1
            keep = jnp.where(far, value[:, 128:], value[:, :128])
            send = jnp.where(far, value[:, :128], value[:, 128:])
            for i in range(8):
                at = slice(i * count, (i + 1) * count)
                put(i ^ dp, keep[at], send[at])
            return
        bit = {"y": 0, "z1": 1, "z2": 2}[name]
        other = (dp >> bit) & 1 == 1
        for pair in range(2):
            lead = (pair ^ line) * 4
            for i in range(8):
                if i >> bit & 1:
                    continue
                j = i | 1 << bit
                lanes = slice(pair * 128, pair * 128 + 128)
                first = value[i * count : (i + 1) * count, lanes]
                second = value[j * count : (j + 1) * count, lanes]
                put(
                    lead + (squeeze(i, bit) ^ squeeze(dp, bit)),
                    jnp.where(other, second, first),
                    jnp.where(other, first, second),
                )

    def store(block, value):
        value = value.astype(BF)
        if not plan:
            outs[0][block * channels : (block + 1) * channels, 0 : value.shape[1]] = value
            return
        part = 0
        while block >= plan[part][0] // 4:
            block -= plan[part][0] // 4
            part += 1
        place_rows(part, block * BLOCK, BLOCK, value)
        done[part] = done.get(part, 0) + 4
        if done[part] == plan[part][0]:
            stores[2 * part].start()
            stores[2 * part + 1].start()

    def taps(save_at, low_at, first_block):
        for n, save in enumerate(saves):
            for c in range(crops):
                for k in chunks(channels):
                    rows = save[save_at + c * pixels : save_at + (c + 1) * pixels, k]
                    put_shifted(pad_ref, n * crops + c, k, rows.astype(F32), side)
        grad = low_rows(low_at, crops * pixels)
        for tap in range(9):
            a, b = tap // 3, tap % 3
            rows = [
                pad_ref[c, b, side * a : side * a + pixels, :] for c in range(n_set * crops)
            ]
            store(first_block + tap, mm(jnp.concatenate(rows, axis=0), grad, TN))

    arrive(0)
    taps(crops * pixels, 0, 0)
    arrive(1)
    base = 2 * crops * pixels
    dred = low_rows(base, tokens)
    for tap in range(4):
        at = base + tap * tokens
        rows = jnp.concatenate([save[at : at + tokens, :] for save in saves], axis=0)
        store(9 + tap, mm(rows, dred, TN))
    arrive(2)
    taps(0, crops * pixels, 13)
    at = base + 4 * tokens
    rows = jnp.concatenate([save[at : at + tokens, :] for save in saves], axis=0)
    dlat = [low[base + tokens : base + 2 * tokens, 0:width] for low in lows]
    if not plan:
        store(22, mm(rows, dlat[0], TN))
        stores[0].start()
        stores[0].wait()
        return
    narrow = []
    for part in dlat:
        pieces = [part[:, k : k + 64] for k in range(0, width, 64)]
        narrow.append(
            jnp.concatenate(
                [
                    jnp.where(odd, pieces[1], pieces[0]),
                    jnp.where(odd, pieces[3], pieces[2]),
                ],
                axis=1,
            )
        )
    proj = mm(rows, jnp.concatenate(narrow, axis=0), TN).astype(BF)
    lines = []
    first = norms[0][0:2, :] + norms[1][0:2, :]
    at = base + 2 * tokens
    second = lows[0][at : at + 16, :].astype(F32) + lows[1][at : at + 16, :].astype(F32)
    for rows in (first, second[0:2]):
        for k in range(2):
            lines += [rows[k : k + 1, lanes] for lanes in chunks(channels)]
    lines = jnp.concatenate(lines, axis=0).astype(BF)
    folded = []
    for i in range(8):
        top = proj[i * 64 : i * 64 + 32]
        low = proj[i * 64 + 32 : (i + 1) * 64]
        block = jnp.concatenate([top[:, 0:64], low[:, 0:64], top[:, 64:], low[:, 64:]], axis=1)
        folded.append(
            jnp.concatenate([block, jnp.concatenate([lines, lines], axis=1)], axis=0)
        )
    last = len(plan) - 1
    place_rows(last, outs[2 * last].shape[1] - TAIL, TAIL, jnp.concatenate(folded, axis=0))
    stores[2 * last].start()
    stores[2 * last + 1].start()
    for store_ in stores:
        store_.wait()


def matrix_call(place, saves, lows, norms, side, crops, pixels, width, plan, room=None):
    channels = saves[0].shape[1]
    n_set = len(saves)
    if plan:
        outs, shapes = [], []
        for units, order in plan:
            rows = 8 * 16 * units
            shapes += [(8, 16 * units, 128), (rows, 128)]
            outs.append(jax.ShapeDtypeStruct(shapes[-2], BF))
            outs.append(jax.ShapeDtypeStruct((rows + room.get(order.split()[0], 0), 128), BF))
    else:
        outs = [jax.ShapeDtypeStruct((23 * channels, channels), BF)]
        shapes = [outs[0].shape]
    return pl.pallas_call(
        functools.partial(matrix_kernel, side, crops, pixels, width, plan, n_set),
        out_shape=outs,
        in_specs=[smem()] + [hbm()] * (3 * n_set),
        out_specs=[hbm()] * len(outs),
        scratch_shapes=[pltpu.VMEM(a.shape, a.dtype) for a in (*saves, *lows, *norms)]
        + [pltpu.VMEM(shape, BF) for shape in shapes]
        + [
            pltpu.VMEM((n_set * crops, 3, pixels + 2 * side, channels), BF),
            pltpu.SemaphoreType.DMA((3, 3 * n_set)),
            pltpu.SemaphoreType.DMA((len(outs),)),
        ],
        compiler_params=pltpu.CompilerParams(vmem_limit_bytes=LIMIT),
        cost_estimate=SMALL_COST,
        name="matrix_backward",
    )(place, *saves, *lows, *norms)


def swap(array, axis, bit):
    count = lax.axis_size(axis)
    return lax.ppermute(array, axis, [(i, i ^ bit) for i in range(count)])


def add_low(first, second):
    return (first.astype(F32) + second.astype(F32)).astype(BF)


LINKS = {"x": ("code", 2), "y": ("dp", 1), "z1": ("dp", 2), "z2": ("dp", 4)}
BITS = ("x", "z2", "z1", "y")
CODE_PLAN = ((36, "z1 x y z2"), (36, "x y z1 z2"))
MATRIX_PLAN = ((28, "x y z1 z2"), (40, "z1 x y z2"), (23, "y z2 x z1"))


class Part:
    def __init__(self, array, low, rows, order, arrival):
        self.array, self.low, self.rows = array, low, rows
        self.order, self.dims = order.split(), list(BITS)
        self.arrival, self.offset = arrival, None


def split_parts(keep, arrival, plan):
    shape = (keep.shape[0] * keep.shape[1],) + keep.shape[2:]
    keep, arrival = keep.reshape(shape), arrival.reshape(shape)
    assert 16 * sum(units for units, _ in plan) == shape[1]
    parts, low = [], 0
    for units, order in plan:
        parts.append(Part(keep, low, 16 * units, order, arrival))
        low += 16 * units
    return parts


def merge_kernel(jobs, n_in, n_out, *refs):
    ins, outs, scratch = refs[:n_in], refs[n_in : n_in + n_out], refs[n_in + n_out :]
    sem = scratch[-1]
    loads, stores = [], []
    for j, job in enumerate(jobs):
        mine, other = scratch[4 * j], scratch[4 * j + 1]
        source = ins[job["array"]].at[:, pl.ds(job["low"], job["rows"]), :]
        first = pltpu.make_async_copy(source, mine, sem.at[4 * j])
        if job["flat"] is None:
            source = ins[job["arrival"]].at[:, pl.ds(job["low"], job["rows"]), :]
        else:
            source = ins[job["arrival"]].at[pl.ds(job["flat"], other.shape[0]), :]
        second = pltpu.make_async_copy(source, other, sem.at[4 * j + 1])
        first.start()
        second.start()
        loads.append((first, second))
    for j, job in enumerate(jobs):
        mine, other, keep, send = scratch[4 * j : 4 * j + 4]
        for load in loads[j]:
            load.wait()
        rows, count = job["rows"], [0, 0]
        for lead in range(mine.shape[0]):
            at = slice(lead * rows, (lead + 1) * rows)
            value = add_low(mine[lead], other[lead] if job["flat"] is None else other[at, :])
            half = lead >> job["bit"] & 1
            if half == 0:
                keep[count[0]] = value
            else:
                send[count[1] * rows : (count[1] + 1) * rows, :] = value
            count[half] += 1
        target = outs[job["send"]].at[pl.ds(job["place"], send.shape[0]), :]
        for pair in ((keep, outs[job["keep"]]), (send, target)):
            copy = pltpu.make_async_copy(*pair, sem.at[4 * j + 2 + len(stores) % 2])
            copy.start()
            stores.append(copy)
    for copy in stores:
        copy.wait()


def operand_index(arrays, array):
    for k, known in enumerate(arrays):
        if known is array:
            return k
    arrays.append(array)
    return len(arrays) - 1


def merge(parts, given=()):
    sizes, groups = {}, {}
    arrays, jobs, scratch = [], [], []
    for name, _, group in given:
        groups[name] = list(group)
        sizes[name] = sum(p.rows * 2 ** (len(p.dims) - 1) for p in group)
    names = sorted({p.order[0] for p in parts})
    for k, part in enumerate(parts):
        lead = 2 ** len(part.dims)
        name = part.order[0]
        jobs.append(
            {
                "array": operand_index(arrays, part.array),
                "arrival": operand_index(arrays, part.arrival),
                "low": part.low,
                "rows": part.rows,
                "flat": part.offset,
                "keep": k,
                "bit": len(part.dims) - 1 - part.dims.index(name),
                "send": len(parts) + names.index(name),
                "place": sizes.get(name, 0),
            }
        )
        part.offset = sizes.get(name, 0)
        sizes[name] = part.offset + part.rows * lead // 2
        groups.setdefault(name, []).append(part)
        flat = jobs[-1]["flat"] is not None
        scratch += [
            pltpu.VMEM((lead, part.rows, 128), BF),
            pltpu.VMEM((lead * part.rows, 128) if flat else (lead, part.rows, 128), BF),
            pltpu.VMEM((lead // 2, part.rows, 128), BF),
            pltpu.VMEM((lead // 2 * part.rows, 128), BF),
        ]
    outs = [jax.ShapeDtypeStruct((2 ** (len(p.dims) - 1), p.rows, 128), BF) for p in parts]
    outs += [jax.ShapeDtypeStruct((sizes[name], 128), BF) for name in names]
    aliases = {}
    for name, array, _ in given:
        if name in names:
            assert array.shape == (sizes[name], 128)
            aliases[len(arrays)] = len(parts) + names.index(name)
            arrays.append(array)
    result = pl.pallas_call(
        functools.partial(merge_kernel, jobs, len(arrays), len(outs)),
        out_shape=outs,
        input_output_aliases=aliases,
        in_specs=[anywhere()] * len(arrays),
        out_specs=[anywhere()] * len(outs),
        scratch_shapes=scratch + [pltpu.SemaphoreType.DMA((4 * len(parts),))],
        compiler_params=pltpu.CompilerParams(vmem_limit_bytes=LIMIT),
        cost_estimate=SMALL_COST,
        name="merge_parts",
    )(*arrays)
    for k, part in enumerate(parts):
        part.array, part.low, part.arrival = result[k], 0, None
    sends = [(name, result[len(parts) + k], groups[name]) for k, name in enumerate(names)]
    return sends + [entry for entry in given if entry[0] not in names]


def fly(sends):
    return [(name, swap(array, *LINKS[name]), group) for name, array, group in sends]


def land(flights, *others):
    tied = lax.optimization_barrier(tuple(array for _, array, _ in flights) + tuple(others))
    for (name, _, group), array in zip(flights, tied):
        for part in group:
            part.order.pop(0)
            part.dims.remove(name)
            part.arrival = array
    return tied[len(flights) :]


def final_kernel(
    n_code, parts, n_in, rates, code_rate, mean_count, *refs
):
    n_all = n_in + 18
    sources, targets, refs = refs[:n_all], refs[n_all : n_all + 16], refs[n_all + 16 :]
    locals_, outs, refs = refs[:n_all], refs[n_all : n_all + 16], refs[n_all + 16 :]
    code_ref, mat_ref, in_sem, out_sem = refs
    loads = [pltpu.make_async_copy(sources[k], locals_[k], in_sem.at[k]) for k in range(n_all)]
    for load in loads:
        load.start()
    stores = [pltpu.make_async_copy(outs[k], targets[k], out_sem.at[k]) for k in range(16)]
    ins = locals_[:n_in]
    (
        conv_m, conv_v, conv_a, down_m, down_v, down_a, proj_m, proj_v, proj_a,
        norm_m, norm_v, norm_a, code_m, code_v, code_a, own_ref, select_ref, chosen_ref,
    ) = locals_[n_in:]
    for load in loads[:n_in]:
        load.wait()
    at = [0, 0]
    for k, part in enumerate(parts):
        which = 0 if k < n_code else 1
        target = (code_ref, mat_ref)[which]
        rows = part["rows"]
        value = ins[part["array"]][0].astype(F32)
        value = value + ins[part["arrival"]][part["offset"] : part["offset"] + rows, :].astype(F32)
        target[at[which] : at[which] + rows, :] = value
        at[which] += rows

    def step(refs, index, grad, rate, results):
        master, moment, average = refs
        moment_new = MOMENTUM * moment[index] + grad
        master_new = master[index] - rate * (grad + MOMENTUM * moment_new)
        results[0][index] = moment_new
        results[1][index] = master_new
        results[2][index] = AVERAGE_DECAY * average[index] + (1.0 - AVERAGE_DECAY) * master_new

    for load in loads[n_in : n_in + 12]:
        load.wait()
    weight_rate, norm_rate = rates
    block = conv_m.shape[0] // 18
    for conv in range(2):
        for tap in range(9):
            row = (13 + tap if conv == 0 else tap) * block
            index = (pl.ds(tap * 2 + conv, block, stride=18), slice(None))
            grad = mat_ref[row : row + block, :]
            step((conv_m, conv_v, conv_a), index, grad, weight_rate, outs[0:3])
    for tap in range(4):
        index = (pl.ds(tap, block, stride=4), slice(None))
        grad = mat_ref[(9 + tap) * block : (10 + tap) * block, :]
        step((down_m, down_v, down_a), index, grad, weight_rate, outs[3:6])
    tail = 22 * block
    for k in range(2):
        index = (slice(k * block // 2, (k + 1) * block // 2), slice(None))
        grad = mat_ref[tail : tail + block // 2, k * 64 : (k + 1) * 64]
        step((proj_m, proj_v, proj_a), index, grad, weight_rate, outs[6:9])
    tail += block // 2
    lines = norm_m.shape[1] // 128
    for k in range(4):
        for j in range(lines):
            index = (slice(k, k + 1), slice(j * 128, (j + 1) * 128))
            row = tail + k * lines + j
            step((norm_m, norm_v, norm_a), index, mat_ref[row : row + 1, :], norm_rate, outs[9:12])

    for store in stores[:12]:
        store.start()
    for load in loads[n_in + 12 :]:
        load.wait()
    cols, codes = code_m.shape
    tiles = codes // 128
    base = tiles * cols
    spans = select_ref.shape[0] // 128
    source = jnp.concatenate(
        [code_ref[base + k * cols : base + (k + 1) * cols, :] for k in range(spans)], axis=1
    ).astype(BF)
    base += spans * cols
    counts = code_ref[base : base + tiles, :]
    outs[15][...] = counts * (1.0 / mean_count)
    wide = 512
    for k in range(codes // wide):
        lanes = slice(k * wide, (k + 1) * wide)
        four = range(k * wide // 128, (k + 1) * wide // 128)
        grad = jnp.concatenate([code_ref[t * cols : (t + 1) * cols, :] for t in four], axis=1)
        slope_sum = jnp.concatenate(
            [code_ref[base + tiles + t : base + tiles + t + 1, :] for t in four], axis=1
        )
        count = jnp.concatenate([code_ref[base + t : base + t + 1, :] for t in four], axis=1)
        grad = grad - own_ref[:, lanes].astype(F32) * slope_sum
        moment_new = MOMENTUM * code_v[:, lanes] + grad
        stepped = code_m[:, lanes] - code_rate * (grad + MOMENTUM * moment_new)
        renewed = mm(source, select_ref[:, lanes])
        share = chosen_ref[:, lanes] * (mean_count / (mean_count + count))
        master_new = stepped + share * (renewed - stepped)
        outs[12][:, lanes] = moment_new
        outs[13][:, lanes] = master_new
        outs[14][:, lanes] = (
            AVERAGE_DECAY * code_a[:, lanes] + (1.0 - AVERAGE_DECAY) * master_new
        )
    for store in stores[12:]:
        store.start()
    for store in stores:
        store.wait()


def final_call(codes, mats, states, own, select, chosen, rates, code_rate, mean_count):
    arrays, parts = [], []
    for part in codes + mats:
        parts.append(
            {
                "array": operand_index(arrays, part.array),
                "arrival": operand_index(arrays, part.arrival),
                "offset": part.offset,
                "rows": part.rows,
            }
        )
    shapes = [states[k].shape for k in (0, 0, 0, 3, 3, 3, 6, 6, 6, 9, 9, 9, 12, 12, 12)]
    outs = [jax.ShapeDtypeStruct(shape, F32) for shape in shapes]
    outs.append(jax.ShapeDtypeStruct((own.shape[1] // 128, 128), F32))
    args = arrays + list(states) + [own, select, chosen]
    return pl.pallas_call(
        functools.partial(
            final_kernel, len(codes), parts, len(arrays), rates, code_rate, mean_count
        ),
        out_shape=outs,
        in_specs=[hbm()] * len(args),
        out_specs=[hbm()] * len(outs),
        scratch_shapes=[pltpu.VMEM(a.shape, a.dtype) for a in args]
        + [pltpu.VMEM(out.shape, F32) for out in outs]
        + [
            pltpu.VMEM((sum(p.rows for p in codes), 128), F32),
            pltpu.VMEM((sum(p.rows for p in mats), 128), F32),
            pltpu.SemaphoreType.DMA((len(args),)),
            pltpu.SemaphoreType.DMA((16,)),
        ],
        compiler_params=pltpu.CompilerParams(vmem_limit_bytes=LIMIT),
        cost_estimate=SMALL_COST,
        name="updates",
    )(*args)


def nesterov_step(master, moment, average, grad, rate):
    moment_new = MOMENTUM * moment + grad
    master_new = master - rate * (grad + MOMENTUM * moment_new)
    return (moment_new, master_new, AVERAGE_DECAY * average + (1.0 - AVERAGE_DECAY) * master_new)


def body(
    crops_in,
    crop_weight,
    cotangent,
    conv_copy,
    down_copy,
    proj_copy,
    norm_copy,
    codebook,
    conv_master,
    conv_moment,
    conv_average,
    down_master,
    down_moment,
    down_average,
    proj_master,
    proj_moment,
    proj_average,
    norm_master,
    norm_moment,
    norm_average,
    code_master,
    code_moment,
    code_average,
    repl_code,
    repl_src,
):
    dp_count = lax.axis_size("dp")
    code_count = lax.axis_size("code")
    dp_at = lax.axis_index("dp")
    code_at = lax.axis_index("code")
    halves = dp_count == 8 and code_count == 4
    place = jnp.stack([dp_at, code_at]).astype(jnp.int32)

    local = lax.all_to_all(crops_in, "dp", split_axis=1, concat_axis=2, tiled=True)[0]
    crop_dev, pixels, channels = local.shape
    side = math.isqrt(pixels)
    lat = pixels // 4
    tokens = crop_dev * lat
    width = proj_copy.shape[1]
    code_dev = codebook.shape[0]
    codes_all = code_dev * code_count

    crops_set = crop_dev * dp_count
    flat_src = repl_src.reshape(-1)
    crop_id = flat_src // lat % crops_set
    owner = (crop_id // crop_dev == dp_at) & (flat_src // (crops_set * lat) == code_at)
    row_id = crop_id % crop_dev * lat + flat_src % lat
    depth_id = jnp.repeat(jnp.arange(DEPTH, dtype=jnp.int32), repl_src.shape[1])
    pick = (
        jnp.where(owner, depth_id * tokens + row_id, -1)[None, :]
        == jnp.arange(DEPTH * tokens, dtype=jnp.int32)[:, None]
    ).astype(BF)
    weight_col = jnp.broadcast_to(
        crop_weight.astype(F32).reshape(crop_dev, 1), (crop_dev, lat)
    ).reshape(tokens, 1)
    w = conv_copy.transpose(1, 2, 0, 3)
    dn = down_copy.transpose(1, 0, 2)
    gains = norm_copy.T.astype(F32)
    if halves:
        quarter = code_dev // 4
        corner = (dp_at & 1) * 2 + ((dp_at >> 1) & 1)
        mine = lax.dynamic_slice_in_dim(codebook, corner * quarter, quarter, 0)
        over_x = swap(mine, "code", 2)
        over_y, over_z = swap(over_x, "dp", 1), swap(over_x, "dp", 2)
        core = swap(codebook, "code", 1)
        diag = [swap(over_x, "code", 1)]
        over_y, over_z, local, w, dn, gains, core, diag[0], pick, weight_col, place = (
            lax.optimization_barrier(
                (over_y, over_z, local, w, dn, gains, core, diag[0], pick, weight_col, place)
            )
        )
        last = [swap(over_z[: quarter // 2], "dp", 1), swap(over_y[quarter // 2 :], "dp", 2)]
        diag = diag + [swap(piece, "code", 1) for piece in (over_y, over_z)]
    else:
        every = lax.all_gather(codebook, "code", axis=0)
        pieces = [every[k] for k in range(code_count)]

    conv1, stats, save, latent = forward_call(local, gains, w, dn, proj_copy, side)
    if halves:
        last[0], last[1], latent = lax.optimization_barrier((last[0], last[1], latent))
        diag = diag + [swap(piece, "code", 1) for piece in last]
        pieces = [codebook, core, over_x, over_y, over_z] + last + diag
        saves = (save, swap(save, "code", 1))

    n_row = dp_count if halves else 1
    quantized, dlat, rows, extra, *code_grads = quant_call(
        place,
        latent,
        weight_col,
        cotangent.reshape(tokens, width),
        pick,
        pieces,
        halves,
        code_count,
        n_row,
    )
    pixels_all = crop_dev * pixels * dp_count * code_count
    weight_rate = WEIGHT_RATE / math.sqrt(pixels_all)
    norm_rate = NORM_RATE / math.sqrt(pixels_all)
    crops_all = crop_dev * dp_count * code_count
    mean_count = DEPTH * lat * crops_all / codes_all
    code_rate = CODE_RATE / math.sqrt(mean_count)
    own_codes = lax.dynamic_slice_in_dim(codebook, dp_at * (width // dp_count), width // dp_count, 1).T
    select = (
        repl_code.reshape(-1)[:, None] - code_at * code_dev
        == jnp.arange(code_dev, dtype=jnp.int32)[None, :]
    )
    chosen = jnp.sum(select.astype(F32), axis=0)
    low = second_call(dlat, proj_copy, stats, gains, dn, conv1, w, side)

    if halves:
        code_core = swap(code_grads[1], "code", 1)
        low_mate = swap(low, "code", 1)
        code_core, low, save_mate = lax.optimization_barrier((code_core, low, saves[1]))
        codes = split_parts(code_grads[0], code_core, CODE_PLAN)
        sends = merge(codes)
        tied = lax.optimization_barrier(tuple(array for _, array, _ in sends) + (low, low_mate))
        low, low_mate = tied[-2:]
        flights = fly([(name, tied[k], group) for k, (name, _, group) in enumerate(sends)])
        image, ngrad = first_call(local, stats, gains, low, w, side)
        ngrad_mate = swap(ngrad, "code", 1)
        input_back = lax.all_to_all(image[None], "dp", split_axis=2, concat_axis=1, tiled=True)
        room = {}
        for part in codes:
            name = part.order[1]
            room[name] = room.get(name, 0) + part.rows * 2 ** (len(part.dims) - 2)
        results = matrix_call(
            place, (save, save_mate), (low, low_mate), (ngrad, ngrad_mate), side, crop_dev, pixels,
            width, MATRIX_PLAN, room,
        )
        mats, given = [], []
        results = land(flights, *results)
        for k, (units, order) in enumerate(MATRIX_PLAN):
            part = Part(results[2 * k], 0, 16 * units, order, None)
            part.offset = 0
            mats.append(part)
            given.append((part.order[0], results[2 * k + 1], [part]))
        flights = fly(merge(codes, given))
        (input_back,) = land(flights, input_back)
        parts = codes + mats
        for _ in range(3):
            land(fly(merge([part for part in parts if part.order])))
        input_back = input_back.astype(F32)

        def flat(array):
            return array.transpose(0, 2, 1, 3).reshape(-1, 128)

        states = [flat(array) for array in (conv_master, conv_moment, conv_average)]
        states += [a.reshape(-1, 128) for a in (down_master, down_moment, down_average)]
        states += [proj_master, proj_moment, proj_average]
        states += [a.T for a in (norm_master, norm_moment, norm_average)]
        states += [a.T for a in (code_master, code_moment, code_average)]
        out = final_call(
            codes, mats, states, own_codes, select.astype(BF), chosen[None, :],
            (weight_rate, norm_rate), code_rate, mean_count,
        )
        rows_in = channels // dp_count
        conv_out = [
            a.reshape(rows_in, 9, 2, channels // code_count).transpose(0, 2, 1, 3) for a in out[0:3]
        ]
        return (
            quantized.reshape(1, crop_dev, lat, width),
            input_back,
            *conv_out,
            *[a.reshape(down_master.shape) for a in out[3:6]],
            *out[6:9],
            *[a.T for a in out[9:12]],
            *[a.T for a in out[12:15]],
            out[15].reshape(code_dev),
        )

    image, ngrad = first_call(local, stats, gains, low, w, side)
    (grads,) = matrix_call(
        place, (save,), (low,), (ngrad,), side, crop_dev, pixels, width, None
    )
    grads = grads.reshape(23, channels, channels)
    base = 2 * crop_dev * pixels + 2 * tokens
    norm_grad = jnp.concatenate([ngrad[0:2], low[base : base + 2].astype(F32)], axis=0)
    flat = lax.psum_scatter(code_grads[0], "code", scatter_dimension=0, tiled=True)[0]
    code_grad = lax.psum_scatter(flat, "dp", scatter_dimension=0, tiled=True).astype(F32)
    sums = lax.psum_scatter(extra, "code", scatter_dimension=1, tiled=True)
    sums = lax.psum(sums, "dp")
    source = mm(rows.reshape(DEPTH * tokens, width), pick, TN).astype(BF)
    source_rows = lax.psum_scatter(source, "dp", scatter_dimension=0, tiled=True)
    source_rows = lax.psum(source_rows, "code")

    def matrix(array, scatter):
        array = lax.psum_scatter(array, "dp", scatter_dimension=0, tiled=True)
        return lax.psum_scatter(array, "code", scatter_dimension=scatter, tiled=True).astype(F32)

    conv_part = matrix(jnp.stack([grads[13:22], grads[0:9]]).transpose(2, 0, 1, 3), 3)
    down_part = matrix(grads[9:13].transpose(1, 0, 2), 2)
    proj_part = matrix(grads[22, :, :width], 1)
    norm_grad = lax.psum(norm_grad, ("dp", "code"))
    input_back = lax.all_to_all(
        image[None], "dp", split_axis=2, concat_axis=1, tiled=True
    ).astype(F32)
    conv_out = nesterov_step(conv_master, conv_moment, conv_average, conv_part, weight_rate)
    down_out = nesterov_step(down_master, down_moment, down_average, down_part, weight_rate)
    proj_out = nesterov_step(proj_master, proj_moment, proj_average, proj_part, weight_rate)
    norm_out = nesterov_step(norm_master, norm_moment, norm_average, norm_grad.T, norm_rate)

    counts_all, slope_sum = sums[0], sums[1]
    share = mean_count / (mean_count + counts_all)
    code_load = counts_all / mean_count
    code_grad = code_grad - own_codes.astype(F32) * slope_sum[None, :]
    code_moment_new = MOMENTUM * code_moment.T + code_grad
    stepped = code_master.T - code_rate * (code_grad + MOMENTUM * code_moment_new)
    renewed = mm(source_rows, select.astype(BF))
    code_master_new = stepped + (chosen * share)[None, :] * (renewed - stepped)
    code_average_new = AVERAGE_DECAY * code_average.T + (1.0 - AVERAGE_DECAY) * code_master_new
    return (
        quantized.reshape(1, crop_dev, lat, width),
        input_back,
        *conv_out,
        *down_out,
        *proj_out,
        *norm_out,
        code_moment_new.T,
        code_master_new.T,
        code_average_new.T,
        code_load,
    )


def solution(mesh):
    in_specs = (
        P("code", None, "dp", None),
        P("code", "dp"),
        P("code", "dp", None, None),
        P(),
        P(),
        P(),
        P(),
        P("code", None),
        P("dp", None, None, "code"),
        P("dp", None, None, "code"),
        P("dp", None, None, "code"),
        P("dp", None, "code"),
        P("dp", None, "code"),
        P("dp", None, "code"),
        P("dp", "code"),
        P("dp", "code"),
        P("dp", "code"),
        P(),
        P(),
        P(),
        P("code", "dp"),
        P("code", "dp"),
        P("code", "dp"),
        P(),
        P(),
    )
    out_specs = (
        P("code", "dp", None, None),
        P("code", None, "dp", None),
        P("dp", None, None, "code"),
        P("dp", None, None, "code"),
        P("dp", None, None, "code"),
        P("dp", None, "code"),
        P("dp", None, "code"),
        P("dp", None, "code"),
        P("dp", "code"),
        P("dp", "code"),
        P("dp", "code"),
        P(),
        P(),
        P(),
        P("code", "dp"),
        P("code", "dp"),
        P("code", "dp"),
        P("code"),
    )
    return jax.shard_map(body, mesh=mesh, in_specs=in_specs, out_specs=out_specs, check_vma=False)
```

```python
import functools
import math

import jax
import jax.numpy as jnp
from jax import lax
from jax.experimental import pallas as pl
from jax.experimental.pallas import tpu as pltpu
from jax.sharding import PartitionSpec as P

GROUPS = 32
DEPTH = 4
BETA = 0.0625
EPSILON = 1e-05
MOMENTUM = 0.5
AVERAGE_DECAY = 0.5
COMMIT = 0.25
WEIGHT_RATE = 0.05
NORM_RATE = 0.5
CODE_RATE = 0.5

BF = jnp.bfloat16
F32 = jnp.float32
NT = (((1,), (1,)), ((), ()))
NN = (((1,), (0,)), ((), ()))
TN = (((0,), (0,)), ((), ()))
MIB = 1 << 20
LIMIT = 62 * MIB
SMALL_COST = pl.CostEstimate(flops=1 << 20, bytes_accessed=1 << 16, transcendentals=0)


def mm(a, b, dims=NN):
    return lax.dot_general(a, b, dims, preferred_element_type=F32)


def vmem():
    return pl.BlockSpec(memory_space=pltpu.VMEM)


def smem():
    return pl.BlockSpec(memory_space=pltpu.SMEM)


def anywhere():
    return pl.BlockSpec(memory_space=pl.ANY)


def hbm():
    return pl.BlockSpec(memory_space=pltpu.HBM)


def group_sum(rows, per_group):
    lanes = rows.shape[1]
    at = lax.broadcasted_iota(jnp.int32, rows.shape, 1)
    step = 1
    while step < per_group:
        up = pltpu.roll(rows, step, 1)
        down = pltpu.roll(rows, lanes - step, 1)
        rows = rows + jnp.where((at & step) != 0, up, down)
        step *= 2
    return rows


def col_sum(values):
    rows, lanes = values.shape
    return jnp.sum(jnp.sum(values.reshape(rows // 8, 8, lanes), axis=0), axis=0, keepdims=True)


def put_shifted(pad_ref, crop, lanes, values, side):
    pixels = values.shape[0]
    col = lax.broadcasted_iota(jnp.int32, values.shape, 0) % side
    left = jnp.where(col == 0, 0.0, pltpu.roll(values, 1, 0))
    right = jnp.where(col == side - 1, 0.0, pltpu.roll(values, pixels - 1, 0))
    for shift, grid in enumerate((left, values, right)):
        pad_ref[crop, shift, side : side + pixels, lanes] = grid.astype(BF)


def zero_borders(pad_ref, side):
    rows = pad_ref.shape[2]
    edge = jnp.zeros((side, pad_ref.shape[3]), BF)
    for crop in range(pad_ref.shape[0]):
        for shift in range(3):
            pad_ref[crop, shift, 0:side, :] = edge
            pad_ref[crop, shift, rows - side : rows, :] = edge


def pixel_order(pixels, side):
    half = side // 2
    lat = half * half
    row = lax.broadcasted_iota(jnp.int32, (pixels, pixels), 0)
    col = lax.broadcasted_iota(jnp.int32, (pixels, pixels), 1)
    tap, pos = row // lat, row % lat
    at = (2 * (pos // half) + tap // 2) * side + 2 * (pos % half) + tap % 2
    return jnp.where(at == col, 1.0, 0.0).astype(BF)


def chunks(channels):
    return [slice(k, k + 128) for k in range(0, channels, 128)]


def norm_stats(read, crops, pixels, channels, per_group):
    count = float(pixels * per_group)
    result = []
    sums = [
        jnp.concatenate([col_sum(read(c, k)) for k in chunks(channels)], axis=1)
        for c in range(crops)
    ]
    means = [group_sum(s, per_group) * (1.0 / count) for s in sums]
    for c in range(crops):
        parts = []
        for k in chunks(channels):
            d = read(c, k) - means[c][:, k]
            parts.append(col_sum(d * d))
        spread = group_sum(jnp.concatenate(parts, axis=1), per_group) * (1.0 / count)
        result.append((means[c], lax.rsqrt(spread + EPSILON)))
    return result


def conv_apply(pad_ref, crop, w_ref, side, pixels):
    total = None
    for b in range(3):
        rows = jnp.concatenate(
            [pad_ref[crop, b, side * a : side * a + pixels, :] for a in range(3)], axis=1
        )
        part = None
        weight = jnp.concatenate([w_ref[3 * a + b] for a in range(3)], axis=0)
        part = mm(rows, weight)
        total = part if total is None else total + part
    return total


def forward_kernel(
    side,
    x_ref,
    norm_ref,
    w_hbm,
    dn_hbm,
    pj_ref,
    conv_hbm,
    stats_ref,
    save_hbm,
    lat_ref,
    w_ref,
    dn_ref,
    pad_ref,
    sum_ref,
    conv_ref,
    sel_ref,
    sem,
):
    crops, pixels, channels = x_ref.shape
    per_group = channels // GROUPS
    lat = pixels // 4
    tokens = crops * lat
    copies = [pltpu.make_async_copy(w_hbm.at[k], w_ref.at[k], sem.at[k]) for k in range(2)]
    dn_copy = pltpu.make_async_copy(dn_hbm, dn_ref, sem.at[2])
    for copy in copies + [dn_copy]:
        copy.start()
    conv_save = pltpu.make_async_copy(conv_ref, conv_hbm, sem.at[3])
    zero_borders(pad_ref, side)
    for stage in range(2):
        if stage == 0:

            def read(c, k):
                return x_ref[c, :, k].astype(F32)

        else:

            def read(c, k):
                return conv_ref[c, :, k]

        stats = norm_stats(read, crops, pixels, channels, per_group)
        for c in range(crops):
            mean, inverse = stats[c]
            stats_ref[c, 2 * stage : 2 * stage + 1, :] = mean
            stats_ref[c, 2 * stage + 1 : 2 * stage + 2, :] = inverse
            for k in chunks(channels):
                normed = (read(c, k) - mean[:, k]) * inverse[:, k]
                out = normed * norm_ref[2 * stage : 2 * stage + 1, k]
                out = out + norm_ref[2 * stage + 1 : 2 * stage + 2, k]
                put_shifted(pad_ref, c, k, out * jax.nn.sigmoid(out), side)
        acts = [
            pltpu.make_async_copy(
                pad_ref.at[c, 1, pl.ds(side, pixels), :],
                save_hbm.at[pl.ds((stage * crops + c) * pixels, pixels), :],
                sem.at[4 + c],
            )
            for c in range(crops)
        ]
        for act in acts:
            act.start()
        copies[stage].wait()
        for c in range(crops):
            total = conv_apply(pad_ref, c, w_ref.at[stage], side, pixels)
            if stage == 0:
                conv_ref[c] = total
            else:
                sum_ref[c] = (x_ref[c].astype(F32) + total).astype(BF)
        for act in acts:
            act.wait()
        if stage == 0:
            conv_save.start()
    order = pixel_order(pixels, side)
    for c in range(crops):
        picked = mm(order, sum_ref[c]).astype(BF)
        for tap in range(4):
            at = tap * tokens + c * lat
            sel_ref[at : at + lat, :] = picked[tap * lat : (tap + 1) * lat]
    dn_copy.wait()
    reduced = mm(sel_ref[0:tokens], dn_ref[0])
    for tap in range(1, 4):
        reduced = reduced + mm(sel_ref[tap * tokens : (tap + 1) * tokens], dn_ref[tap])
    reduced = reduced.astype(BF)
    sel_ref[4 * tokens : 5 * tokens, :] = reduced
    sel_save = pltpu.make_async_copy(
        sel_ref, save_hbm.at[pl.ds(2 * crops * pixels, 5 * tokens), :], sem.at[4 + crops]
    )
    sel_save.start()
    lat_ref[...] = mm(reduced, pj_ref[...]).astype(BF)
    conv_save.wait()
    sel_save.wait()


def forward_call(x, norm, w, dn, pj, side):
    crops, pixels, channels = x.shape
    tokens = crops * pixels // 4
    return pl.pallas_call(
        functools.partial(forward_kernel, side),
        out_shape=[
            jax.ShapeDtypeStruct((crops, pixels, channels), F32),
            jax.ShapeDtypeStruct((crops, 8, channels), F32),
            jax.ShapeDtypeStruct((2 * crops * pixels + 5 * tokens, channels), BF),
            jax.ShapeDtypeStruct((tokens, pj.shape[1]), BF),
        ],
        in_specs=[vmem(), vmem(), hbm(), hbm(), vmem()],
        out_specs=[hbm(), vmem(), hbm(), vmem()],
        scratch_shapes=[
            pltpu.VMEM(w.shape, BF),
            pltpu.VMEM(dn.shape, BF),
            pltpu.VMEM((crops, 3, pixels + 2 * side, channels), BF),
            pltpu.VMEM((crops, pixels, channels), BF),
            pltpu.VMEM((crops, pixels, channels), F32),
            pltpu.VMEM((5 * tokens, channels), BF),
            pltpu.SemaphoreType.DMA((5 + crops,)),
        ],
        compiler_params=pltpu.CompilerParams(vmem_limit_bytes=LIMIT),
        cost_estimate=SMALL_COST,
        name="residual_forward",
    )(x, norm, w, dn, pj)


TILE = 1024
SUB = 1024
SPAN = 4096


def quant_kernel(n_shard, halves, n_piece, place_ref, lat_ref, weight_ref, cot_ref, pick_ref, *rest):
    shard_hbm = rest[:n_piece]
    n_out = 6 if halves else 5
    q_ref, g_ref, rows_ref, extra_ref = rest[n_piece : n_piece + 4]
    grad_hbm = rest[n_piece + 4 : n_piece + n_out]
    (
        code_ref,
        codet_ref,
        score_ref,
        stack_ref,
        res_ref,
        q_level_ref,
        fac_ref,
        side_ref,
        acc_ref,
        count_ref,
        norms_ref,
        carry_ref,
        stage_ref,
        more_ref,
        in_sem,
        out_sem,
        more_sem,
    ) = rest[n_piece + n_out :]
    tokens, width = lat_ref.shape
    codes = code_ref.shape[0]
    shard = codes // n_shard
    part = codes // 2
    tile = min(TILE, part)

    if halves:
        quarter = shard // 4
        corner = (place_ref[0] & 1) * 2 + ((place_ref[0] >> 1) & 1)
        starts = [0, shard]
        for base in (2 * shard, 3 * shard):
            starts += [base + (corner ^ k) * quarter for k in (0, 2, 1, 3)]
            starts.append(starts[-1] + quarter // 2)
    else:
        starts = [k * shard for k in range(n_shard)]
    copies = [
        pltpu.make_async_copy(
            shard_hbm[k],
            code_ref.at[pl.ds(pl.multiple_of(starts[k], 256), shard_hbm[k].shape[0]), :],
            in_sem.at[k],
        )
        for k in range(n_piece)
    ]
    for copy in copies:
        copy.start()

    def fold(values, combine):
        out = values[:, :128]
        for k in range(128, values.shape[1], 128):
            out = combine(out, values[:, k : k + 128])
        return out

    def level_forward(level, first):
        residual = res_ref[level]
        low = residual.astype(BF)
        rows_ref[level] = low
        scaled = low * jnp.asarray(2.0 * BETA, BF)
        at_row = pl.multiple_of(level * tokens, tokens)
        peaks, sums, picks = [], [], []
        for h in range(2):
            best = jnp.full((tokens, 128), -jnp.inf, F32)
            for k in range(part // tile):
                at = h * part + k * tile
                lanes = slice(at, at + tile)
                if first:
                    if halves:
                        if at % shard == 0:
                            group = at // shard
                            for piece in ([group] if group < 2 else range(5 * group - 8, 5 * group - 3)):
                                copies[piece].wait()
                    else:
                        if at % shard == 0:
                            copies[at // shard].wait()
                    for j in range(at, at + tile, 512):
                        turned = code_ref[j : j + 512, :].T
                        codet_ref[:, j : j + 512] = turned
                        wide = turned.astype(F32)
                        norms_ref[:, j : j + 512] = BETA * col_sum(wide * wide)
                s = mm(scaled, codet_ref[:, lanes]) - norms_ref[:, lanes]
                score_ref[:, k * tile : (k + 1) * tile] = s
                best = jnp.maximum(best, fold(s, jnp.maximum))
            peak = jnp.max(best, axis=1, keepdims=True)
            acc_ref[h] = jnp.zeros((tokens, width), F32)

            def power(i, total):
                for k in range(SPAN // tile):
                    at = pl.multiple_of(i * SPAN + k * tile, tile)
                    lanes = pl.ds(pl.multiple_of(h * part + at, tile), tile)
                    p = jnp.exp(score_ref[:, pl.ds(at, tile)] - peak)
                    low_p = p.astype(BF)
                    stack_ref[pl.ds(at_row, tokens), lanes] = low_p
                    acc_ref[h] += mm(low_p, code_ref[lanes, :])
                    total = total + fold(p, jnp.add)
                return total

            total = lax.fori_loop(0, part // SPAN, power, jnp.zeros((tokens, 128), F32))
            peaks.append(peak)
            sums.append(jnp.sum(total, axis=1, keepdims=True))
        top = jnp.maximum(peaks[0], peaks[1])
        scales = [jnp.exp(peak - top) for peak in peaks]
        inverse = 1.0 / (sums[0] * scales[0] + sums[1] * scales[1])
        factors = [scale * inverse for scale in scales]
        for h in range(2):
            fac_ref[level, h] = jnp.broadcast_to(factors[h], (tokens, 128))
        picked = acc_ref[0] * factors[0] + acc_ref[1] * factors[1]
        q_level_ref[level] = picked
        res_ref[level + 1] = residual - picked

    res_ref[0] = lat_ref[...].astype(F32)
    level_forward(0, True)

    def later(level, nothing):
        level_forward(level, False)
        return nothing

    lax.fori_loop(1, DEPTH, later, 0)
    q_ref[...] = (q_level_ref[0] + q_level_ref[1]) + (q_level_ref[2] + q_level_ref[3])

    n_crop = weight_ref.shape[0]
    weight = jnp.concatenate(
        [jnp.full((tokens // n_crop, 1), weight_ref[c], F32) for c in range(n_crop)], axis=0
    )
    count_ref[...] = jnp.zeros(count_ref.shape, F32)
    carry_ref[...] = 2.0 * COMMIT * weight * res_ref[DEPTH]

    def level_back(step, nothing):
        level = DEPTH - 1 - step
        carry = carry_ref[...]
        grad = cot_ref[...].astype(F32) - carry
        dot = jnp.sum(grad * q_level_ref[level], axis=1, keepdims=True)
        ex_row = pl.multiple_of(level * tokens, tokens)
        in_row = pl.multiple_of((DEPTH + level) * tokens, tokens)
        turned_rows = grad_t(rows_ref[level])
        for h in range(2):
            factor = fac_ref[level, h][:, 0:1]
            down = (grad * factor).astype(BF)
            small = down * jnp.asarray(2.0 * BETA, BF)
            total_grad = dot * factor * (-2.0 * BETA)
            share = weight * factor
            side_ref[h, :, pl.ds(ex_row, tokens)] = grad_t(down)
            side_ref[h, :, pl.ds(in_row, tokens)] = turned_rows
            for k in range(part // tile):
                lanes = slice(h * part + k * tile, h * part + (k + 1) * tile)
                p = stack_ref[pl.ds(ex_row, tokens), lanes].astype(F32)
                ds = (mm(small, codet_ref[:, lanes]) + total_grad) * p
                inner = ds.astype(BF)
                stack_ref[pl.ds(in_row, tokens), lanes] = inner
                value = mm(inner, code_ref[lanes, :])
                if h == 0 and k == 0:
                    acc_ref[0] = value
                else:
                    acc_ref[0] += value
                weighted = (p * share).reshape(tokens // 8, 8, tile)
                count_ref[0, :, lanes] += jnp.sum(weighted, axis=0)
                count_ref[1, :, lanes] += jnp.sum(ds.reshape(tokens // 8, 8, tile), axis=0)
        pull = jnp.where(level > 0, 2.0 * COMMIT, 0.0)
        carry_ref[...] = carry + acc_ref[0] + pull * weight * res_ref[level]
        return nothing

    lax.fori_loop(0, DEPTH, level_back, 0)
    g_ref[...] = carry_ref[...].astype(BF)
    extra_ref[0:1, :] = jnp.sum(count_ref[0], axis=0, keepdims=True)
    extra_ref[1:2, :] = jnp.sum(count_ref[1], axis=0, keepdims=True)

    place = place_ref[0]
    pending = []
    n_row = stage_ref.shape[1] if halves else 1
    block = width // n_row
    if halves:
        flat = jnp.concatenate([rows_ref[level] for level in range(DEPTH)], axis=0)
        source = mm(flat, pick_ref[...], TN).astype(BF)
        spans = source.shape[1] // 128
        for k in range(n_shard):
            lines = []
            for row in range(2):
                for at in range(k * shard, (k + 1) * shard, 128):
                    lines.append(extra_ref[row : row + 1, at : at + 128])
            lines = jnp.concatenate(lines, axis=0).astype(BF)
            for r in range(n_row):
                for span in range(spans):
                    more_ref[k, r ^ place, span * block : (span + 1) * block, :] = source[
                        r * block : (r + 1) * block, span * 128 : (span + 1) * 128
                    ]
                more_ref[k, r ^ place, spans * block :, :] = lines
            rows = more_ref.shape[2]
            target = grad_hbm[k % 2].at[k // 2, :, pl.ds(shard // 128 * block, rows), :]
            copy = pltpu.make_async_copy(more_ref.at[k], target, more_sem.at[k])
            copy.start()
            pending.append(copy)
    slots = [None, None]
    for k in range(n_shard):
        for j in range(shard // min(SUB, shard)):
            sub = min(SUB, shard)
            at = k * shard + j * sub
            slot = (at // sub) % 2
            value = mm(side_ref[at // part], stack_ref[:, at : at + sub]).astype(BF)
            if slots[slot] is not None:
                slots[slot].wait()
            if halves:
                for r in range(n_row):
                    for t in range(sub // 128):
                        stage_ref[slot, r ^ place, t * block : (t + 1) * block, :] = value[
                            r * block : (r + 1) * block, t * 128 : (t + 1) * 128
                        ]
                rows = sub // 128 * block
                target = grad_hbm[k % 2].at[k // 2, :, pl.ds(j * rows, rows), :]
            else:
                stage_ref[slot] = value
                target = grad_hbm[0].at[k, :, pl.ds(j * sub, sub)]
            slots[slot] = pltpu.make_async_copy(stage_ref.at[slot], target, out_sem.at[slot])
            slots[slot].start()
    for copy in slots + pending:
        copy.wait()


def grad_t(values):
    return values.astype(F32).T.astype(BF)


def quant_call(place, latent, weight, cot, pick, pieces, halves, n_shard, n_row):
    tokens, width = latent.shape
    codes = sum(piece.shape[0] for piece in pieces)
    shard = codes // n_shard
    n_piece = len(pieces)
    sub = min(SUB, shard)
    block = width // n_row
    more = (n_shard, n_row, pick.shape[1] // 128 * block + 2 * shard // 128, 128)
    if halves:
        rows = shard // 128 * block + more[2]
        grads = [jax.ShapeDtypeStruct((n_shard // 2, n_row, rows, 128), BF)] * 2
        stage = (2, n_row, sub // 128 * block, 128)
    else:
        grads = [jax.ShapeDtypeStruct((n_shard, width, shard), BF)]
        stage = (2, width, sub)
        more = (1, 1, 16, 128)
    outs = [
        jax.ShapeDtypeStruct((tokens, width), F32),
        jax.ShapeDtypeStruct((tokens, width), BF),
        jax.ShapeDtypeStruct((DEPTH, tokens, width), BF),
        jax.ShapeDtypeStruct((2, codes), F32),
    ] + grads
    return pl.pallas_call(
        functools.partial(quant_kernel, n_shard, halves, n_piece),
        out_shape=outs,
        in_specs=[smem(), vmem(), smem(), vmem(), vmem()] + [hbm()] * n_piece,
        out_specs=[vmem()] * 4 + [hbm()] * len(grads),
        scratch_shapes=[
            pltpu.VMEM((codes, width), BF),
            pltpu.VMEM((width, codes), BF),
            pltpu.VMEM((tokens, codes // 2), F32),
            pltpu.VMEM((2 * DEPTH * tokens, codes), BF),
            pltpu.VMEM((DEPTH + 1, tokens, width), F32),
            pltpu.VMEM((DEPTH, tokens, width), F32),
            pltpu.VMEM((DEPTH, 2, tokens, 128), F32),
            pltpu.VMEM((2, width, 2 * DEPTH * tokens), BF),
            pltpu.VMEM((2, tokens, width), F32),
            pltpu.VMEM((2, 8, codes), F32),
            pltpu.VMEM((1, codes), F32),
            pltpu.VMEM((tokens, width), F32),
            pltpu.VMEM(stage, BF),
            pltpu.VMEM(more, BF),
            pltpu.SemaphoreType.DMA((n_piece,)),
            pltpu.SemaphoreType.DMA((2,)),
            pltpu.SemaphoreType.DMA((n_shard,)),
        ],
        compiler_params=pltpu.CompilerParams(vmem_limit_bytes=63 * MIB),
        cost_estimate=pl.CostEstimate(
            flops=48 * tokens * width * codes,
            bytes_accessed=18 * MIB,
            transcendentals=DEPTH * tokens * codes,
        ),
        name="soft_quantize",
    )(place, latent, weight, cot, pick, *pieces)


def slope(values):
    sigma = jax.nn.sigmoid(values)
    return sigma * (1.0 + values * (1.0 - sigma))


def norm_back(grad, normed, inverse, gain, per_group, count):
    dn = grad * gain
    first = group_sum(col_sum(dn), per_group) * (1.0 / count)
    second = group_sum(col_sum(dn * normed), per_group) * (1.0 / count)
    return inverse * (dn - first - normed * second)


def conv_back_image(pad_ref, crop, w_ref, side, pixels):
    total = None
    for tap in range(9):
        a, b = tap // 3, tap % 3
        rows = pad_ref[crop, 2 - b, side * (2 - a) : side * (2 - a) + pixels, :]
        part = mm(rows, w_ref[tap], NT)
        total = part if total is None else total + part
    return total


def act_back(read, dact_ref, stats_ref, norm_ref, stage, crops, pixels, channels, grads_ref, store):
    per_group = channels // GROUPS
    count = float(pixels * per_group)
    for k in chunks(channels):
        gain_row = norm_ref[2 * stage : 2 * stage + 1, k]
        bias_row = norm_ref[2 * stage + 1 : 2 * stage + 2, k]
        grad_gain = jnp.zeros((1, 128), F32)
        grad_bias = jnp.zeros((1, 128), F32)
        for c in range(crops):
            inverse = stats_ref[c, 2 * stage + 1 : 2 * stage + 2, k]
            normed = (read(c, k) - stats_ref[c, 2 * stage : 2 * stage + 1, k]) * inverse
            dout = dact_ref[c, :, k] * slope(normed * gain_row + bias_row)
            grad_gain = grad_gain + col_sum(dout * normed)
            grad_bias = grad_bias + col_sum(dout)
            store(c, k, norm_back(dout, normed, inverse, gain_row, per_group, count))
        grads_ref[0:1, k] = grad_gain
        grads_ref[1:2, k] = grad_bias


def second_kernel(
    side,
    dlat_ref,
    pj_ref,
    stats_ref,
    norm_ref,
    dn_hbm,
    conv_hbm,
    w_hbm,
    low_ref,
    dn_ref,
    conv_ref,
    w_ref,
    pad_ref,
    dact_ref,
    ngrad_ref,
    sem,
):
    crops, pixels, channels = conv_ref.shape
    lat = pixels // 4
    tokens, width = dlat_ref.shape
    pairs = ((dn_hbm, dn_ref), (w_hbm.at[1], w_ref), (conv_hbm, conv_ref))
    copies = [pltpu.make_async_copy(*pair, sem.at[k]) for k, pair in enumerate(pairs)]
    for copy in copies:
        copy.start()
    zero_borders(pad_ref, side)
    dlat = dlat_ref[...]
    dred = mm(dlat, pj_ref[...], NT).astype(BF)
    base = 2 * crops * pixels
    low_ref[base : base + tokens, :] = dred
    low_ref[base + tokens : base + 2 * tokens, 0:width] = dlat
    low_ref[base + tokens : base + 2 * tokens, width:] = jnp.zeros((tokens, channels - width), BF)
    order = pixel_order(pixels, side)
    copies[0].wait()
    pieces = [mm(dred, dn_ref[tap], NT).astype(BF) for tap in range(4)]
    for c in range(crops):
        mixed = jnp.concatenate([p[c * lat : (c + 1) * lat] for p in pieces], axis=0)
        low_ref[c * pixels : (c + 1) * pixels, :] = mm(order, mixed, TN).astype(BF)
        for k in chunks(channels):
            rows = low_ref[c * pixels : (c + 1) * pixels, k].astype(F32)
            put_shifted(pad_ref, c, k, rows, side)
    for copy in copies[1:]:
        copy.wait()
    for c in range(crops):
        dact_ref[c] = conv_back_image(pad_ref, c, w_ref, side, pixels)

    def read(c, k):
        return conv_ref[c, :, k]

    def store(c, k, value):
        at = (crops + c) * pixels
        low_ref[at : at + pixels, k] = value.astype(BF)

    act_back(read, dact_ref, stats_ref, norm_ref, 1, crops, pixels, channels, ngrad_ref, store)
    ngrad_ref[2:8, :] = jnp.zeros((6, channels), F32)
    lines = jnp.concatenate([ngrad_ref[...], jnp.zeros((8, channels), F32)], axis=0)
    low_ref[base + 2 * tokens : base + 2 * tokens + 16, :] = lines.astype(BF)


def second_call(dlat, pj, stats, norm, dn, conv, w, side):
    crops, pixels, channels = conv.shape
    tokens = dlat.shape[0]
    return pl.pallas_call(
        functools.partial(second_kernel, side),
        out_shape=jax.ShapeDtypeStruct((2 * crops * pixels + 2 * tokens + 16, channels), BF),
        in_specs=[vmem()] * 4 + [hbm()] * 3,
        out_specs=vmem(),
        scratch_shapes=[
            pltpu.VMEM(dn.shape, BF),
            pltpu.VMEM(conv.shape, F32),
            pltpu.VMEM(w.shape[1:], BF),
            pltpu.VMEM((crops, 3, pixels + 2 * side, channels), BF),
            pltpu.VMEM(conv.shape, F32),
            pltpu.VMEM((8, channels), F32),
            pltpu.SemaphoreType.DMA((3,)),
        ],
        compiler_params=pltpu.CompilerParams(vmem_limit_bytes=LIMIT),
        cost_estimate=SMALL_COST,
        name="second_backward",
    )(dlat, pj, stats, norm, dn, conv, w)


def first_kernel(
    side, n_part, place_ref, x_ref, stats_ref, norm_ref, low_ref, w_hbm, image_out, ngrad_ref, *scratch
):
    w_ref, pad_ref, dact_ref, image_ref, sem = scratch
    crops, pixels, channels = x_ref.shape
    copy = pltpu.make_async_copy(w_hbm.at[0], w_ref, sem.at[0])
    copy.start()
    zero_borders(pad_ref, side)

    def read(c, k):
        return x_ref[c, :, k].astype(F32)

    def store(c, k, value):
        rows = low_ref[c * pixels : (c + 1) * pixels, k].astype(F32)
        image_ref[c, :, k] = (value + rows).astype(BF)

    for c in range(crops):
        at = (crops + c) * pixels
        for k in chunks(channels):
            put_shifted(pad_ref, c, k, low_ref[at : at + pixels, k].astype(F32), side)
    copy.wait()
    for c in range(crops):
        dact_ref[c] = conv_back_image(pad_ref, c, w_ref, side, pixels)
    act_back(read, dact_ref, stats_ref, norm_ref, 0, crops, pixels, channels, ngrad_ref, store)
    ngrad_ref[2:8, :] = jnp.zeros((6, channels), F32)
    if n_part == 1:
        image_out[...] = image_ref[...]
        return
    span = pixels // n_part
    row = 0
    for k in range(n_part):
        at = pl.multiple_of((place_ref[0] ^ k) * span, span)
        for c in range(crops):
            for lanes in chunks(channels):
                image_out[row : row + span, :] = image_ref[c, pl.ds(at, span), lanes]
                row += span


def first_call(place, x, stats, norm, low, w, side, n_part):
    crops, pixels, channels = x.shape
    shape = (crops, pixels, channels) if n_part == 1 else (x.size // 128, 128)
    return pl.pallas_call(
        functools.partial(first_kernel, side, n_part),
        out_shape=[
            jax.ShapeDtypeStruct(shape, BF),
            jax.ShapeDtypeStruct((8, channels), F32),
        ],
        in_specs=[smem()] + [vmem()] * 4 + [hbm()],
        out_specs=[vmem()] * 2,
        scratch_shapes=[
            pltpu.VMEM(w.shape[1:], BF),
            pltpu.VMEM((crops, 3, pixels + 2 * side, channels), BF),
            pltpu.VMEM(x.shape, F32),
            pltpu.VMEM(x.shape, BF),
            pltpu.SemaphoreType.DMA((1,)),
        ],
        compiler_params=pltpu.CompilerParams(vmem_limit_bytes=LIMIT),
        cost_estimate=SMALL_COST,
        name="first_backward",
    )(place, x, stats, norm, low, w)


class Image:
    def __init__(self, array, count):
        self.rows = array.shape[0] // count
        self.chunks = {(0, k): (array, k * self.rows) for k in range(count)}
        self.order = list(IMAGE_PLAN)

    def leaving(self):
        bit = LINKS[self.order[0]][1]
        return sorted(key for key in self.chunks if key[1] & bit)

    def arrive(self, array, base):
        bit = LINKS[self.order[0]][1]
        for k, key in enumerate(self.leaving()):
            del self.chunks[key]
            self.chunks[key[0] ^ bit, key[1] & ~bit] = (array, base + k * self.rows)
        self.order.pop(0)


def image_kernel(rows, jobs, n_in, place_ref, *refs):
    ins, (out_ref, chunk_ref, sem) = refs[:n_in], refs[n_in:]
    loads = [
        pltpu.make_async_copy(ins[k].at[pl.ds(row, rows), :], chunk_ref.at[source], sem.at[source])
        for source, k, row in jobs
    ]
    for load in loads:
        load.start()
    for load in loads:
        load.wait()
    span, channels = out_ref.shape[1:]
    crops = out_ref.shape[0] // len(jobs)
    for source in range(len(jobs)):
        row = 0
        for c in range(crops):
            for lanes in chunks(channels):
                value = chunk_ref[source, row : row + span, :].astype(F32)
                out_ref[(place_ref[0] ^ source) * crops + c, :, lanes] = value
                row += span


def image_call(place, image, shape):
    arrays, jobs = [], []
    for (source, _), (array, row) in sorted(image.chunks.items(), key=lambda item: item[0]):
        jobs.append((source, operand_index(arrays, array), row))
    return pl.pallas_call(
        functools.partial(image_kernel, image.rows, jobs, len(arrays)),
        out_shape=jax.ShapeDtypeStruct(shape, F32),
        in_specs=[smem()] + [anywhere()] * len(arrays),
        out_specs=vmem(),
        scratch_shapes=[
            pltpu.VMEM((len(jobs), image.rows, 128), BF),
            pltpu.SemaphoreType.DMA((len(jobs),)),
        ],
        compiler_params=pltpu.CompilerParams(vmem_limit_bytes=LIMIT),
        cost_estimate=SMALL_COST,
        name="image_assembly",
    )(place, *arrays)


BLOCK = 64
TAIL = 48


def matrix_kernel(side, crops, pixels, width, plan, n_set, place_ref, *refs):
    sources, refs = refs[: 3 * n_set], refs[3 * n_set :]
    n_out = 2 * len(plan) if plan else 1
    targets, refs = refs[:n_out], refs[n_out:]
    saves, refs = refs[:n_set], refs[n_set:]
    lows, refs = refs[:n_set], refs[n_set:]
    norms, refs = refs[:n_set], refs[n_set:]
    outs, (pad_ref, in_sem, out_sem) = refs[:n_out], refs[n_out:]
    channels = pad_ref.shape[3]
    locals_ = list(saves) + list(lows) + list(norms)
    image = crops * pixels
    loads = []
    for save_at, low_at in ((image, 0), (2 * image, 2 * image), (0, image)):
        group = []
        for k in range(2 * n_set):
            at = save_at if k < n_set else low_at
            count = image if at < 2 * image else sources[k].shape[0] - 2 * image
            rows = pl.ds(at, count)
            group.append(
                pltpu.make_async_copy(
                    sources[k].at[rows, :], locals_[k].at[rows, :], in_sem.at[len(loads), k]
                )
            )
        loads.append(group)
    for k in range(2 * n_set, 3 * n_set):
        loads[1].append(pltpu.make_async_copy(sources[k], locals_[k], in_sem.at[1, k]))
    for group in loads:
        for load in group:
            load.start()
    stores = [
        pltpu.make_async_copy(outs[k], targets[k].at[pl.ds(0, outs[k].shape[0])], out_sem.at[k])
        for k in range(n_out)
    ]
    done = {}
    tokens = crops * pixels // 4
    odd = place_ref[1] % 2 == 1
    line = place_ref[1] // 2 % 2
    dp = place_ref[0]
    zero_borders(pad_ref, side)

    def arrive(group):
        for load in loads[group]:
            load.wait()

    def half(values):
        if not plan:
            return values
        parts = []
        for k in range(0, values.shape[1], 256):
            parts.append(jnp.where(odd, values[:, k + 128 : k + 256], values[:, k : k + 128]))
        return jnp.concatenate(parts, axis=1)

    def low_rows(at, count):
        return jnp.concatenate([half(low[at : at + count, :]) for low in lows], axis=0)

    def squeeze(index, bit):
        return (index >> (bit + 1) << bit) | (index & ((1 << bit) - 1))

    def place_rows(part, row, count, value):
        keep_ref, send_ref = outs[2 * part], outs[2 * part + 1]
        rows = keep_ref.shape[1]
        name = plan[part][1].split()[0]

        def put(lead, keep, send):
            keep_ref[lead, row : row + count, :] = keep
            send_ref[pl.ds(pl.multiple_of(lead * rows + row, 16), count), :] = send

        if name == "x":
            far = line == 1
            keep = jnp.where(far, value[:, 128:], value[:, :128])
            send = jnp.where(far, value[:, :128], value[:, 128:])
            for i in range(8):
                at = slice(i * count, (i + 1) * count)
                put(i ^ dp, keep[at], send[at])
            return
        bit = {"y": 0, "z1": 1, "z2": 2}[name]
        other = (dp >> bit) & 1 == 1
        for pair in range(2):
            lead = (pair ^ line) * 4
            for i in range(8):
                if i >> bit & 1:
                    continue
                j = i | 1 << bit
                lanes = slice(pair * 128, pair * 128 + 128)
                first = value[i * count : (i + 1) * count, lanes]
                second = value[j * count : (j + 1) * count, lanes]
                put(
                    lead + (squeeze(i, bit) ^ squeeze(dp, bit)),
                    jnp.where(other, second, first),
                    jnp.where(other, first, second),
                )

    def store(block, value):
        value = value.astype(BF)
        if not plan:
            outs[0][block * channels : (block + 1) * channels, 0 : value.shape[1]] = value
            return
        part = 0
        while block >= plan[part][0] // 4:
            block -= plan[part][0] // 4
            part += 1
        place_rows(part, block * BLOCK, BLOCK, value)
        done[part] = done.get(part, 0) + 4
        if done[part] == plan[part][0]:
            stores[2 * part].start()
            stores[2 * part + 1].start()

    def taps(save_at, low_at, first_block):
        for n, save in enumerate(saves):
            for c in range(crops):
                for k in chunks(channels):
                    rows = save[save_at + c * pixels : save_at + (c + 1) * pixels, k]
                    put_shifted(pad_ref, n * crops + c, k, rows.astype(F32), side)
        grad = low_rows(low_at, crops * pixels)
        for tap in range(9):
            a, b = tap // 3, tap % 3
            rows = [
                pad_ref[c, b, side * a : side * a + pixels, :] for c in range(n_set * crops)
            ]
            store(first_block + tap, mm(jnp.concatenate(rows, axis=0), grad, TN))

    arrive(0)
    taps(crops * pixels, 0, 0)
    arrive(1)
    base = 2 * crops * pixels
    dred = low_rows(base, tokens)
    for tap in range(4):
        at = base + tap * tokens
        rows = jnp.concatenate([save[at : at + tokens, :] for save in saves], axis=0)
        store(9 + tap, mm(rows, dred, TN))
    arrive(2)
    taps(0, crops * pixels, 13)
    at = base + 4 * tokens
    rows = jnp.concatenate([save[at : at + tokens, :] for save in saves], axis=0)
    dlat = [low[base + tokens : base + 2 * tokens, 0:width] for low in lows]
    if not plan:
        store(22, mm(rows, dlat[0], TN))
        stores[0].start()
        stores[0].wait()
        return
    narrow = []
    for part in dlat:
        pieces = [part[:, k : k + 64] for k in range(0, width, 64)]
        narrow.append(
            jnp.concatenate(
                [
                    jnp.where(odd, pieces[1], pieces[0]),
                    jnp.where(odd, pieces[3], pieces[2]),
                ],
                axis=1,
            )
        )
    proj = mm(rows, jnp.concatenate(narrow, axis=0), TN).astype(BF)
    lines = []
    first = norms[0][0:2, :] + norms[1][0:2, :]
    at = base + 2 * tokens
    second = lows[0][at : at + 16, :].astype(F32) + lows[1][at : at + 16, :].astype(F32)
    for rows in (first, second[0:2]):
        for k in range(2):
            lines += [rows[k : k + 1, lanes] for lanes in chunks(channels)]
    lines = jnp.concatenate(lines, axis=0).astype(BF)
    folded = []
    for i in range(8):
        top = proj[i * 64 : i * 64 + 32]
        low = proj[i * 64 + 32 : (i + 1) * 64]
        block = jnp.concatenate([top[:, 0:64], low[:, 0:64], top[:, 64:], low[:, 64:]], axis=1)
        folded.append(
            jnp.concatenate([block, jnp.concatenate([lines, lines], axis=1)], axis=0)
        )
    last = len(plan) - 1
    place_rows(last, outs[2 * last].shape[1] - TAIL, TAIL, jnp.concatenate(folded, axis=0))
    stores[2 * last].start()
    stores[2 * last + 1].start()
    for store_ in stores:
        store_.wait()


def matrix_call(place, saves, lows, norms, side, crops, pixels, width, plan, room=None):
    channels = saves[0].shape[1]
    n_set = len(saves)
    if plan:
        outs, shapes = [], []
        for units, order in plan:
            rows = 8 * 16 * units
            shapes += [(8, 16 * units, 128), (rows, 128)]
            outs.append(jax.ShapeDtypeStruct(shapes[-2], BF))
            outs.append(jax.ShapeDtypeStruct((rows + room.get(order.split()[0], 0), 128), BF))
    else:
        outs = [jax.ShapeDtypeStruct((23 * channels, channels), BF)]
        shapes = [outs[0].shape]
    return pl.pallas_call(
        functools.partial(matrix_kernel, side, crops, pixels, width, plan, n_set),
        out_shape=outs,
        in_specs=[smem()] + [hbm()] * (3 * n_set),
        out_specs=[hbm()] * len(outs),
        scratch_shapes=[pltpu.VMEM(a.shape, a.dtype) for a in (*saves, *lows, *norms)]
        + [pltpu.VMEM(shape, BF) for shape in shapes]
        + [
            pltpu.VMEM((n_set * crops, 3, pixels + 2 * side, channels), BF),
            pltpu.SemaphoreType.DMA((3, 3 * n_set)),
            pltpu.SemaphoreType.DMA((len(outs),)),
        ],
        compiler_params=pltpu.CompilerParams(vmem_limit_bytes=LIMIT),
        cost_estimate=SMALL_COST,
        name="matrix_backward",
    )(place, *saves, *lows, *norms)


def swap(array, axis, bit):
    count = lax.axis_size(axis)
    return lax.ppermute(array, axis, [(i, i ^ bit) for i in range(count)])


def add_low(first, second):
    return (first.astype(F32) + second.astype(F32)).astype(BF)


LINKS = {"x": ("code", 2), "y": ("dp", 1), "z1": ("dp", 2), "z2": ("dp", 4)}
BITS = ("x", "z2", "z1", "y")
CODE_PLAN = ((36, "z1 y x z2"), (36, "y x z2 z1"))
MATRIX_PLAN = ((28, "x z1 y z2"), (28, "y x z2 z1"), (35, "z1 y x z2"))
IMAGE_PLAN = ("z2", "y", "z1")


class Part:
    def __init__(self, array, low, rows, order, arrival):
        self.array, self.low, self.rows = array, low, rows
        self.order, self.dims = order.split(), list(BITS)
        self.arrival, self.offset = arrival, None


def split_parts(keep, arrival, plan):
    shape = (keep.shape[0] * keep.shape[1],) + keep.shape[2:]
    keep, arrival = keep.reshape(shape), arrival.reshape(shape)
    assert 16 * sum(units for units, _ in plan) == shape[1]
    parts, low = [], 0
    for units, order in plan:
        parts.append(Part(keep, low, 16 * units, order, arrival))
        low += 16 * units
    return parts


def merge_kernel(jobs, moves, n_in, n_out, *refs):
    ins, outs, scratch = refs[:n_in], refs[n_in : n_in + n_out], refs[n_in + n_out :]
    sem = scratch[-1]
    loads, stores = [], []
    passing = []
    for k, (source, row, target, place, rows) in enumerate(moves):
        held = scratch[-2].at[k]
        at = 4 * len(jobs) + 2 * k
        load = pltpu.make_async_copy(ins[source].at[pl.ds(row, rows), :], held, sem.at[at])
        store = pltpu.make_async_copy(held, outs[target].at[pl.ds(place, rows), :], sem.at[at + 1])
        load.start()
        passing.append((load, store))
    for j, job in enumerate(jobs):
        mine, other = scratch[4 * j], scratch[4 * j + 1]
        source = ins[job["array"]].at[:, pl.ds(job["low"], job["rows"]), :]
        first = pltpu.make_async_copy(source, mine, sem.at[4 * j])
        if job["flat"] is None:
            source = ins[job["arrival"]].at[:, pl.ds(job["low"], job["rows"]), :]
        else:
            source = ins[job["arrival"]].at[pl.ds(job["flat"], other.shape[0]), :]
        second = pltpu.make_async_copy(source, other, sem.at[4 * j + 1])
        first.start()
        second.start()
        loads.append((first, second))
    for load, store in passing:
        load.wait()
        store.start()
        stores.append(store)
    for j, job in enumerate(jobs):
        mine, other, keep, send = scratch[4 * j : 4 * j + 4]
        for load in loads[j]:
            load.wait()
        rows, count = job["rows"], [0, 0]
        for lead in range(mine.shape[0]):
            at = slice(lead * rows, (lead + 1) * rows)
            value = add_low(mine[lead], other[lead] if job["flat"] is None else other[at, :])
            half = lead >> job["bit"] & 1
            if half == 0:
                keep[count[0]] = value
            else:
                send[count[1] * rows : (count[1] + 1) * rows, :] = value
            count[half] += 1
        target = outs[job["send"]].at[pl.ds(job["place"], send.shape[0]), :]
        for k, pair in enumerate(((keep, outs[job["keep"]]), (send, target))):
            copy = pltpu.make_async_copy(*pair, sem.at[4 * j + 2 + k])
            copy.start()
            stores.append(copy)
    for copy in stores:
        copy.wait()


def operand_index(arrays, array):
    for k, known in enumerate(arrays):
        if known is array:
            return k
    arrays.append(array)
    return len(arrays) - 1


def merge(parts, given=(), image=None):
    sizes, groups = {}, {}
    arrays, jobs, scratch = [], [], []
    for name, _, group in given:
        groups[name] = list(group)
        sizes[name] = sum(p.rows * 2 ** (len(p.dims) - 1) for p in group)
    links = {p.order[0] for p in parts}
    if image is not None:
        links.add(image.order[0])
    names = sorted(links)
    for k, part in enumerate(parts):
        lead = 2 ** len(part.dims)
        name = part.order[0]
        jobs.append(
            {
                "array": operand_index(arrays, part.array),
                "arrival": operand_index(arrays, part.arrival),
                "low": part.low,
                "rows": part.rows,
                "flat": part.offset,
                "keep": k,
                "bit": len(part.dims) - 1 - part.dims.index(name),
                "send": len(parts) + names.index(name),
                "place": sizes.get(name, 0),
            }
        )
        part.offset = sizes.get(name, 0)
        sizes[name] = part.offset + part.rows * lead // 2
        groups.setdefault(name, []).append(part)
        flat = jobs[-1]["flat"] is not None
        scratch += [
            pltpu.VMEM((lead, part.rows, 128), BF),
            pltpu.VMEM((lead * part.rows, 128) if flat else (lead, part.rows, 128), BF),
            pltpu.VMEM((lead // 2, part.rows, 128), BF),
            pltpu.VMEM((lead // 2 * part.rows, 128), BF),
        ]
    moves = []
    if image is not None:
        name = image.order[0]
        image.base = sizes.get(name, 0)
        for key in image.leaving():
            array, row = image.chunks[key]
            at = sizes.get(name, 0)
            moves.append(
                (operand_index(arrays, array), row, len(parts) + names.index(name), at, image.rows)
            )
            sizes[name] = at + image.rows
        groups.setdefault(name, []).append(image)
    outs = [jax.ShapeDtypeStruct((2 ** (len(p.dims) - 1), p.rows, 128), BF) for p in parts]
    outs += [jax.ShapeDtypeStruct((sizes[name], 128), BF) for name in names]
    aliases = {}
    for name, array, _ in given:
        if name in names:
            assert array.shape == (sizes[name], 128)
            aliases[len(arrays)] = len(parts) + names.index(name)
            arrays.append(array)
    result = pl.pallas_call(
        functools.partial(merge_kernel, jobs, moves, len(arrays), len(outs)),
        out_shape=outs,
        input_output_aliases=aliases,
        in_specs=[anywhere()] * len(arrays),
        out_specs=[anywhere()] * len(outs),
        scratch_shapes=scratch
        + [
            pltpu.VMEM((max(len(moves), 1), image.rows if image is not None else 16, 128), BF),
            pltpu.SemaphoreType.DMA((4 * len(parts) + 2 * len(moves),)),
        ],
        compiler_params=pltpu.CompilerParams(vmem_limit_bytes=LIMIT),
        cost_estimate=SMALL_COST,
        name="merge_parts",
    )(*arrays)
    for k, part in enumerate(parts):
        part.array, part.low, part.arrival = result[k], 0, None
    sends = [(name, result[len(parts) + k], groups[name]) for k, name in enumerate(names)]
    return sends + [entry for entry in given if entry[0] not in names]


def fly(sends):
    return [(name, swap(array, *LINKS[name]), group) for name, array, group in sends]


def land(flights, *others):
    tied = lax.optimization_barrier(tuple(array for _, array, _ in flights) + tuple(others))
    for (name, _, group), array in zip(flights, tied):
        for part in group:
            if isinstance(part, Image):
                part.arrive(array, part.base)
                continue
            part.order.pop(0)
            part.dims.remove(name)
            part.arrival = array
    return tied[len(flights) :]


def final_kernel(
    n_code, parts, n_in, rates, code_rate, mean_count, *refs
):
    n_all = n_in + 18
    sources, targets, refs = refs[:n_all], refs[n_all : n_all + 16], refs[n_all + 16 :]
    locals_, outs, refs = refs[:n_all], refs[n_all : n_all + 16], refs[n_all + 16 :]
    code_ref, mat_ref, in_sem, out_sem = refs
    loads = [pltpu.make_async_copy(sources[k], locals_[k], in_sem.at[k]) for k in range(n_all)]
    for load in loads:
        load.start()
    stores = [pltpu.make_async_copy(outs[k], targets[k], out_sem.at[k]) for k in range(16)]
    ins = locals_[:n_in]
    (
        conv_m, conv_v, conv_a, down_m, down_v, down_a, proj_m, proj_v, proj_a,
        norm_m, norm_v, norm_a, code_m, code_v, code_a, own_ref, select_ref, chosen_ref,
    ) = locals_[n_in:]
    for load in loads[:n_in]:
        load.wait()
    at = [0, 0]
    for k, part in enumerate(parts):
        which = 0 if k < n_code else 1
        target = (code_ref, mat_ref)[which]
        rows = part["rows"]
        value = ins[part["array"]][0].astype(F32)
        value = value + ins[part["arrival"]][part["offset"] : part["offset"] + rows, :].astype(F32)
        target[at[which] : at[which] + rows, :] = value
        at[which] += rows

    def step(refs, index, grad, rate, results):
        master, moment, average = refs
        moment_new = MOMENTUM * moment[index] + grad
        master_new = master[index] - rate * (grad + MOMENTUM * moment_new)
        results[0][index] = moment_new
        results[1][index] = master_new
        results[2][index] = AVERAGE_DECAY * average[index] + (1.0 - AVERAGE_DECAY) * master_new

    for load in loads[n_in : n_in + 12]:
        load.wait()
    weight_rate, norm_rate = rates
    block = conv_m.shape[0] // 18
    for conv in range(2):
        for tap in range(9):
            row = (13 + tap if conv == 0 else tap) * block
            index = (pl.ds(tap * 2 + conv, block, stride=18), slice(None))
            grad = mat_ref[row : row + block, :]
            step((conv_m, conv_v, conv_a), index, grad, weight_rate, outs[0:3])
    for tap in range(4):
        index = (pl.ds(tap, block, stride=4), slice(None))
        grad = mat_ref[(9 + tap) * block : (10 + tap) * block, :]
        step((down_m, down_v, down_a), index, grad, weight_rate, outs[3:6])
    tail = 22 * block
    for k in range(2):
        index = (slice(k * block // 2, (k + 1) * block // 2), slice(None))
        grad = mat_ref[tail : tail + block // 2, k * 64 : (k + 1) * 64]
        step((proj_m, proj_v, proj_a), index, grad, weight_rate, outs[6:9])
    tail += block // 2
    lines = norm_m.shape[1] // 128
    for k in range(4):
        for j in range(lines):
            index = (slice(k, k + 1), slice(j * 128, (j + 1) * 128))
            row = tail + k * lines + j
            step((norm_m, norm_v, norm_a), index, mat_ref[row : row + 1, :], norm_rate, outs[9:12])

    for store in stores[:12]:
        store.start()
    for load in loads[n_in + 12 :]:
        load.wait()
    cols, codes = code_m.shape
    tiles = codes // 128
    base = tiles * cols
    spans = select_ref.shape[0] // 128
    source = jnp.concatenate(
        [code_ref[base + k * cols : base + (k + 1) * cols, :] for k in range(spans)], axis=1
    ).astype(BF)
    base += spans * cols
    counts = code_ref[base : base + tiles, :]
    outs[15][...] = counts * (1.0 / mean_count)
    wide = 512
    for k in range(codes // wide):
        lanes = slice(k * wide, (k + 1) * wide)
        four = range(k * wide // 128, (k + 1) * wide // 128)
        grad = jnp.concatenate([code_ref[t * cols : (t + 1) * cols, :] for t in four], axis=1)
        slope_sum = jnp.concatenate(
            [code_ref[base + tiles + t : base + tiles + t + 1, :] for t in four], axis=1
        )
        count = jnp.concatenate([code_ref[base + t : base + t + 1, :] for t in four], axis=1)
        grad = grad - own_ref[:, lanes].astype(F32) * slope_sum
        moment_new = MOMENTUM * code_v[:, lanes] + grad
        stepped = code_m[:, lanes] - code_rate * (grad + MOMENTUM * moment_new)
        renewed = mm(source, select_ref[:, lanes])
        share = chosen_ref[:, lanes] * (mean_count / (mean_count + count))
        master_new = stepped + share * (renewed - stepped)
        outs[12][:, lanes] = moment_new
        outs[13][:, lanes] = master_new
        outs[14][:, lanes] = (
            AVERAGE_DECAY * code_a[:, lanes] + (1.0 - AVERAGE_DECAY) * master_new
        )
    for store in stores[12:]:
        store.start()
    for store in stores:
        store.wait()


def final_call(codes, mats, states, own, select, chosen, rates, code_rate, mean_count):
    arrays, parts = [], []
    for part in codes + mats:
        parts.append(
            {
                "array": operand_index(arrays, part.array),
                "arrival": operand_index(arrays, part.arrival),
                "offset": part.offset,
                "rows": part.rows,
            }
        )
    shapes = [states[k].shape for k in (0, 0, 0, 3, 3, 3, 6, 6, 6, 9, 9, 9, 12, 12, 12)]
    outs = [jax.ShapeDtypeStruct(shape, F32) for shape in shapes]
    outs.append(jax.ShapeDtypeStruct((own.shape[1] // 128, 128), F32))
    args = arrays + list(states) + [own, select, chosen]
    return pl.pallas_call(
        functools.partial(
            final_kernel, len(codes), parts, len(arrays), rates, code_rate, mean_count
        ),
        out_shape=outs,
        in_specs=[hbm()] * len(args),
        out_specs=[hbm()] * len(outs),
        scratch_shapes=[pltpu.VMEM(a.shape, a.dtype) for a in args]
        + [pltpu.VMEM(out.shape, F32) for out in outs]
        + [
            pltpu.VMEM((sum(p.rows for p in codes), 128), F32),
            pltpu.VMEM((sum(p.rows for p in mats), 128), F32),
            pltpu.SemaphoreType.DMA((len(args),)),
            pltpu.SemaphoreType.DMA((16,)),
        ],
        compiler_params=pltpu.CompilerParams(vmem_limit_bytes=LIMIT),
        cost_estimate=SMALL_COST,
        name="updates",
    )(*args)


def nesterov_step(master, moment, average, grad, rate):
    moment_new = MOMENTUM * moment + grad
    master_new = master - rate * (grad + MOMENTUM * moment_new)
    return (moment_new, master_new, AVERAGE_DECAY * average + (1.0 - AVERAGE_DECAY) * master_new)


def body(
    crops_in,
    crop_weight,
    cotangent,
    conv_copy,
    down_copy,
    proj_copy,
    norm_copy,
    codebook,
    conv_master,
    conv_moment,
    conv_average,
    down_master,
    down_moment,
    down_average,
    proj_master,
    proj_moment,
    proj_average,
    norm_master,
    norm_moment,
    norm_average,
    code_master,
    code_moment,
    code_average,
    repl_code,
    repl_src,
):
    dp_count = lax.axis_size("dp")
    code_count = lax.axis_size("code")
    dp_at = lax.axis_index("dp")
    code_at = lax.axis_index("code")
    halves = dp_count == 8 and code_count == 4
    place = jnp.stack([dp_at, code_at]).astype(jnp.int32)

    local = lax.all_to_all(crops_in, "dp", split_axis=1, concat_axis=2, tiled=True)[0]
    crop_dev, pixels, channels = local.shape
    side = math.isqrt(pixels)
    lat = pixels // 4
    tokens = crop_dev * lat
    width = proj_copy.shape[1]
    code_dev = codebook.shape[0]
    codes_all = code_dev * code_count

    crops_set = crop_dev * dp_count
    flat_src = repl_src.reshape(-1)
    crop_id = flat_src // lat % crops_set
    owner = (crop_id // crop_dev == dp_at) & (flat_src // (crops_set * lat) == code_at)
    row_id = crop_id % crop_dev * lat + flat_src % lat
    depth_id = jnp.repeat(jnp.arange(DEPTH, dtype=jnp.int32), repl_src.shape[1])
    pick = (
        jnp.where(owner, depth_id * tokens + row_id, -1)[None, :]
        == jnp.arange(DEPTH * tokens, dtype=jnp.int32)[:, None]
    ).astype(BF)
    weight_col = crop_weight.astype(F32).reshape(crop_dev)
    dn = down_copy.transpose(1, 0, 2)
    gains = norm_copy.T.astype(F32)
    if halves:
        quarter = code_dev // 4
        corner = (dp_at & 1) * 2 + ((dp_at >> 1) & 1)
        mine = lax.dynamic_slice_in_dim(codebook, corner * quarter, quarter, 0)
        over_x = swap(mine, "code", 2)
        over_x, conv_copy = lax.optimization_barrier((over_x, conv_copy))
        over_y, over_z = swap(over_x, "dp", 1), swap(over_x, "dp", 2)
        core = swap(codebook, "code", 1)
        diag = [swap(over_x, "code", 1)]
        w = conv_copy.transpose(1, 2, 0, 3)
        over_y, over_z, local, w, dn, gains, core, diag[0], pick, weight_col, place = (
            lax.optimization_barrier(
                (over_y, over_z, local, w, dn, gains, core, diag[0], pick, weight_col, place)
            )
        )
        last = [swap(over_z[: quarter // 2], "dp", 1), swap(over_y[quarter // 2 :], "dp", 2)]
        diag = diag + [swap(piece, "code", 1) for piece in (over_y, over_z)]
    else:
        w = conv_copy.transpose(1, 2, 0, 3)
        every = lax.all_gather(codebook, "code", axis=0)
        pieces = [every[k] for k in range(code_count)]

    conv1, stats, save, latent = forward_call(local, gains, w, dn, proj_copy, side)
    if halves:
        last[0], last[1], latent = lax.optimization_barrier((last[0], last[1], latent))
        diag = diag + [swap(piece, "code", 1) for piece in last]
        pieces = [codebook, core, over_x, over_y, over_z] + last + diag
        saves = (save, swap(save, "code", 1))

    n_row = dp_count if halves else 1
    quantized, dlat, rows, extra, *code_grads = quant_call(
        place,
        latent,
        weight_col,
        cotangent.reshape(tokens, width),
        pick,
        pieces,
        halves,
        code_count,
        n_row,
    )
    pixels_all = crop_dev * pixels * dp_count * code_count
    weight_rate = WEIGHT_RATE / math.sqrt(pixels_all)
    norm_rate = NORM_RATE / math.sqrt(pixels_all)
    crops_all = crop_dev * dp_count * code_count
    mean_count = DEPTH * lat * crops_all / codes_all
    code_rate = CODE_RATE / math.sqrt(mean_count)
    own_codes = lax.dynamic_slice_in_dim(codebook, dp_at * (width // dp_count), width // dp_count, 1).T
    select = (
        repl_code.reshape(-1)[:, None] - code_at * code_dev
        == jnp.arange(code_dev, dtype=jnp.int32)[None, :]
    )
    chosen = jnp.sum(select.astype(F32), axis=0)
    low = second_call(dlat, proj_copy, stats, gains, dn, conv1, w, side)

    if halves:
        code_core = swap(code_grads[1], "code", 1)
        low_mate = swap(low, "code", 1)
        code_core, low, save_mate = lax.optimization_barrier((code_core, low, saves[1]))
        codes = split_parts(code_grads[0], code_core, CODE_PLAN)
        sends = merge(codes)
        tied = lax.optimization_barrier(tuple(array for _, array, _ in sends) + (low, low_mate))
        low, low_mate = tied[-2:]
        flights = fly([(name, tied[k], group) for k, (name, _, group) in enumerate(sends)])
        image, ngrad = first_call(place, local, stats, gains, low, w, side, dp_count)
        ngrad_mate = swap(ngrad, "code", 1)
        image = Image(image, dp_count)
        room = {}
        for part in codes:
            name = part.order[1]
            room[name] = room.get(name, 0) + part.rows * 2 ** (len(part.dims) - 2)
        results = matrix_call(
            place, (save, save_mate), (low, low_mate), (ngrad, ngrad_mate), side, crop_dev, pixels,
            width, MATRIX_PLAN, room,
        )
        mats, given = [], []
        results = land(flights, *results)
        for k, (units, order) in enumerate(MATRIX_PLAN):
            part = Part(results[2 * k], 0, 16 * units, order, None)
            part.offset = 0
            mats.append(part)
            given.append((part.order[0], results[2 * k + 1], [part]))
        own_codes, select, chosen = land(
            fly(merge(codes, given, image)), own_codes, select.astype(BF), chosen[None, :]
        )
        parts = codes + mats
        for _ in range(3):
            active = [part for part in parts if part.order]
            land(fly(merge(active, image=image if image.order else None)))
        shape = (crop_dev * dp_count, pixels // dp_count, channels)
        input_back = image_call(place, image, shape)[None]

        def flat(array):
            return array.transpose(0, 2, 1, 3).reshape(-1, 128)

        states = [flat(array) for array in (conv_master, conv_moment, conv_average)]
        states += [a.reshape(-1, 128) for a in (down_master, down_moment, down_average)]
        states += [proj_master, proj_moment, proj_average]
        states += [a.T for a in (norm_master, norm_moment, norm_average)]
        states += [a.T for a in (code_master, code_moment, code_average)]
        out = final_call(
            codes, mats, states, own_codes, select, chosen,
            (weight_rate, norm_rate), code_rate, mean_count,
        )
        rows_in = channels // dp_count
        conv_out = [
            a.reshape(rows_in, 9, 2, channels // code_count).transpose(0, 2, 1, 3) for a in out[0:3]
        ]
        return (
            quantized.reshape(1, crop_dev, lat, width),
            input_back,
            *conv_out,
            *[a.reshape(down_master.shape) for a in out[3:6]],
            *out[6:9],
            *[a.T for a in out[9:12]],
            *[a.T for a in out[12:15]],
            out[15].reshape(code_dev),
        )

    image, ngrad = first_call(place, local, stats, gains, low, w, side, 1)
    (grads,) = matrix_call(
        place, (save,), (low,), (ngrad,), side, crop_dev, pixels, width, None
    )
    grads = grads.reshape(23, channels, channels)
    base = 2 * crop_dev * pixels + 2 * tokens
    norm_grad = jnp.concatenate([ngrad[0:2], low[base : base + 2].astype(F32)], axis=0)
    flat = lax.psum_scatter(code_grads[0], "code", scatter_dimension=0, tiled=True)[0]
    code_grad = lax.psum_scatter(flat, "dp", scatter_dimension=0, tiled=True).astype(F32)
    sums = lax.psum_scatter(extra, "code", scatter_dimension=1, tiled=True)
    sums = lax.psum(sums, "dp")
    source = mm(rows.reshape(DEPTH * tokens, width), pick, TN).astype(BF)
    source_rows = lax.psum_scatter(source, "dp", scatter_dimension=0, tiled=True)
    source_rows = lax.psum(source_rows, "code")

    def matrix(array, scatter):
        array = lax.psum_scatter(array, "dp", scatter_dimension=0, tiled=True)
        return lax.psum_scatter(array, "code", scatter_dimension=scatter, tiled=True).astype(F32)

    conv_part = matrix(jnp.stack([grads[13:22], grads[0:9]]).transpose(2, 0, 1, 3), 3)
    down_part = matrix(grads[9:13].transpose(1, 0, 2), 2)
    proj_part = matrix(grads[22, :, :width], 1)
    norm_grad = lax.psum(norm_grad, ("dp", "code"))
    input_back = lax.all_to_all(
        image[None], "dp", split_axis=2, concat_axis=1, tiled=True
    ).astype(F32)
    conv_out = nesterov_step(conv_master, conv_moment, conv_average, conv_part, weight_rate)
    down_out = nesterov_step(down_master, down_moment, down_average, down_part, weight_rate)
    proj_out = nesterov_step(proj_master, proj_moment, proj_average, proj_part, weight_rate)
    norm_out = nesterov_step(norm_master, norm_moment, norm_average, norm_grad.T, norm_rate)

    counts_all, slope_sum = sums[0], sums[1]
    share = mean_count / (mean_count + counts_all)
    code_load = counts_all / mean_count
    code_grad = code_grad - own_codes.astype(F32) * slope_sum[None, :]
    code_moment_new = MOMENTUM * code_moment.T + code_grad
    stepped = code_master.T - code_rate * (code_grad + MOMENTUM * code_moment_new)
    renewed = mm(source_rows, select.astype(BF))
    code_master_new = stepped + (chosen * share)[None, :] * (renewed - stepped)
    code_average_new = AVERAGE_DECAY * code_average.T + (1.0 - AVERAGE_DECAY) * code_master_new
    return (
        quantized.reshape(1, crop_dev, lat, width),
        input_back,
        *conv_out,
        *down_out,
        *proj_out,
        *norm_out,
        code_moment_new.T,
        code_master_new.T,
        code_average_new.T,
        code_load,
    )


def solution(mesh):
    in_specs = (
        P("code", None, "dp", None),
        P("code", "dp"),
        P("code", "dp", None, None),
        P(),
        P(),
        P(),
        P(),
        P("code", None),
        P("dp", None, None, "code"),
        P("dp", None, None, "code"),
        P("dp", None, None, "code"),
        P("dp", None, "code"),
        P("dp", None, "code"),
        P("dp", None, "code"),
        P("dp", "code"),
        P("dp", "code"),
        P("dp", "code"),
        P(),
        P(),
        P(),
        P("code", "dp"),
        P("code", "dp"),
        P("code", "dp"),
        P(),
        P(),
    )
    out_specs = (
        P("code", "dp", None, None),
        P("code", None, "dp", None),
        P("dp", None, None, "code"),
        P("dp", None, None, "code"),
        P("dp", None, None, "code"),
        P("dp", None, "code"),
        P("dp", None, "code"),
        P("dp", None, "code"),
        P("dp", "code"),
        P("dp", "code"),
        P("dp", "code"),
        P(),
        P(),
        P(),
        P("code", "dp"),
        P("code", "dp"),
        P("code", "dp"),
        P("code"),
    )
    return jax.shard_map(body, mesh=mesh, in_specs=in_specs, out_specs=out_specs, check_vma=False)
```

```python
import functools
import math

import jax
import jax.numpy as jnp
from jax import lax
from jax.experimental import pallas as pl
from jax.experimental.pallas import tpu as pltpu
from jax.sharding import PartitionSpec as P

GROUPS = 32
DEPTH = 4
BETA = 0.0625
EPSILON = 1e-05
MOMENTUM = 0.5
AVERAGE_DECAY = 0.5
COMMIT = 0.25
WEIGHT_RATE = 0.05
NORM_RATE = 0.5
CODE_RATE = 0.5

BF = jnp.bfloat16
F32 = jnp.float32
NT = (((1,), (1,)), ((), ()))
NN = (((1,), (0,)), ((), ()))
TN = (((0,), (0,)), ((), ()))
MIB = 1 << 20
LIMIT = 62 * MIB
SMALL_COST = pl.CostEstimate(flops=1 << 20, bytes_accessed=1 << 16, transcendentals=0)


def mm(a, b, dims=NN):
    return lax.dot_general(a, b, dims, preferred_element_type=F32)


def vmem():
    return pl.BlockSpec(memory_space=pltpu.VMEM)


def smem():
    return pl.BlockSpec(memory_space=pltpu.SMEM)


def anywhere():
    return pl.BlockSpec(memory_space=pl.ANY)


def hbm():
    return pl.BlockSpec(memory_space=pltpu.HBM)


def group_sum(rows, per_group):
    lanes = rows.shape[1]
    at = lax.broadcasted_iota(jnp.int32, rows.shape, 1)
    step = 1
    while step < per_group:
        up = pltpu.roll(rows, step, 1)
        down = pltpu.roll(rows, lanes - step, 1)
        rows = rows + jnp.where((at & step) != 0, up, down)
        step *= 2
    return rows


def col_sum(values):
    rows, lanes = values.shape
    return jnp.sum(jnp.sum(values.reshape(rows // 8, 8, lanes), axis=0), axis=0, keepdims=True)


def put_shifted(pad_ref, crop, lanes, values, side):
    pixels = values.shape[0]
    col = lax.broadcasted_iota(jnp.int32, values.shape, 0) % side
    left = jnp.where(col == 0, 0.0, pltpu.roll(values, 1, 0))
    right = jnp.where(col == side - 1, 0.0, pltpu.roll(values, pixels - 1, 0))
    for shift, grid in enumerate((left, values, right)):
        pad_ref[crop, shift, side : side + pixels, lanes] = grid.astype(BF)


def zero_borders(pad_ref, side):
    rows = pad_ref.shape[2]
    edge = jnp.zeros((side, pad_ref.shape[3]), BF)
    for crop in range(pad_ref.shape[0]):
        for shift in range(3):
            pad_ref[crop, shift, 0:side, :] = edge
            pad_ref[crop, shift, rows - side : rows, :] = edge


def pixel_order(pixels, side):
    half = side // 2
    lat = half * half
    row = lax.broadcasted_iota(jnp.int32, (pixels, pixels), 0)
    col = lax.broadcasted_iota(jnp.int32, (pixels, pixels), 1)
    tap, pos = row // lat, row % lat
    at = (2 * (pos // half) + tap // 2) * side + 2 * (pos % half) + tap % 2
    return jnp.where(at == col, 1.0, 0.0).astype(BF)


def chunks(channels):
    return [slice(k, k + 128) for k in range(0, channels, 128)]


def norm_stats(read, crops, pixels, channels, per_group):
    count = float(pixels * per_group)
    result = []
    sums = [
        jnp.concatenate([col_sum(read(c, k)) for k in chunks(channels)], axis=1)
        for c in range(crops)
    ]
    means = [group_sum(s, per_group) * (1.0 / count) for s in sums]
    for c in range(crops):
        parts = []
        for k in chunks(channels):
            d = read(c, k) - means[c][:, k]
            parts.append(col_sum(d * d))
        spread = group_sum(jnp.concatenate(parts, axis=1), per_group) * (1.0 / count)
        result.append((means[c], lax.rsqrt(spread + EPSILON)))
    return result


def conv_apply(pad_ref, crop, w_ref, side, pixels):
    total = None
    for b in range(3):
        rows = jnp.concatenate(
            [pad_ref[crop, b, side * a : side * a + pixels, :] for a in range(3)], axis=1
        )
        part = None
        weight = jnp.concatenate([w_ref[3 * a + b] for a in range(3)], axis=0)
        part = mm(rows, weight)
        total = part if total is None else total + part
    return total


def forward_kernel(
    side,
    x_ref,
    norm_ref,
    w_hbm,
    dn_hbm,
    pj_ref,
    conv_hbm,
    stats_ref,
    save_hbm,
    lat_ref,
    w_ref,
    dn_ref,
    pad_ref,
    sum_ref,
    conv_ref,
    sel_ref,
    sem,
):
    crops, pixels, channels = x_ref.shape
    per_group = channels // GROUPS
    lat = pixels // 4
    tokens = crops * lat
    copies = [pltpu.make_async_copy(w_hbm.at[k], w_ref.at[k], sem.at[k]) for k in range(2)]
    dn_copy = pltpu.make_async_copy(dn_hbm, dn_ref, sem.at[2])
    for copy in copies + [dn_copy]:
        copy.start()
    conv_save = pltpu.make_async_copy(conv_ref, conv_hbm, sem.at[3])
    zero_borders(pad_ref, side)
    for stage in range(2):
        if stage == 0:

            def read(c, k):
                return x_ref[c, :, k].astype(F32)

        else:

            def read(c, k):
                return conv_ref[c, :, k]

        stats = norm_stats(read, crops, pixels, channels, per_group)
        for c in range(crops):
            mean, inverse = stats[c]
            stats_ref[c, 2 * stage : 2 * stage + 1, :] = mean
            stats_ref[c, 2 * stage + 1 : 2 * stage + 2, :] = inverse
            for k in chunks(channels):
                normed = (read(c, k) - mean[:, k]) * inverse[:, k]
                out = normed * norm_ref[2 * stage : 2 * stage + 1, k]
                out = out + norm_ref[2 * stage + 1 : 2 * stage + 2, k]
                put_shifted(pad_ref, c, k, out * jax.nn.sigmoid(out), side)
        acts = [
            pltpu.make_async_copy(
                pad_ref.at[c, 1, pl.ds(side, pixels), :],
                save_hbm.at[pl.ds((stage * crops + c) * pixels, pixels), :],
                sem.at[4 + c],
            )
            for c in range(crops)
        ]
        for act in acts:
            act.start()
        copies[stage].wait()
        for c in range(crops):
            total = conv_apply(pad_ref, c, w_ref.at[stage], side, pixels)
            if stage == 0:
                conv_ref[c] = total
            else:
                sum_ref[c] = (x_ref[c].astype(F32) + total).astype(BF)
        for act in acts:
            act.wait()
        if stage == 0:
            conv_save.start()
    order = pixel_order(pixels, side)
    for c in range(crops):
        picked = mm(order, sum_ref[c]).astype(BF)
        for tap in range(4):
            at = tap * tokens + c * lat
            sel_ref[at : at + lat, :] = picked[tap * lat : (tap + 1) * lat]
    dn_copy.wait()
    reduced = mm(sel_ref[0:tokens], dn_ref[0])
    for tap in range(1, 4):
        reduced = reduced + mm(sel_ref[tap * tokens : (tap + 1) * tokens], dn_ref[tap])
    reduced = reduced.astype(BF)
    sel_ref[4 * tokens : 5 * tokens, :] = reduced
    sel_save = pltpu.make_async_copy(
        sel_ref, save_hbm.at[pl.ds(2 * crops * pixels, 5 * tokens), :], sem.at[4 + crops]
    )
    sel_save.start()
    lat_ref[...] = mm(reduced, pj_ref[...]).astype(BF)
    conv_save.wait()
    sel_save.wait()


def forward_call(x, norm, w, dn, pj, side):
    crops, pixels, channels = x.shape
    tokens = crops * pixels // 4
    return pl.pallas_call(
        functools.partial(forward_kernel, side),
        out_shape=[
            jax.ShapeDtypeStruct((crops, pixels, channels), F32),
            jax.ShapeDtypeStruct((crops, 8, channels), F32),
            jax.ShapeDtypeStruct((2 * crops * pixels + 5 * tokens, channels), BF),
            jax.ShapeDtypeStruct((tokens, pj.shape[1]), BF),
        ],
        in_specs=[vmem(), vmem(), hbm(), hbm(), vmem()],
        out_specs=[hbm(), vmem(), hbm(), vmem()],
        scratch_shapes=[
            pltpu.VMEM(w.shape, BF),
            pltpu.VMEM(dn.shape, BF),
            pltpu.VMEM((crops, 3, pixels + 2 * side, channels), BF),
            pltpu.VMEM((crops, pixels, channels), BF),
            pltpu.VMEM((crops, pixels, channels), F32),
            pltpu.VMEM((5 * tokens, channels), BF),
            pltpu.SemaphoreType.DMA((5 + crops,)),
        ],
        compiler_params=pltpu.CompilerParams(vmem_limit_bytes=LIMIT),
        cost_estimate=SMALL_COST,
        name="residual_forward",
    )(x, norm, w, dn, pj)


TILE = 1024
SUB = 1024
SPAN = 4096


def quant_kernel(n_shard, halves, n_piece, place_ref, lat_ref, weight_ref, cot_ref, pick_ref, *rest):
    shard_hbm = rest[:n_piece]
    n_out = 6 if halves else 5
    q_ref, g_ref, rows_ref, extra_ref = rest[n_piece : n_piece + 4]
    grad_hbm = rest[n_piece + 4 : n_piece + n_out]
    (
        code_ref,
        codet_ref,
        score_ref,
        stack_ref,
        res_ref,
        q_level_ref,
        fac_ref,
        side_ref,
        acc_ref,
        count_ref,
        norms_ref,
        carry_ref,
        stage_ref,
        more_ref,
        in_sem,
        out_sem,
        more_sem,
    ) = rest[n_piece + n_out :]
    tokens, width = lat_ref.shape
    codes = code_ref.shape[0]
    shard = codes // n_shard
    part = codes // 2
    tile = min(TILE, part)

    if halves:
        quarter = shard // 4
        corner = (place_ref[0] & 1) * 2 + ((place_ref[0] >> 1) & 1)
        starts = [0, shard]
        for base in (2 * shard, 3 * shard):
            starts += [base + (corner ^ k) * quarter for k in (0, 2, 1, 3)]
            starts.append(starts[-1] + quarter // 2)
    else:
        starts = [k * shard for k in range(n_shard)]
    copies = [
        pltpu.make_async_copy(
            shard_hbm[k],
            code_ref.at[pl.ds(pl.multiple_of(starts[k], 256), shard_hbm[k].shape[0]), :],
            in_sem.at[k],
        )
        for k in range(n_piece)
    ]
    for copy in copies:
        copy.start()

    def fold(values, combine):
        out = values[:, :128]
        for k in range(128, values.shape[1], 128):
            out = combine(out, values[:, k : k + 128])
        return out

    def level_forward(level, first):
        residual = res_ref[level]
        low = residual.astype(BF)
        rows_ref[level] = low
        scaled = low * jnp.asarray(2.0 * BETA, BF)
        at_row = pl.multiple_of(level * tokens, tokens)
        peaks, sums, picks = [], [], []
        for h in range(2):
            best = jnp.full((tokens, 128), -jnp.inf, F32)
            for k in range(part // tile):
                at = h * part + k * tile
                lanes = slice(at, at + tile)
                if first:
                    if halves:
                        if at % shard == 0:
                            group = at // shard
                            for piece in ([group] if group < 2 else range(5 * group - 8, 5 * group - 3)):
                                copies[piece].wait()
                    else:
                        if at % shard == 0:
                            copies[at // shard].wait()
                    for j in range(at, at + tile, 512):
                        turned = code_ref[j : j + 512, :].T
                        codet_ref[:, j : j + 512] = turned
                        wide = turned.astype(F32)
                        norms_ref[:, j : j + 512] = BETA * col_sum(wide * wide)
                s = mm(scaled, codet_ref[:, lanes]) - norms_ref[:, lanes]
                score_ref[:, k * tile : (k + 1) * tile] = s
                best = jnp.maximum(best, fold(s, jnp.maximum))
            peak = jnp.max(best, axis=1, keepdims=True)
            acc_ref[h] = jnp.zeros((tokens, width), F32)

            def power(i, total):
                for k in range(SPAN // tile):
                    at = pl.multiple_of(i * SPAN + k * tile, tile)
                    lanes = pl.ds(pl.multiple_of(h * part + at, tile), tile)
                    p = jnp.exp(score_ref[:, pl.ds(at, tile)] - peak)
                    low_p = p.astype(BF)
                    stack_ref[pl.ds(at_row, tokens), lanes] = low_p
                    acc_ref[h] += mm(low_p, code_ref[lanes, :])
                    total = total + fold(p, jnp.add)
                return total

            total = lax.fori_loop(0, part // SPAN, power, jnp.zeros((tokens, 128), F32))
            peaks.append(peak)
            sums.append(jnp.sum(total, axis=1, keepdims=True))
        top = jnp.maximum(peaks[0], peaks[1])
        scales = [jnp.exp(peak - top) for peak in peaks]
        inverse = 1.0 / (sums[0] * scales[0] + sums[1] * scales[1])
        factors = [scale * inverse for scale in scales]
        for h in range(2):
            fac_ref[level, h] = jnp.broadcast_to(factors[h], (tokens, 128))
        picked = acc_ref[0] * factors[0] + acc_ref[1] * factors[1]
        q_level_ref[level] = picked
        res_ref[level + 1] = residual - picked

    res_ref[0] = lat_ref[...].astype(F32)
    level_forward(0, True)

    def later(level, nothing):
        level_forward(level, False)
        return nothing

    lax.fori_loop(1, DEPTH, later, 0)
    q_ref[...] = (q_level_ref[0] + q_level_ref[1]) + (q_level_ref[2] + q_level_ref[3])

    n_crop = weight_ref.shape[0]
    weight = jnp.concatenate(
        [jnp.full((tokens // n_crop, 1), weight_ref[c], F32) for c in range(n_crop)], axis=0
    )
    count_ref[...] = jnp.zeros(count_ref.shape, F32)
    carry_ref[...] = 2.0 * COMMIT * weight * res_ref[DEPTH]

    def level_back(step, nothing):
        level = DEPTH - 1 - step
        carry = carry_ref[...]
        grad = cot_ref[...].astype(F32) - carry
        dot = jnp.sum(grad * q_level_ref[level], axis=1, keepdims=True)
        ex_row = pl.multiple_of(level * tokens, tokens)
        in_row = pl.multiple_of((DEPTH + level) * tokens, tokens)
        turned_rows = grad_t(rows_ref[level])
        for h in range(2):
            factor = fac_ref[level, h][:, 0:1]
            down = (grad * factor).astype(BF)
            small = down * jnp.asarray(2.0 * BETA, BF)
            total_grad = dot * factor * (-2.0 * BETA)
            share = weight * factor
            side_ref[h, :, pl.ds(ex_row, tokens)] = grad_t(down)
            side_ref[h, :, pl.ds(in_row, tokens)] = turned_rows
            for k in range(part // tile):
                lanes = slice(h * part + k * tile, h * part + (k + 1) * tile)
                p = stack_ref[pl.ds(ex_row, tokens), lanes].astype(F32)
                ds = (mm(small, codet_ref[:, lanes]) + total_grad) * p
                inner = ds.astype(BF)
                stack_ref[pl.ds(in_row, tokens), lanes] = inner
                value = mm(inner, code_ref[lanes, :])
                if h == 0 and k == 0:
                    acc_ref[0] = value
                else:
                    acc_ref[0] += value
                weighted = (p * share).reshape(tokens // 8, 8, tile)
                count_ref[0, :, lanes] += jnp.sum(weighted, axis=0)
                count_ref[1, :, lanes] += jnp.sum(ds.reshape(tokens // 8, 8, tile), axis=0)
        pull = jnp.where(level > 0, 2.0 * COMMIT, 0.0)
        carry_ref[...] = carry + acc_ref[0] + pull * weight * res_ref[level]
        return nothing

    lax.fori_loop(0, DEPTH, level_back, 0)
    g_ref[...] = carry_ref[...].astype(BF)
    extra_ref[0:1, :] = jnp.sum(count_ref[0], axis=0, keepdims=True)
    extra_ref[1:2, :] = jnp.sum(count_ref[1], axis=0, keepdims=True)

    place = place_ref[0]
    pending = []
    n_row = stage_ref.shape[1] if halves else 1
    block = width // n_row
    if halves:
        flat = jnp.concatenate([rows_ref[level] for level in range(DEPTH)], axis=0)
        source = mm(flat, pick_ref[...], TN).astype(BF)
        spans = source.shape[1] // 128
        for k in range(n_shard):
            lines = []
            for row in range(2):
                for at in range(k * shard, (k + 1) * shard, 128):
                    lines.append(extra_ref[row : row + 1, at : at + 128])
            lines = jnp.concatenate(lines, axis=0).astype(BF)
            for r in range(n_row):
                for span in range(spans):
                    more_ref[k, r ^ place, span * block : (span + 1) * block, :] = source[
                        r * block : (r + 1) * block, span * 128 : (span + 1) * 128
                    ]
                more_ref[k, r ^ place, spans * block :, :] = lines
            rows = more_ref.shape[2]
            target = grad_hbm[k % 2].at[k // 2, :, pl.ds(shard // 128 * block, rows), :]
            copy = pltpu.make_async_copy(more_ref.at[k], target, more_sem.at[k])
            copy.start()
            pending.append(copy)
    slots = [None, None]
    for k in range(n_shard):
        for j in range(shard // min(SUB, shard)):
            sub = min(SUB, shard)
            at = k * shard + j * sub
            slot = (at // sub) % 2
            value = mm(side_ref[at // part], stack_ref[:, at : at + sub]).astype(BF)
            if slots[slot] is not None:
                slots[slot].wait()
            if halves:
                for r in range(n_row):
                    for t in range(sub // 128):
                        stage_ref[slot, r ^ place, t * block : (t + 1) * block, :] = value[
                            r * block : (r + 1) * block, t * 128 : (t + 1) * 128
                        ]
                rows = sub // 128 * block
                target = grad_hbm[k % 2].at[k // 2, :, pl.ds(j * rows, rows), :]
            else:
                stage_ref[slot] = value
                target = grad_hbm[0].at[k, :, pl.ds(j * sub, sub)]
            slots[slot] = pltpu.make_async_copy(stage_ref.at[slot], target, out_sem.at[slot])
            slots[slot].start()
    for copy in slots + pending:
        copy.wait()


def grad_t(values):
    return values.astype(F32).T.astype(BF)


def quant_call(place, latent, weight, cot, pick, pieces, halves, n_shard, n_row):
    tokens, width = latent.shape
    codes = sum(piece.shape[0] for piece in pieces)
    shard = codes // n_shard
    n_piece = len(pieces)
    sub = min(SUB, shard)
    block = width // n_row
    more = (n_shard, n_row, pick.shape[1] // 128 * block + 2 * shard // 128, 128)
    if halves:
        rows = shard // 128 * block + more[2]
        grads = [jax.ShapeDtypeStruct((n_shard // 2, n_row, rows, 128), BF)] * 2
        stage = (2, n_row, sub // 128 * block, 128)
    else:
        grads = [jax.ShapeDtypeStruct((n_shard, width, shard), BF)]
        stage = (2, width, sub)
        more = (1, 1, 16, 128)
    outs = [
        jax.ShapeDtypeStruct((tokens, width), F32),
        jax.ShapeDtypeStruct((tokens, width), BF),
        jax.ShapeDtypeStruct((DEPTH, tokens, width), BF),
        jax.ShapeDtypeStruct((2, codes), F32),
    ] + grads
    return pl.pallas_call(
        functools.partial(quant_kernel, n_shard, halves, n_piece),
        out_shape=outs,
        in_specs=[smem(), vmem(), smem(), vmem(), vmem()] + [hbm()] * n_piece,
        out_specs=[vmem()] * 4 + [hbm()] * len(grads),
        scratch_shapes=[
            pltpu.VMEM((codes, width), BF),
            pltpu.VMEM((width, codes), BF),
            pltpu.VMEM((tokens, codes // 2), F32),
            pltpu.VMEM((2 * DEPTH * tokens, codes), BF),
            pltpu.VMEM((DEPTH + 1, tokens, width), F32),
            pltpu.VMEM((DEPTH, tokens, width), F32),
            pltpu.VMEM((DEPTH, 2, tokens, 128), F32),
            pltpu.VMEM((2, width, 2 * DEPTH * tokens), BF),
            pltpu.VMEM((2, tokens, width), F32),
            pltpu.VMEM((2, 8, codes), F32),
            pltpu.VMEM((1, codes), F32),
            pltpu.VMEM((tokens, width), F32),
            pltpu.VMEM(stage, BF),
            pltpu.VMEM(more, BF),
            pltpu.SemaphoreType.DMA((n_piece,)),
            pltpu.SemaphoreType.DMA((2,)),
            pltpu.SemaphoreType.DMA((n_shard,)),
        ],
        compiler_params=pltpu.CompilerParams(vmem_limit_bytes=63 * MIB),
        cost_estimate=pl.CostEstimate(
            flops=48 * tokens * width * codes,
            bytes_accessed=18 * MIB,
            transcendentals=DEPTH * tokens * codes,
        ),
        name="soft_quantize",
    )(place, latent, weight, cot, pick, *pieces)


def slope(values):
    sigma = jax.nn.sigmoid(values)
    return sigma * (1.0 + values * (1.0 - sigma))


def norm_back(grad, normed, inverse, gain, per_group, count):
    dn = grad * gain
    first = group_sum(col_sum(dn), per_group) * (1.0 / count)
    second = group_sum(col_sum(dn * normed), per_group) * (1.0 / count)
    return inverse * (dn - first - normed * second)


def conv_back_image(pad_ref, crop, w_ref, side, pixels):
    total = None
    for tap in range(9):
        a, b = tap // 3, tap % 3
        rows = pad_ref[crop, 2 - b, side * (2 - a) : side * (2 - a) + pixels, :]
        part = mm(rows, w_ref[tap], NT)
        total = part if total is None else total + part
    return total


def act_back(read, dact_ref, stats_ref, norm_ref, stage, crops, pixels, channels, grads_ref, store):
    per_group = channels // GROUPS
    count = float(pixels * per_group)
    for k in chunks(channels):
        gain_row = norm_ref[2 * stage : 2 * stage + 1, k]
        bias_row = norm_ref[2 * stage + 1 : 2 * stage + 2, k]
        grad_gain = jnp.zeros((1, 128), F32)
        grad_bias = jnp.zeros((1, 128), F32)
        for c in range(crops):
            inverse = stats_ref[c, 2 * stage + 1 : 2 * stage + 2, k]
            normed = (read(c, k) - stats_ref[c, 2 * stage : 2 * stage + 1, k]) * inverse
            dout = dact_ref[c, :, k] * slope(normed * gain_row + bias_row)
            grad_gain = grad_gain + col_sum(dout * normed)
            grad_bias = grad_bias + col_sum(dout)
            store(c, k, norm_back(dout, normed, inverse, gain_row, per_group, count))
        grads_ref[0:1, k] = grad_gain
        grads_ref[1:2, k] = grad_bias


def second_kernel(
    side,
    dlat_ref,
    pj_ref,
    stats_ref,
    norm_ref,
    dn_hbm,
    conv_hbm,
    w_hbm,
    low_ref,
    dn_ref,
    conv_ref,
    w_ref,
    pad_ref,
    dact_ref,
    ngrad_ref,
    sem,
):
    crops, pixels, channels = conv_ref.shape
    lat = pixels // 4
    tokens, width = dlat_ref.shape
    pairs = ((dn_hbm, dn_ref), (w_hbm.at[1], w_ref), (conv_hbm, conv_ref))
    copies = [pltpu.make_async_copy(*pair, sem.at[k]) for k, pair in enumerate(pairs)]
    for copy in copies:
        copy.start()
    zero_borders(pad_ref, side)
    dlat = dlat_ref[...]
    dred = mm(dlat, pj_ref[...], NT).astype(BF)
    base = 2 * crops * pixels
    low_ref[base : base + tokens, :] = dred
    low_ref[base + tokens : base + 2 * tokens, 0:width] = dlat
    low_ref[base + tokens : base + 2 * tokens, width:] = jnp.zeros((tokens, channels - width), BF)
    order = pixel_order(pixels, side)
    copies[0].wait()
    pieces = [mm(dred, dn_ref[tap], NT).astype(BF) for tap in range(4)]
    for c in range(crops):
        mixed = jnp.concatenate([p[c * lat : (c + 1) * lat] for p in pieces], axis=0)
        low_ref[c * pixels : (c + 1) * pixels, :] = mm(order, mixed, TN).astype(BF)
        for k in chunks(channels):
            rows = low_ref[c * pixels : (c + 1) * pixels, k].astype(F32)
            put_shifted(pad_ref, c, k, rows, side)
    for copy in copies[1:]:
        copy.wait()
    for c in range(crops):
        dact_ref[c] = conv_back_image(pad_ref, c, w_ref, side, pixels)

    def read(c, k):
        return conv_ref[c, :, k]

    def store(c, k, value):
        at = (crops + c) * pixels
        low_ref[at : at + pixels, k] = value.astype(BF)

    act_back(read, dact_ref, stats_ref, norm_ref, 1, crops, pixels, channels, ngrad_ref, store)
    ngrad_ref[2:8, :] = jnp.zeros((6, channels), F32)
    lines = jnp.concatenate([ngrad_ref[...], jnp.zeros((8, channels), F32)], axis=0)
    low_ref[base + 2 * tokens : base + 2 * tokens + 16, :] = lines.astype(BF)


def second_call(dlat, pj, stats, norm, dn, conv, w, side):
    crops, pixels, channels = conv.shape
    tokens = dlat.shape[0]
    return pl.pallas_call(
        functools.partial(second_kernel, side),
        out_shape=jax.ShapeDtypeStruct((2 * crops * pixels + 2 * tokens + 16, channels), BF),
        in_specs=[vmem()] * 4 + [hbm()] * 3,
        out_specs=vmem(),
        scratch_shapes=[
            pltpu.VMEM(dn.shape, BF),
            pltpu.VMEM(conv.shape, F32),
            pltpu.VMEM(w.shape[1:], BF),
            pltpu.VMEM((crops, 3, pixels + 2 * side, channels), BF),
            pltpu.VMEM(conv.shape, F32),
            pltpu.VMEM((8, channels), F32),
            pltpu.SemaphoreType.DMA((3,)),
        ],
        compiler_params=pltpu.CompilerParams(vmem_limit_bytes=LIMIT),
        cost_estimate=SMALL_COST,
        name="second_backward",
    )(dlat, pj, stats, norm, dn, conv, w)


def first_kernel(
    side, n_part, place_ref, x_ref, stats_ref, norm_ref, low_ref, w_hbm, image_out, ngrad_ref, *scratch
):
    w_ref, pad_ref, dact_ref, image_ref, sem = scratch
    crops, pixels, channels = x_ref.shape
    copy = pltpu.make_async_copy(w_hbm.at[0], w_ref, sem.at[0])
    copy.start()
    zero_borders(pad_ref, side)

    def read(c, k):
        return x_ref[c, :, k].astype(F32)

    def store(c, k, value):
        rows = low_ref[c * pixels : (c + 1) * pixels, k].astype(F32)
        image_ref[c, :, k] = (value + rows).astype(BF)

    for c in range(crops):
        at = (crops + c) * pixels
        for k in chunks(channels):
            put_shifted(pad_ref, c, k, low_ref[at : at + pixels, k].astype(F32), side)
    copy.wait()
    for c in range(crops):
        dact_ref[c] = conv_back_image(pad_ref, c, w_ref, side, pixels)
    act_back(read, dact_ref, stats_ref, norm_ref, 0, crops, pixels, channels, ngrad_ref, store)
    ngrad_ref[2:8, :] = jnp.zeros((6, channels), F32)
    if n_part == 1:
        image_out[...] = image_ref[...]
        return
    span = pixels // n_part
    row = 0
    for k in range(n_part):
        at = pl.multiple_of((place_ref[0] ^ k) * span, span)
        for c in range(crops):
            for lanes in chunks(channels):
                image_out[row : row + span, :] = image_ref[c, pl.ds(at, span), lanes]
                row += span


def first_call(place, x, stats, norm, low, w, side, n_part):
    crops, pixels, channels = x.shape
    shape = (crops, pixels, channels) if n_part == 1 else (x.size // 128, 128)
    return pl.pallas_call(
        functools.partial(first_kernel, side, n_part),
        out_shape=[
            jax.ShapeDtypeStruct(shape, BF),
            jax.ShapeDtypeStruct((8, channels), F32),
        ],
        in_specs=[smem()] + [vmem()] * 4 + [hbm()],
        out_specs=[vmem()] * 2,
        scratch_shapes=[
            pltpu.VMEM(w.shape[1:], BF),
            pltpu.VMEM((crops, 3, pixels + 2 * side, channels), BF),
            pltpu.VMEM(x.shape, F32),
            pltpu.VMEM(x.shape, BF),
            pltpu.SemaphoreType.DMA((1,)),
        ],
        compiler_params=pltpu.CompilerParams(vmem_limit_bytes=LIMIT),
        cost_estimate=SMALL_COST,
        name="first_backward",
    )(place, x, stats, norm, low, w)


class Image:
    def __init__(self, array, count):
        self.rows = array.shape[0] // count
        self.chunks = {(0, k): (array, k * self.rows) for k in range(count)}
        self.order = list(IMAGE_PLAN)

    def leaving(self):
        bit = LINKS[self.order[0]][1]
        return sorted(key for key in self.chunks if key[1] & bit)

    def arrive(self, array, base):
        bit = LINKS[self.order[0]][1]
        for k, key in enumerate(self.leaving()):
            del self.chunks[key]
            self.chunks[key[0] ^ bit, key[1] & ~bit] = (array, base + k * self.rows)
        self.order.pop(0)


def image_kernel(rows, jobs, n_in, place_ref, *refs):
    ins, (out_ref, chunk_ref, sem) = refs[:n_in], refs[n_in:]
    loads = [
        pltpu.make_async_copy(ins[k].at[pl.ds(row, rows), :], chunk_ref.at[source], sem.at[source])
        for source, k, row in jobs
    ]
    for load in loads:
        load.start()
    for load in loads:
        load.wait()
    span, channels = out_ref.shape[1:]
    crops = out_ref.shape[0] // len(jobs)
    for source in range(len(jobs)):
        row = 0
        for c in range(crops):
            for lanes in chunks(channels):
                value = chunk_ref[source, row : row + span, :].astype(F32)
                out_ref[(place_ref[0] ^ source) * crops + c, :, lanes] = value
                row += span


def image_call(place, image, shape):
    arrays, jobs = [], []
    for (source, _), (array, row) in sorted(image.chunks.items(), key=lambda item: item[0]):
        jobs.append((source, operand_index(arrays, array), row))
    return pl.pallas_call(
        functools.partial(image_kernel, image.rows, jobs, len(arrays)),
        out_shape=jax.ShapeDtypeStruct(shape, F32),
        in_specs=[smem()] + [anywhere()] * len(arrays),
        out_specs=vmem(),
        scratch_shapes=[
            pltpu.VMEM((len(jobs), image.rows, 128), BF),
            pltpu.SemaphoreType.DMA((len(jobs),)),
        ],
        compiler_params=pltpu.CompilerParams(vmem_limit_bytes=LIMIT),
        cost_estimate=SMALL_COST,
        name="image_assembly",
    )(place, *arrays)


BLOCK = 64
TAIL = 48


def matrix_kernel(side, crops, pixels, width, plan, n_set, place_ref, *refs):
    sources, refs = refs[: 3 * n_set], refs[3 * n_set :]
    n_out = 2 * len(plan) if plan else 1
    targets, refs = refs[:n_out], refs[n_out:]
    saves, refs = refs[:n_set], refs[n_set:]
    lows, refs = refs[:n_set], refs[n_set:]
    norms, refs = refs[:n_set], refs[n_set:]
    outs, (pad_ref, in_sem, out_sem) = refs[:n_out], refs[n_out:]
    channels = pad_ref.shape[3]
    locals_ = list(saves) + list(lows) + list(norms)
    image = crops * pixels
    loads = []
    for save_at, low_at in ((image, 0), (2 * image, 2 * image), (0, image)):
        group = []
        for k in range(2 * n_set):
            at = save_at if k < n_set else low_at
            count = image if at < 2 * image else sources[k].shape[0] - 2 * image
            rows = pl.ds(at, count)
            group.append(
                pltpu.make_async_copy(
                    sources[k].at[rows, :], locals_[k].at[rows, :], in_sem.at[len(loads), k]
                )
            )
        loads.append(group)
    for k in range(2 * n_set, 3 * n_set):
        loads[1].append(pltpu.make_async_copy(sources[k], locals_[k], in_sem.at[1, k]))
    for group in loads:
        for load in group:
            load.start()
    stores = [
        pltpu.make_async_copy(outs[k], targets[k].at[pl.ds(0, outs[k].shape[0])], out_sem.at[k])
        for k in range(n_out)
    ]
    done = {}
    tokens = crops * pixels // 4
    odd = place_ref[1] % 2 == 1
    line = place_ref[1] // 2 % 2
    dp = place_ref[0]
    zero_borders(pad_ref, side)

    def arrive(group):
        for load in loads[group]:
            load.wait()

    def half(values):
        if not plan:
            return values
        parts = []
        for k in range(0, values.shape[1], 256):
            parts.append(jnp.where(odd, values[:, k + 128 : k + 256], values[:, k : k + 128]))
        return jnp.concatenate(parts, axis=1)

    def low_rows(at, count):
        return jnp.concatenate([half(low[at : at + count, :]) for low in lows], axis=0)

    def squeeze(index, bit):
        return (index >> (bit + 1) << bit) | (index & ((1 << bit) - 1))

    def place_rows(part, row, count, value):
        keep_ref, send_ref = outs[2 * part], outs[2 * part + 1]
        rows = keep_ref.shape[1]
        name = plan[part][1].split()[0]

        def put(lead, keep, send):
            keep_ref[lead, row : row + count, :] = keep
            send_ref[pl.ds(pl.multiple_of(lead * rows + row, 16), count), :] = send

        if name == "x":
            far = line == 1
            keep = jnp.where(far, value[:, 128:], value[:, :128])
            send = jnp.where(far, value[:, :128], value[:, 128:])
            for i in range(8):
                at = slice(i * count, (i + 1) * count)
                put(i ^ dp, keep[at], send[at])
            return
        bit = {"y": 0, "z1": 1, "z2": 2}[name]
        other = (dp >> bit) & 1 == 1
        for pair in range(2):
            lead = (pair ^ line) * 4
            for i in range(8):
                if i >> bit & 1:
                    continue
                j = i | 1 << bit
                lanes = slice(pair * 128, pair * 128 + 128)
                first = value[i * count : (i + 1) * count, lanes]
                second = value[j * count : (j + 1) * count, lanes]
                put(
                    lead + (squeeze(i, bit) ^ squeeze(dp, bit)),
                    jnp.where(other, second, first),
                    jnp.where(other, first, second),
                )

    def store(block, value):
        value = value.astype(BF)
        if not plan:
            outs[0][block * channels : (block + 1) * channels, 0 : value.shape[1]] = value
            return
        part = 0
        while block >= plan[part][0] // 4:
            block -= plan[part][0] // 4
            part += 1
        place_rows(part, block * BLOCK, BLOCK, value)
        done[part] = done.get(part, 0) + 4
        if done[part] == plan[part][0]:
            stores[2 * part].start()
            stores[2 * part + 1].start()

    def taps(save_at, low_at, first_block):
        for n, save in enumerate(saves):
            for c in range(crops):
                for k in chunks(channels):
                    rows = save[save_at + c * pixels : save_at + (c + 1) * pixels, k]
                    put_shifted(pad_ref, n * crops + c, k, rows.astype(F32), side)
        grad = low_rows(low_at, crops * pixels).T
        for tap in range(9):
            a, b = tap // 3, tap % 3
            rows = [
                pad_ref[c, b, side * a : side * a + pixels, :] for c in range(n_set * crops)
            ]
            store(first_block + tap, mm(grad, jnp.concatenate(rows, axis=0)).astype(BF).T)

    arrive(0)
    taps(crops * pixels, 0, 0)
    arrive(1)
    base = 2 * crops * pixels
    dred = low_rows(base, tokens).T
    for tap in range(4):
        at = base + tap * tokens
        rows = jnp.concatenate([save[at : at + tokens, :] for save in saves], axis=0)
        store(9 + tap, mm(dred, rows).astype(BF).T)
    arrive(2)
    taps(0, crops * pixels, 13)
    at = base + 4 * tokens
    rows = jnp.concatenate([save[at : at + tokens, :] for save in saves], axis=0)
    dlat = [low[base + tokens : base + 2 * tokens, 0:width] for low in lows]
    if not plan:
        store(22, mm(rows, dlat[0], TN))
        stores[0].start()
        stores[0].wait()
        return
    narrow = []
    for part in dlat:
        pieces = [part[:, k : k + 64] for k in range(0, width, 64)]
        narrow.append(
            jnp.concatenate(
                [
                    jnp.where(odd, pieces[1], pieces[0]),
                    jnp.where(odd, pieces[3], pieces[2]),
                ],
                axis=1,
            )
        )
    proj = mm(rows, jnp.concatenate(narrow, axis=0), TN).astype(BF)
    lines = []
    first = norms[0][0:2, :] + norms[1][0:2, :]
    at = base + 2 * tokens
    second = lows[0][at : at + 16, :].astype(F32) + lows[1][at : at + 16, :].astype(F32)
    for rows in (first, second[0:2]):
        for k in range(2):
            lines += [rows[k : k + 1, lanes] for lanes in chunks(channels)]
    lines = jnp.concatenate(lines, axis=0).astype(BF)
    folded = []
    for i in range(8):
        top = proj[i * 64 : i * 64 + 32]
        low = proj[i * 64 + 32 : (i + 1) * 64]
        block = jnp.concatenate([top[:, 0:64], low[:, 0:64], top[:, 64:], low[:, 64:]], axis=1)
        folded.append(
            jnp.concatenate([block, jnp.concatenate([lines, lines], axis=1)], axis=0)
        )
    last = len(plan) - 1
    place_rows(last, outs[2 * last].shape[1] - TAIL, TAIL, jnp.concatenate(folded, axis=0))
    stores[2 * last].start()
    stores[2 * last + 1].start()
    for store_ in stores:
        store_.wait()


def matrix_call(place, saves, lows, norms, side, crops, pixels, width, plan, room=None):
    channels = saves[0].shape[1]
    n_set = len(saves)
    if plan:
        outs, shapes = [], []
        for units, order in plan:
            rows = 8 * 16 * units
            shapes += [(8, 16 * units, 128), (rows, 128)]
            outs.append(jax.ShapeDtypeStruct(shapes[-2], BF))
            outs.append(jax.ShapeDtypeStruct((rows + room.get(order.split()[0], 0), 128), BF))
    else:
        outs = [jax.ShapeDtypeStruct((23 * channels, channels), BF)]
        shapes = [outs[0].shape]
    return pl.pallas_call(
        functools.partial(matrix_kernel, side, crops, pixels, width, plan, n_set),
        out_shape=outs,
        in_specs=[smem()] + [hbm()] * (3 * n_set),
        out_specs=[hbm()] * len(outs),
        scratch_shapes=[pltpu.VMEM(a.shape, a.dtype) for a in (*saves, *lows, *norms)]
        + [pltpu.VMEM(shape, BF) for shape in shapes]
        + [
            pltpu.VMEM((n_set * crops, 3, pixels + 2 * side, channels), BF),
            pltpu.SemaphoreType.DMA((3, 3 * n_set)),
            pltpu.SemaphoreType.DMA((len(outs),)),
        ],
        compiler_params=pltpu.CompilerParams(vmem_limit_bytes=LIMIT),
        cost_estimate=SMALL_COST,
        name="matrix_backward",
    )(place, *saves, *lows, *norms)


def swap(array, axis, bit):
    count = lax.axis_size(axis)
    return lax.ppermute(array, axis, [(i, i ^ bit) for i in range(count)])


def add_low(first, second):
    return (first.astype(F32) + second.astype(F32)).astype(BF)


LINKS = {"x": ("code", 2), "y": ("dp", 1), "z1": ("dp", 2), "z2": ("dp", 4)}
BITS = ("x", "z2", "z1", "y")
CODE_PLAN = ((36, "z1 y x z2"), (36, "y x z2 z1"))
MATRIX_PLAN = ((28, "x z1 y z2"), (28, "y x z2 z1"), (35, "z1 y x z2"))
IMAGE_PLAN = ("z2", "y", "z1")


class Part:
    def __init__(self, array, low, rows, order, arrival):
        self.array, self.low, self.rows = array, low, rows
        self.order, self.dims = order.split(), list(BITS)
        self.arrival, self.offset = arrival, None


def split_parts(keep, arrival, plan):
    shape = (keep.shape[0] * keep.shape[1],) + keep.shape[2:]
    keep, arrival = keep.reshape(shape), arrival.reshape(shape)
    assert 16 * sum(units for units, _ in plan) == shape[1]
    parts, low = [], 0
    for units, order in plan:
        parts.append(Part(keep, low, 16 * units, order, arrival))
        low += 16 * units
    return parts


def merge_kernel(jobs, moves, n_in, n_out, *refs):
    ins, outs, scratch = refs[:n_in], refs[n_in : n_in + n_out], refs[n_in + n_out :]
    sem = scratch[-1]
    loads, stores = [], []
    passing = []
    for k, (source, row, target, place, rows) in enumerate(moves):
        held = scratch[-2].at[k]
        at = 4 * len(jobs) + 2 * k
        load = pltpu.make_async_copy(ins[source].at[pl.ds(row, rows), :], held, sem.at[at])
        store = pltpu.make_async_copy(held, outs[target].at[pl.ds(place, rows), :], sem.at[at + 1])
        load.start()
        passing.append((load, store))
    for j, job in enumerate(jobs):
        mine, other = scratch[4 * j], scratch[4 * j + 1]
        source = ins[job["array"]].at[:, pl.ds(job["low"], job["rows"]), :]
        first = pltpu.make_async_copy(source, mine, sem.at[4 * j])
        if job["flat"] is None:
            source = ins[job["arrival"]].at[:, pl.ds(job["low"], job["rows"]), :]
        else:
            source = ins[job["arrival"]].at[pl.ds(job["flat"], other.shape[0]), :]
        second = pltpu.make_async_copy(source, other, sem.at[4 * j + 1])
        first.start()
        second.start()
        loads.append((first, second))
    for load, store in passing:
        load.wait()
        store.start()
        stores.append(store)
    for j, job in enumerate(jobs):
        mine, other, keep, send = scratch[4 * j : 4 * j + 4]
        for load in loads[j]:
            load.wait()
        rows, count = job["rows"], [0, 0]
        for lead in range(mine.shape[0]):
            at = slice(lead * rows, (lead + 1) * rows)
            value = add_low(mine[lead], other[lead] if job["flat"] is None else other[at, :])
            half = lead >> job["bit"] & 1
            if half == 0:
                keep[count[0]] = value
            else:
                send[count[1] * rows : (count[1] + 1) * rows, :] = value
            count[half] += 1
        target = outs[job["send"]].at[pl.ds(job["place"], send.shape[0]), :]
        for k, pair in enumerate(((keep, outs[job["keep"]]), (send, target))):
            copy = pltpu.make_async_copy(*pair, sem.at[4 * j + 2 + k])
            copy.start()
            stores.append(copy)
    for copy in stores:
        copy.wait()


def operand_index(arrays, array):
    for k, known in enumerate(arrays):
        if known is array:
            return k
    arrays.append(array)
    return len(arrays) - 1


def merge(parts, given=(), image=None):
    sizes, groups = {}, {}
    arrays, jobs, scratch = [], [], []
    for name, _, group in given:
        groups[name] = list(group)
        sizes[name] = sum(p.rows * 2 ** (len(p.dims) - 1) for p in group)
    links = {p.order[0] for p in parts}
    if image is not None:
        links.add(image.order[0])
    names = sorted(links)
    for k, part in enumerate(parts):
        lead = 2 ** len(part.dims)
        name = part.order[0]
        jobs.append(
            {
                "array": operand_index(arrays, part.array),
                "arrival": operand_index(arrays, part.arrival),
                "low": part.low,
                "rows": part.rows,
                "flat": part.offset,
                "keep": k,
                "bit": len(part.dims) - 1 - part.dims.index(name),
                "send": len(parts) + names.index(name),
                "place": sizes.get(name, 0),
            }
        )
        part.offset = sizes.get(name, 0)
        sizes[name] = part.offset + part.rows * lead // 2
        groups.setdefault(name, []).append(part)
        flat = jobs[-1]["flat"] is not None
        scratch += [
            pltpu.VMEM((lead, part.rows, 128), BF),
            pltpu.VMEM((lead * part.rows, 128) if flat else (lead, part.rows, 128), BF),
            pltpu.VMEM((lead // 2, part.rows, 128), BF),
            pltpu.VMEM((lead // 2 * part.rows, 128), BF),
        ]
    moves = []
    if image is not None:
        name = image.order[0]
        image.base = sizes.get(name, 0)
        for key in image.leaving():
            array, row = image.chunks[key]
            at = sizes.get(name, 0)
            moves.append(
                (operand_index(arrays, array), row, len(parts) + names.index(name), at, image.rows)
            )
            sizes[name] = at + image.rows
        groups.setdefault(name, []).append(image)
    outs = [jax.ShapeDtypeStruct((2 ** (len(p.dims) - 1), p.rows, 128), BF) for p in parts]
    outs += [jax.ShapeDtypeStruct((sizes[name], 128), BF) for name in names]
    aliases = {}
    for name, array, _ in given:
        if name in names:
            assert array.shape == (sizes[name], 128)
            aliases[len(arrays)] = len(parts) + names.index(name)
            arrays.append(array)
    result = pl.pallas_call(
        functools.partial(merge_kernel, jobs, moves, len(arrays), len(outs)),
        out_shape=outs,
        input_output_aliases=aliases,
        in_specs=[anywhere()] * len(arrays),
        out_specs=[anywhere()] * len(outs),
        scratch_shapes=scratch
        + [
            pltpu.VMEM((max(len(moves), 1), image.rows if image is not None else 16, 128), BF),
            pltpu.SemaphoreType.DMA((4 * len(parts) + 2 * len(moves),)),
        ],
        compiler_params=pltpu.CompilerParams(vmem_limit_bytes=LIMIT),
        cost_estimate=SMALL_COST,
        name="merge_parts",
    )(*arrays)
    for k, part in enumerate(parts):
        part.array, part.low, part.arrival = result[k], 0, None
    sends = [(name, result[len(parts) + k], groups[name]) for k, name in enumerate(names)]
    return sends + [entry for entry in given if entry[0] not in names]


def fly(sends):
    return [(name, swap(array, *LINKS[name]), group) for name, array, group in sends]


def land(flights, *others):
    tied = lax.optimization_barrier(tuple(array for _, array, _ in flights) + tuple(others))
    for (name, _, group), array in zip(flights, tied):
        for part in group:
            if isinstance(part, Image):
                part.arrive(array, part.base)
                continue
            part.order.pop(0)
            part.dims.remove(name)
            part.arrival = array
    return tied[len(flights) :]


def sum_parts(parts, ins, target):
    at = 0
    for part in parts:
        rows = part["rows"]
        value = ins[part["array"]][0].astype(F32)
        value = value + ins[part["arrival"]][part["offset"] : part["offset"] + rows, :].astype(F32)
        target[at : at + rows, :] = value
        at += rows


def matrix_update_kernel(parts, n_in, rates, *refs):
    n_all = n_in + 12
    sources, targets, refs = refs[:n_all], refs[n_all : n_all + 12], refs[n_all + 12 :]
    locals_, outs, refs = refs[:n_all], refs[n_all : n_all + 12], refs[n_all + 12 :]
    mat_ref, in_sem, out_sem = refs
    loads = [pltpu.make_async_copy(sources[k], locals_[k], in_sem.at[k]) for k in range(n_all)]
    for load in loads:
        load.start()
    stores = [pltpu.make_async_copy(outs[k], targets[k], out_sem.at[k]) for k in range(12)]
    conv_m, conv_v, conv_a, down_m, down_v, down_a, proj_m, proj_v, proj_a, *rest = locals_[n_in:]
    norm_m, norm_v, norm_a = rest
    for load in loads[:n_in]:
        load.wait()
    sum_parts(parts, locals_[:n_in], mat_ref)
    for load in loads[n_in:]:
        load.wait()

    def step(refs, index, grad, rate, results):
        master, moment, average = refs
        moment_new = MOMENTUM * moment[index] + grad
        master_new = master[index] - rate * (grad + MOMENTUM * moment_new)
        results[0][index] = moment_new
        results[1][index] = master_new
        results[2][index] = AVERAGE_DECAY * average[index] + (1.0 - AVERAGE_DECAY) * master_new

    weight_rate, norm_rate = rates
    block = conv_m.shape[0] // 18
    for conv in range(2):
        for tap in range(9):
            row = (13 + tap if conv == 0 else tap) * block
            index = (pl.ds(tap * 2 + conv, block, stride=18), slice(None))
            grad = mat_ref[row : row + block, :]
            step((conv_m, conv_v, conv_a), index, grad, weight_rate, outs[0:3])
    for store in stores[:3]:
        store.start()
    for tap in range(4):
        index = (pl.ds(tap, block, stride=4), slice(None))
        grad = mat_ref[(9 + tap) * block : (10 + tap) * block, :]
        step((down_m, down_v, down_a), index, grad, weight_rate, outs[3:6])
    tail = 22 * block
    for k in range(2):
        index = (slice(k * block // 2, (k + 1) * block // 2), slice(None))
        grad = mat_ref[tail : tail + block // 2, k * 64 : (k + 1) * 64]
        step((proj_m, proj_v, proj_a), index, grad, weight_rate, outs[6:9])
    tail += block // 2
    lines = norm_m.shape[1] // 128
    for k in range(4):
        for j in range(lines):
            index = (slice(k, k + 1), slice(j * 128, (j + 1) * 128))
            row = tail + k * lines + j
            step((norm_m, norm_v, norm_a), index, mat_ref[row : row + 1, :], norm_rate, outs[9:12])
    for store in stores[3:]:
        store.start()
    for store in stores:
        store.wait()


def code_update_kernel(parts, n_in, code_rate, mean_count, *refs):
    n_all = n_in + 6
    sources, targets, refs = refs[:n_all], refs[n_all : n_all + 4], refs[n_all + 4 :]
    locals_, outs, refs = refs[:n_all], refs[n_all : n_all + 4], refs[n_all + 4 :]
    code_ref, in_sem, out_sem = refs
    loads = [pltpu.make_async_copy(sources[k], locals_[k], in_sem.at[k]) for k in range(n_all)]
    for load in loads:
        load.start()
    stores = [pltpu.make_async_copy(outs[k], targets[k], out_sem.at[k]) for k in range(4)]
    code_m, code_v, code_a, own_ref, select_ref, chosen_ref = locals_[n_in:]
    for load in loads:
        load.wait()
    sum_parts(parts, locals_[:n_in], code_ref)
    cols, codes = code_m.shape
    tiles = codes // 128
    base = tiles * cols
    spans = select_ref.shape[0] // 128
    source = jnp.concatenate(
        [code_ref[base + k * cols : base + (k + 1) * cols, :] for k in range(spans)], axis=1
    ).astype(BF)
    base += spans * cols
    outs[3][...] = code_ref[base : base + tiles, :] * (1.0 / mean_count)
    wide = 512
    for k in range(codes // wide):
        lanes = slice(k * wide, (k + 1) * wide)
        four = range(k * wide // 128, (k + 1) * wide // 128)
        grad = jnp.concatenate([code_ref[t * cols : (t + 1) * cols, :] for t in four], axis=1)
        slope_sum = jnp.concatenate(
            [code_ref[base + tiles + t : base + tiles + t + 1, :] for t in four], axis=1
        )
        count = jnp.concatenate([code_ref[base + t : base + t + 1, :] for t in four], axis=1)
        grad = grad - own_ref[:, lanes].astype(F32) * slope_sum
        moment_new = MOMENTUM * code_v[:, lanes] + grad
        stepped = code_m[:, lanes] - code_rate * (grad + MOMENTUM * moment_new)
        renewed = mm(source, select_ref[:, lanes])
        share = chosen_ref[:, lanes] * (mean_count / (mean_count + count))
        master_new = stepped + share * (renewed - stepped)
        outs[0][:, lanes] = moment_new
        outs[1][:, lanes] = master_new
        outs[2][:, lanes] = AVERAGE_DECAY * code_a[:, lanes] + (1.0 - AVERAGE_DECAY) * master_new
    for store in stores:
        store.start()
    for store in stores:
        store.wait()


def update_call(kernel, name, parts, states, shapes, *settings):
    arrays, jobs = [], []
    for part in parts:
        jobs.append(
            {
                "array": operand_index(arrays, part.array),
                "arrival": operand_index(arrays, part.arrival),
                "offset": part.offset,
                "rows": part.rows,
            }
        )
    outs = [jax.ShapeDtypeStruct(shape, F32) for shape in shapes]
    args = arrays + list(states)
    return pl.pallas_call(
        functools.partial(kernel, jobs, len(arrays), *settings),
        out_shape=outs,
        in_specs=[hbm()] * len(args),
        out_specs=[hbm()] * len(outs),
        scratch_shapes=[pltpu.VMEM(a.shape, a.dtype) for a in args]
        + [pltpu.VMEM(out.shape, F32) for out in outs]
        + [
            pltpu.VMEM((sum(p.rows for p in parts), 128), F32),
            pltpu.SemaphoreType.DMA((len(args),)),
            pltpu.SemaphoreType.DMA((len(outs),)),
        ],
        compiler_params=pltpu.CompilerParams(vmem_limit_bytes=LIMIT),
        cost_estimate=SMALL_COST,
        name=name,
    )(*args)


def nesterov_step(master, moment, average, grad, rate):
    moment_new = MOMENTUM * moment + grad
    master_new = master - rate * (grad + MOMENTUM * moment_new)
    return (moment_new, master_new, AVERAGE_DECAY * average + (1.0 - AVERAGE_DECAY) * master_new)


def body(
    crops_in,
    crop_weight,
    cotangent,
    conv_copy,
    down_copy,
    proj_copy,
    norm_copy,
    codebook,
    conv_master,
    conv_moment,
    conv_average,
    down_master,
    down_moment,
    down_average,
    proj_master,
    proj_moment,
    proj_average,
    norm_master,
    norm_moment,
    norm_average,
    code_master,
    code_moment,
    code_average,
    repl_code,
    repl_src,
):
    dp_count = lax.axis_size("dp")
    code_count = lax.axis_size("code")
    dp_at = lax.axis_index("dp")
    code_at = lax.axis_index("code")
    halves = dp_count == 8 and code_count == 4
    place = jnp.stack([dp_at, code_at]).astype(jnp.int32)

    local = lax.all_to_all(crops_in, "dp", split_axis=1, concat_axis=2, tiled=True)[0]
    crop_dev, pixels, channels = local.shape
    side = math.isqrt(pixels)
    lat = pixels // 4
    tokens = crop_dev * lat
    width = proj_copy.shape[1]
    code_dev = codebook.shape[0]
    codes_all = code_dev * code_count

    crops_set = crop_dev * dp_count
    flat_src = repl_src.reshape(-1)
    crop_id = flat_src // lat % crops_set
    owner = (crop_id // crop_dev == dp_at) & (flat_src // (crops_set * lat) == code_at)
    row_id = crop_id % crop_dev * lat + flat_src % lat
    depth_id = jnp.repeat(jnp.arange(DEPTH, dtype=jnp.int32), repl_src.shape[1])
    pick = (
        jnp.where(owner, depth_id * tokens + row_id, -1)[None, :]
        == jnp.arange(DEPTH * tokens, dtype=jnp.int32)[:, None]
    ).astype(BF)
    weight_col = crop_weight.astype(F32).reshape(crop_dev)
    dn = down_copy.transpose(1, 0, 2)
    gains = norm_copy.T.astype(F32)
    own_codes = lax.dynamic_slice_in_dim(codebook, dp_at * (width // dp_count), width // dp_count, 1).T
    select = (
        repl_code.reshape(-1)[:, None] - code_at * code_dev
        == jnp.arange(code_dev, dtype=jnp.int32)[None, :]
    )
    chosen = jnp.sum(select.astype(F32), axis=0)
    select = select.astype(BF)
    if halves:
        quarter = code_dev // 4
        corner = (dp_at & 1) * 2 + ((dp_at >> 1) & 1)
        mine = lax.dynamic_slice_in_dim(codebook, corner * quarter, quarter, 0)
        over_x = swap(mine, "code", 2)
        over_x, conv_copy, dn, gains, pick, weight_col, place = lax.optimization_barrier(
            (over_x, conv_copy, dn, gains, pick, weight_col, place)
        )
        over_y, over_z = swap(over_x, "dp", 1), swap(over_x, "dp", 2)
        core = swap(codebook, "code", 1)
        diag = [swap(over_x, "code", 1)]
        w = conv_copy.transpose(1, 2, 0, 3)
        over_y, over_z, local, w, core, diag[0] = lax.optimization_barrier(
            (over_y, over_z, local, w, core, diag[0])
        )
        last = [swap(over_z[: quarter // 2], "dp", 1), swap(over_y[quarter // 2 :], "dp", 2)]
        diag = diag + [swap(piece, "code", 1) for piece in (over_y, over_z)]
    else:
        w = conv_copy.transpose(1, 2, 0, 3)
        every = lax.all_gather(codebook, "code", axis=0)
        pieces = [every[k] for k in range(code_count)]

    conv1, stats, save, latent = forward_call(local, gains, w, dn, proj_copy, side)
    if halves:
        last[0], last[1], latent = lax.optimization_barrier((last[0], last[1], latent))
        diag = diag + [swap(piece, "code", 1) for piece in last]
        pieces = [codebook, core, over_x, over_y, over_z] + last + diag
        saves = (save, swap(save, "code", 1))

    n_row = dp_count if halves else 1
    quantized, dlat, rows, extra, *code_grads = quant_call(
        place,
        latent,
        weight_col,
        cotangent.reshape(tokens, width),
        pick,
        pieces,
        halves,
        code_count,
        n_row,
    )
    pixels_all = crop_dev * pixels * dp_count * code_count
    weight_rate = WEIGHT_RATE / math.sqrt(pixels_all)
    norm_rate = NORM_RATE / math.sqrt(pixels_all)
    crops_all = crop_dev * dp_count * code_count
    mean_count = DEPTH * lat * crops_all / codes_all
    code_rate = CODE_RATE / math.sqrt(mean_count)
    low = second_call(dlat, proj_copy, stats, gains, dn, conv1, w, side)

    if halves:
        code_core = swap(code_grads[1], "code", 1)
        low_mate = swap(low, "code", 1)
        code_core, low, save_mate = lax.optimization_barrier((code_core, low, saves[1]))
        codes = split_parts(code_grads[0], code_core, CODE_PLAN)
        sends = merge(codes)
        tied = lax.optimization_barrier(tuple(array for _, array, _ in sends) + (low, low_mate))
        low, low_mate = tied[-2:]
        flights = fly([(name, tied[k], group) for k, (name, _, group) in enumerate(sends)])
        image, ngrad = first_call(place, local, stats, gains, low, w, side, dp_count)
        ngrad_mate = swap(ngrad, "code", 1)
        image = Image(image, dp_count)
        room = {}
        for part in codes:
            name = part.order[1]
            room[name] = room.get(name, 0) + part.rows * 2 ** (len(part.dims) - 2)
        results = matrix_call(
            place, (save, save_mate), (low, low_mate), (ngrad, ngrad_mate), side, crop_dev, pixels,
            width, MATRIX_PLAN, room,
        )
        mats, given = [], []
        results = land(flights, *results)
        for k, (units, order) in enumerate(MATRIX_PLAN):
            part = Part(results[2 * k], 0, 16 * units, order, None)
            part.offset = 0
            mats.append(part)
            given.append((part.order[0], results[2 * k + 1], [part]))
        own_codes, select, chosen = land(
            fly(merge(codes, given, image)), own_codes, select, chosen
        )
        parts = codes + mats
        for _ in range(3):
            active = [part for part in parts if part.order]
            land(fly(merge(active, image=image if image.order else None)))
        shape = (crop_dev * dp_count, pixels // dp_count, channels)
        input_back = image_call(place, image, shape)[None]

        def flat(array):
            return array.transpose(0, 2, 1, 3).reshape(-1, 128)

        states = [flat(array) for array in (conv_master, conv_moment, conv_average)]
        states += [a.reshape(-1, 128) for a in (down_master, down_moment, down_average)]
        states += [proj_master, proj_moment, proj_average]
        states += [a.T for a in (norm_master, norm_moment, norm_average)]
        out = update_call(
            matrix_update_kernel, "matrix_updates", mats, states, [a.shape for a in states],
            (weight_rate, norm_rate),
        )
        states = [a.T for a in (code_master, code_moment, code_average)]
        states += [own_codes, select, chosen[None, :]]
        shapes = [states[0].shape] * 3 + [(code_dev // 128, 128)]
        code_out = update_call(
            code_update_kernel, "code_updates", codes, states, shapes, code_rate, mean_count
        )
        rows_in = channels // dp_count
        conv_out = [
            a.reshape(rows_in, 9, 2, channels // code_count).transpose(0, 2, 1, 3) for a in out[0:3]
        ]
        return (
            quantized.reshape(1, crop_dev, lat, width),
            input_back,
            *conv_out,
            *[a.reshape(down_master.shape) for a in out[3:6]],
            *out[6:9],
            *[a.T for a in out[9:12]],
            *[a.T for a in code_out[:3]],
            code_out[3].reshape(code_dev),
        )

    image, ngrad = first_call(place, local, stats, gains, low, w, side, 1)
    (grads,) = matrix_call(
        place, (save,), (low,), (ngrad,), side, crop_dev, pixels, width, None
    )
    grads = grads.reshape(23, channels, channels)
    base = 2 * crop_dev * pixels + 2 * tokens
    norm_grad = jnp.concatenate([ngrad[0:2], low[base : base + 2].astype(F32)], axis=0)
    flat = lax.psum_scatter(code_grads[0], "code", scatter_dimension=0, tiled=True)[0]
    code_grad = lax.psum_scatter(flat, "dp", scatter_dimension=0, tiled=True).astype(F32)
    sums = lax.psum_scatter(extra, "code", scatter_dimension=1, tiled=True)
    sums = lax.psum(sums, "dp")
    source = mm(rows.reshape(DEPTH * tokens, width), pick, TN).astype(BF)
    source_rows = lax.psum_scatter(source, "dp", scatter_dimension=0, tiled=True)
    source_rows = lax.psum(source_rows, "code")

    def matrix(array, scatter):
        array = lax.psum_scatter(array, "dp", scatter_dimension=0, tiled=True)
        return lax.psum_scatter(array, "code", scatter_dimension=scatter, tiled=True).astype(F32)

    conv_part = matrix(jnp.stack([grads[13:22], grads[0:9]]).transpose(2, 0, 1, 3), 3)
    down_part = matrix(grads[9:13].transpose(1, 0, 2), 2)
    proj_part = matrix(grads[22, :, :width], 1)
    norm_grad = lax.psum(norm_grad, ("dp", "code"))
    input_back = lax.all_to_all(
        image[None], "dp", split_axis=2, concat_axis=1, tiled=True
    ).astype(F32)
    conv_out = nesterov_step(conv_master, conv_moment, conv_average, conv_part, weight_rate)
    down_out = nesterov_step(down_master, down_moment, down_average, down_part, weight_rate)
    proj_out = nesterov_step(proj_master, proj_moment, proj_average, proj_part, weight_rate)
    norm_out = nesterov_step(norm_master, norm_moment, norm_average, norm_grad.T, norm_rate)

    counts_all, slope_sum = sums[0], sums[1]
    share = mean_count / (mean_count + counts_all)
    code_load = counts_all / mean_count
    code_grad = code_grad - own_codes.astype(F32) * slope_sum[None, :]
    code_moment_new = MOMENTUM * code_moment.T + code_grad
    stepped = code_master.T - code_rate * (code_grad + MOMENTUM * code_moment_new)
    renewed = mm(source_rows, select)
    code_master_new = stepped + (chosen * share)[None, :] * (renewed - stepped)
    code_average_new = AVERAGE_DECAY * code_average.T + (1.0 - AVERAGE_DECAY) * code_master_new
    return (
        quantized.reshape(1, crop_dev, lat, width),
        input_back,
        *conv_out,
        *down_out,
        *proj_out,
        *norm_out,
        code_moment_new.T,
        code_master_new.T,
        code_average_new.T,
        code_load,
    )


def solution(mesh):
    in_specs = (
        P("code", None, "dp", None),
        P("code", "dp"),
        P("code", "dp", None, None),
        P(),
        P(),
        P(),
        P(),
        P("code", None),
        P("dp", None, None, "code"),
        P("dp", None, None, "code"),
        P("dp", None, None, "code"),
        P("dp", None, "code"),
        P("dp", None, "code"),
        P("dp", None, "code"),
        P("dp", "code"),
        P("dp", "code"),
        P("dp", "code"),
        P(),
        P(),
        P(),
        P("code", "dp"),
        P("code", "dp"),
        P("code", "dp"),
        P(),
        P(),
    )
    out_specs = (
        P("code", "dp", None, None),
        P("code", None, "dp", None),
        P("dp", None, None, "code"),
        P("dp", None, None, "code"),
        P("dp", None, None, "code"),
        P("dp", None, "code"),
        P("dp", None, "code"),
        P("dp", None, "code"),
        P("dp", "code"),
        P("dp", "code"),
        P("dp", "code"),
        P(),
        P(),
        P(),
        P("code", "dp"),
        P("code", "dp"),
        P("code", "dp"),
        P("code"),
    )
    return jax.shard_map(body, mesh=mesh, in_specs=in_specs, out_specs=out_specs, check_vma=False)
```

```python
import functools
import math

import jax
import jax.numpy as jnp
from jax import lax
from jax.experimental import pallas as pl
from jax.experimental.pallas import tpu as pltpu
from jax.sharding import PartitionSpec as P

GROUPS = 32
DEPTH = 4
BETA = 0.0625
EPSILON = 1e-05
MOMENTUM = 0.5
AVERAGE_DECAY = 0.5
COMMIT = 0.25
WEIGHT_RATE = 0.05
NORM_RATE = 0.5
CODE_RATE = 0.5

BF = jnp.bfloat16
F32 = jnp.float32
NT = (((1,), (1,)), ((), ()))
NN = (((1,), (0,)), ((), ()))
TN = (((0,), (0,)), ((), ()))
MIB = 1 << 20
LIMIT = 62 * MIB
SMALL_COST = pl.CostEstimate(flops=1 << 20, bytes_accessed=1 << 16, transcendentals=0)


def mm(a, b, dims=NN):
    return lax.dot_general(a, b, dims, preferred_element_type=F32)


def vmem():
    return pl.BlockSpec(memory_space=pltpu.VMEM)


def smem():
    return pl.BlockSpec(memory_space=pltpu.SMEM)


def anywhere():
    return pl.BlockSpec(memory_space=pl.ANY)


def hbm():
    return pl.BlockSpec(memory_space=pltpu.HBM)


def group_sum(rows, per_group):
    lanes = rows.shape[1]
    at = lax.broadcasted_iota(jnp.int32, rows.shape, 1)
    step = 1
    while step < per_group:
        up = pltpu.roll(rows, step, 1)
        down = pltpu.roll(rows, lanes - step, 1)
        rows = rows + jnp.where((at & step) != 0, up, down)
        step *= 2
    return rows


def col_sum(values):
    rows, lanes = values.shape
    return jnp.sum(jnp.sum(values.reshape(rows // 8, 8, lanes), axis=0), axis=0, keepdims=True)


def put_shifted(pad_ref, crop, lanes, values, side):
    pixels = values.shape[0]
    col = lax.broadcasted_iota(jnp.int32, values.shape, 0) % side
    left = jnp.where(col == 0, 0.0, pltpu.roll(values, 1, 0))
    right = jnp.where(col == side - 1, 0.0, pltpu.roll(values, pixels - 1, 0))
    for shift, grid in enumerate((left, values, right)):
        pad_ref[crop, shift, side : side + pixels, lanes] = grid.astype(BF)


def zero_borders(pad_ref, side):
    rows = pad_ref.shape[2]
    edge = jnp.zeros((side, pad_ref.shape[3]), BF)
    for crop in range(pad_ref.shape[0]):
        for shift in range(3):
            pad_ref[crop, shift, 0:side, :] = edge
            pad_ref[crop, shift, rows - side : rows, :] = edge


def pixel_order(pixels, side):
    half = side // 2
    lat = half * half
    row = lax.broadcasted_iota(jnp.int32, (pixels, pixels), 0)
    col = lax.broadcasted_iota(jnp.int32, (pixels, pixels), 1)
    tap, pos = row // lat, row % lat
    at = (2 * (pos // half) + tap // 2) * side + 2 * (pos % half) + tap % 2
    return jnp.where(at == col, 1.0, 0.0).astype(BF)


def chunks(channels):
    return [slice(k, k + 128) for k in range(0, channels, 128)]


def norm_stats(read, crops, pixels, channels, per_group):
    count = float(pixels * per_group)
    result = []
    sums = [
        jnp.concatenate([col_sum(read(c, k)) for k in chunks(channels)], axis=1)
        for c in range(crops)
    ]
    means = [group_sum(s, per_group) * (1.0 / count) for s in sums]
    for c in range(crops):
        parts = []
        for k in chunks(channels):
            d = read(c, k) - means[c][:, k]
            parts.append(col_sum(d * d))
        spread = group_sum(jnp.concatenate(parts, axis=1), per_group) * (1.0 / count)
        result.append((means[c], lax.rsqrt(spread + EPSILON)))
    return result


def conv_apply(pad_ref, crop, w_ref, side, pixels):
    total = None
    for b in range(3):
        rows = jnp.concatenate(
            [pad_ref[crop, b, side * a : side * a + pixels, :] for a in range(3)], axis=1
        )
        part = None
        weight = jnp.concatenate([w_ref[3 * a + b] for a in range(3)], axis=0)
        part = mm(rows, weight)
        total = part if total is None else total + part
    return total


def forward_kernel(
    side,
    x_ref,
    norm_ref,
    w_hbm,
    dn_hbm,
    pj_ref,
    conv_hbm,
    stats_ref,
    save_hbm,
    lat_ref,
    w_ref,
    dn_ref,
    pad_ref,
    sum_ref,
    conv_ref,
    sel_ref,
    sem,
):
    crops, pixels, channels = x_ref.shape
    per_group = channels // GROUPS
    lat = pixels // 4
    tokens = crops * lat
    copies = [pltpu.make_async_copy(w_hbm.at[k], w_ref.at[k], sem.at[k]) for k in range(2)]
    dn_copy = pltpu.make_async_copy(dn_hbm, dn_ref, sem.at[2])
    for copy in copies + [dn_copy]:
        copy.start()
    conv_save = pltpu.make_async_copy(conv_ref, conv_hbm, sem.at[3])
    zero_borders(pad_ref, side)
    for stage in range(2):
        if stage == 0:

            def read(c, k):
                return x_ref[c, :, k].astype(F32)

        else:

            def read(c, k):
                return conv_ref[c, :, k]

        stats = norm_stats(read, crops, pixels, channels, per_group)
        for c in range(crops):
            mean, inverse = stats[c]
            stats_ref[c, 2 * stage : 2 * stage + 1, :] = mean
            stats_ref[c, 2 * stage + 1 : 2 * stage + 2, :] = inverse
            for k in chunks(channels):
                normed = (read(c, k) - mean[:, k]) * inverse[:, k]
                out = normed * norm_ref[2 * stage : 2 * stage + 1, k]
                out = out + norm_ref[2 * stage + 1 : 2 * stage + 2, k]
                put_shifted(pad_ref, c, k, out * jax.nn.sigmoid(out), side)
        acts = [
            pltpu.make_async_copy(
                pad_ref.at[c, 1, pl.ds(side, pixels), :],
                save_hbm.at[pl.ds((stage * crops + c) * pixels, pixels), :],
                sem.at[4 + c],
            )
            for c in range(crops)
        ]
        for act in acts:
            act.start()
        copies[stage].wait()
        for c in range(crops):
            total = conv_apply(pad_ref, c, w_ref.at[stage], side, pixels)
            if stage == 0:
                conv_ref[c] = total
            else:
                sum_ref[c] = (x_ref[c].astype(F32) + total).astype(BF)
        for act in acts:
            act.wait()
        if stage == 0:
            conv_save.start()
    order = pixel_order(pixels, side)
    for c in range(crops):
        picked = mm(order, sum_ref[c]).astype(BF)
        for tap in range(4):
            at = tap * tokens + c * lat
            sel_ref[at : at + lat, :] = picked[tap * lat : (tap + 1) * lat]
    dn_copy.wait()
    reduced = mm(sel_ref[0:tokens], dn_ref[0])
    for tap in range(1, 4):
        reduced = reduced + mm(sel_ref[tap * tokens : (tap + 1) * tokens], dn_ref[tap])
    reduced = reduced.astype(BF)
    sel_ref[4 * tokens : 5 * tokens, :] = reduced
    sel_save = pltpu.make_async_copy(
        sel_ref, save_hbm.at[pl.ds(2 * crops * pixels, 5 * tokens), :], sem.at[4 + crops]
    )
    sel_save.start()
    lat_ref[...] = mm(reduced, pj_ref[...]).astype(BF)
    conv_save.wait()
    sel_save.wait()


def forward_call(x, norm, w, dn, pj, side):
    crops, pixels, channels = x.shape
    tokens = crops * pixels // 4
    return pl.pallas_call(
        functools.partial(forward_kernel, side),
        out_shape=[
            jax.ShapeDtypeStruct((crops, pixels, channels), F32),
            jax.ShapeDtypeStruct((crops, 8, channels), F32),
            jax.ShapeDtypeStruct((2 * crops * pixels + 5 * tokens, channels), BF),
            jax.ShapeDtypeStruct((tokens, pj.shape[1]), BF),
        ],
        in_specs=[vmem(), vmem(), hbm(), hbm(), vmem()],
        out_specs=[hbm(), vmem(), hbm(), vmem()],
        scratch_shapes=[
            pltpu.VMEM(w.shape, BF),
            pltpu.VMEM(dn.shape, BF),
            pltpu.VMEM((crops, 3, pixels + 2 * side, channels), BF),
            pltpu.VMEM((crops, pixels, channels), BF),
            pltpu.VMEM((crops, pixels, channels), F32),
            pltpu.VMEM((5 * tokens, channels), BF),
            pltpu.SemaphoreType.DMA((5 + crops,)),
        ],
        compiler_params=pltpu.CompilerParams(vmem_limit_bytes=LIMIT),
        cost_estimate=SMALL_COST,
        name="residual_forward",
    )(x, norm, w, dn, pj)


TILE = 1024
SUB = 1024
SPAN = 4096


def quant_kernel(n_shard, halves, n_piece, place_ref, lat_ref, weight_ref, cot_ref, pick_ref, *rest):
    shard_hbm = rest[:n_piece]
    n_out = 6 if halves else 5
    q_ref, g_ref, rows_ref, extra_ref = rest[n_piece : n_piece + 4]
    grad_hbm = rest[n_piece + 4 : n_piece + n_out]
    (
        code_ref,
        codet_ref,
        score_ref,
        stack_ref,
        res_ref,
        q_level_ref,
        fac_ref,
        side_ref,
        acc_ref,
        count_ref,
        norms_ref,
        carry_ref,
        stage_ref,
        more_ref,
        in_sem,
        out_sem,
        more_sem,
    ) = rest[n_piece + n_out :]
    tokens, width = lat_ref.shape
    codes = code_ref.shape[0]
    shard = codes // n_shard
    part = codes // 2
    tile = min(TILE, part)

    if halves:
        quarter = shard // 4
        corner = (place_ref[0] & 1) * 2 + ((place_ref[0] >> 1) & 1)
        starts = [0, shard]
        for base in (2 * shard, 3 * shard):
            starts += [base + (corner ^ k) * quarter for k in (0, 2, 1, 3)]
    else:
        starts = [k * shard for k in range(n_shard)]
    copies = [
        pltpu.make_async_copy(
            shard_hbm[k],
            code_ref.at[pl.ds(pl.multiple_of(starts[k], 256), shard_hbm[k].shape[0]), :],
            in_sem.at[k],
        )
        for k in range(n_piece)
    ]
    for copy in copies:
        copy.start()

    def fold(values, combine):
        out = values[:, :128]
        for k in range(128, values.shape[1], 128):
            out = combine(out, values[:, k : k + 128])
        return out

    def level_forward(level, first):
        residual = res_ref[level]
        low = residual.astype(BF)
        rows_ref[level] = low
        scaled = low * jnp.asarray(2.0 * BETA, BF)
        at_row = pl.multiple_of(level * tokens, tokens)
        peaks, sums, picks = [], [], []
        for h in range(2):
            best = jnp.full((tokens, 128), -jnp.inf, F32)
            for k in range(part // tile):
                at = h * part + k * tile
                lanes = slice(at, at + tile)
                if first:
                    if halves:
                        if at % shard == 0:
                            group = at // shard
                            for piece in ([group] if group < 2 else range(4 * group - 6, 4 * group - 2)):
                                copies[piece].wait()
                    else:
                        if at % shard == 0:
                            copies[at // shard].wait()
                    for j in range(at, at + tile, 512):
                        turned = code_ref[j : j + 512, :].T
                        codet_ref[:, j : j + 512] = turned
                        wide = turned.astype(F32)
                        norms_ref[:, j : j + 512] = BETA * col_sum(wide * wide)
                s = mm(scaled, codet_ref[:, lanes]) - norms_ref[:, lanes]
                score_ref[:, k * tile : (k + 1) * tile] = s
                best = jnp.maximum(best, fold(s, jnp.maximum))
            peak = jnp.max(best, axis=1, keepdims=True)
            acc_ref[h] = jnp.zeros((tokens, width), F32)

            def power(i, total):
                for k in range(SPAN // tile):
                    at = pl.multiple_of(i * SPAN + k * tile, tile)
                    lanes = pl.ds(pl.multiple_of(h * part + at, tile), tile)
                    p = jnp.exp(score_ref[:, pl.ds(at, tile)] - peak)
                    low_p = p.astype(BF)
                    stack_ref[pl.ds(at_row, tokens), lanes] = low_p
                    acc_ref[h] += mm(low_p, code_ref[lanes, :])
                    total = total + fold(p, jnp.add)
                return total

            total = lax.fori_loop(0, part // SPAN, power, jnp.zeros((tokens, 128), F32))
            peaks.append(peak)
            sums.append(jnp.sum(total, axis=1, keepdims=True))
        top = jnp.maximum(peaks[0], peaks[1])
        scales = [jnp.exp(peak - top) for peak in peaks]
        inverse = 1.0 / (sums[0] * scales[0] + sums[1] * scales[1])
        factors = [scale * inverse for scale in scales]
        for h in range(2):
            fac_ref[level, h] = jnp.broadcast_to(factors[h], (tokens, 128))
        picked = acc_ref[0] * factors[0] + acc_ref[1] * factors[1]
        q_level_ref[level] = picked
        res_ref[level + 1] = residual - picked

    res_ref[0] = lat_ref[...].astype(F32)
    level_forward(0, True)

    def later(level, nothing):
        level_forward(level, False)
        return nothing

    lax.fori_loop(1, DEPTH, later, 0)
    q_ref[...] = (q_level_ref[0] + q_level_ref[1]) + (q_level_ref[2] + q_level_ref[3])

    n_crop = weight_ref.shape[0]
    weight = jnp.concatenate(
        [jnp.full((tokens // n_crop, 1), weight_ref[c], F32) for c in range(n_crop)], axis=0
    )
    count_ref[...] = jnp.zeros(count_ref.shape, F32)
    carry_ref[...] = 2.0 * COMMIT * weight * res_ref[DEPTH]

    def level_back(step, nothing):
        level = DEPTH - 1 - step
        carry = carry_ref[...]
        grad = cot_ref[...].astype(F32) - carry
        dot = jnp.sum(grad * q_level_ref[level], axis=1, keepdims=True)
        ex_row = pl.multiple_of(level * tokens, tokens)
        in_row = pl.multiple_of((DEPTH + level) * tokens, tokens)
        turned_rows = grad_t(rows_ref[level])
        for h in range(2):
            factor = fac_ref[level, h][:, 0:1]
            down = (grad * factor).astype(BF)
            small = down * jnp.asarray(2.0 * BETA, BF)
            total_grad = dot * factor * (-2.0 * BETA)
            share = weight * factor
            side_ref[h, :, pl.ds(ex_row, tokens)] = grad_t(down)
            side_ref[h, :, pl.ds(in_row, tokens)] = turned_rows
            for k in range(part // tile):
                lanes = slice(h * part + k * tile, h * part + (k + 1) * tile)
                p = stack_ref[pl.ds(ex_row, tokens), lanes].astype(F32)
                ds = (mm(small, codet_ref[:, lanes]) + total_grad) * p
                inner = ds.astype(BF)
                stack_ref[pl.ds(in_row, tokens), lanes] = inner
                value = mm(inner, code_ref[lanes, :])
                if h == 0 and k == 0:
                    acc_ref[0] = value
                else:
                    acc_ref[0] += value
                weighted = (p * share).reshape(tokens // 8, 8, tile)
                count_ref[0, :, lanes] += jnp.sum(weighted, axis=0)
                count_ref[1, :, lanes] += jnp.sum(ds.reshape(tokens // 8, 8, tile), axis=0)
        pull = jnp.where(level > 0, 2.0 * COMMIT, 0.0)
        carry_ref[...] = carry + acc_ref[0] + pull * weight * res_ref[level]
        return nothing

    lax.fori_loop(0, DEPTH, level_back, 0)
    g_ref[...] = carry_ref[...].astype(BF)
    extra_ref[0:1, :] = jnp.sum(count_ref[0], axis=0, keepdims=True)
    extra_ref[1:2, :] = jnp.sum(count_ref[1], axis=0, keepdims=True)

    place = place_ref[0]
    pending = []
    n_row = stage_ref.shape[1] if halves else 1
    block = width // n_row
    if halves:
        flat = jnp.concatenate([rows_ref[level] for level in range(DEPTH)], axis=0)
        source = mm(flat, pick_ref[...], TN).astype(BF)
        spans = source.shape[1] // 128
        for k in range(n_shard):
            lines = []
            for row in range(2):
                for at in range(k * shard, (k + 1) * shard, 128):
                    lines.append(extra_ref[row : row + 1, at : at + 128])
            lines = jnp.concatenate(lines, axis=0).astype(BF)
            for r in range(n_row):
                for span in range(spans):
                    more_ref[k, r ^ place, span * block : (span + 1) * block, :] = source[
                        r * block : (r + 1) * block, span * 128 : (span + 1) * 128
                    ]
                more_ref[k, r ^ place, spans * block :, :] = lines
            rows = more_ref.shape[2]
            target = grad_hbm[k % 2].at[k // 2, :, pl.ds(shard // 128 * block, rows), :]
            copy = pltpu.make_async_copy(more_ref.at[k], target, more_sem.at[k])
            copy.start()
            pending.append(copy)
    slots = [None, None]
    for k in range(n_shard):
        for j in range(shard // min(SUB, shard)):
            sub = min(SUB, shard)
            at = k * shard + j * sub
            slot = (at // sub) % 2
            value = mm(side_ref[at // part], stack_ref[:, at : at + sub]).astype(BF)
            if slots[slot] is not None:
                slots[slot].wait()
            if halves:
                for r in range(n_row):
                    for t in range(sub // 128):
                        stage_ref[slot, r ^ place, t * block : (t + 1) * block, :] = value[
                            r * block : (r + 1) * block, t * 128 : (t + 1) * 128
                        ]
                rows = sub // 128 * block
                target = grad_hbm[k % 2].at[k // 2, :, pl.ds(j * rows, rows), :]
            else:
                stage_ref[slot] = value
                target = grad_hbm[0].at[k, :, pl.ds(j * sub, sub)]
            slots[slot] = pltpu.make_async_copy(stage_ref.at[slot], target, out_sem.at[slot])
            slots[slot].start()
    for copy in slots + pending:
        copy.wait()


def grad_t(values):
    return values.astype(F32).T.astype(BF)


def quant_call(place, latent, weight, cot, pick, pieces, halves, n_shard, n_row):
    tokens, width = latent.shape
    codes = sum(piece.shape[0] for piece in pieces)
    shard = codes // n_shard
    n_piece = len(pieces)
    sub = min(SUB, shard)
    block = width // n_row
    more = (n_shard, n_row, pick.shape[1] // 128 * block + 2 * shard // 128, 128)
    if halves:
        rows = shard // 128 * block + more[2]
        grads = [jax.ShapeDtypeStruct((n_shard // 2, n_row, rows, 128), BF)] * 2
        stage = (2, n_row, sub // 128 * block, 128)
    else:
        grads = [jax.ShapeDtypeStruct((n_shard, width, shard), BF)]
        stage = (2, width, sub)
        more = (1, 1, 16, 128)
    outs = [
        jax.ShapeDtypeStruct((tokens, width), F32),
        jax.ShapeDtypeStruct((tokens, width), BF),
        jax.ShapeDtypeStruct((DEPTH, tokens, width), BF),
        jax.ShapeDtypeStruct((2, codes), F32),
    ] + grads
    return pl.pallas_call(
        functools.partial(quant_kernel, n_shard, halves, n_piece),
        out_shape=outs,
        in_specs=[smem(), vmem(), smem(), vmem(), vmem()] + [hbm()] * n_piece,
        out_specs=[vmem()] * 4 + [hbm()] * len(grads),
        scratch_shapes=[
            pltpu.VMEM((codes, width), BF),
            pltpu.VMEM((width, codes), BF),
            pltpu.VMEM((tokens, codes // 2), F32),
            pltpu.VMEM((2 * DEPTH * tokens, codes), BF),
            pltpu.VMEM((DEPTH + 1, tokens, width), F32),
            pltpu.VMEM((DEPTH, tokens, width), F32),
            pltpu.VMEM((DEPTH, 2, tokens, 128), F32),
            pltpu.VMEM((2, width, 2 * DEPTH * tokens), BF),
            pltpu.VMEM((2, tokens, width), F32),
            pltpu.VMEM((2, 8, codes), F32),
            pltpu.VMEM((1, codes), F32),
            pltpu.VMEM((tokens, width), F32),
            pltpu.VMEM(stage, BF),
            pltpu.VMEM(more, BF),
            pltpu.SemaphoreType.DMA((n_piece,)),
            pltpu.SemaphoreType.DMA((2,)),
            pltpu.SemaphoreType.DMA((n_shard,)),
        ],
        compiler_params=pltpu.CompilerParams(vmem_limit_bytes=63 * MIB),
        cost_estimate=pl.CostEstimate(
            flops=48 * tokens * width * codes,
            bytes_accessed=18 * MIB,
            transcendentals=DEPTH * tokens * codes,
        ),
        name="soft_quantize",
    )(place, latent, weight, cot, pick, *pieces)


def slope(values):
    sigma = jax.nn.sigmoid(values)
    return sigma * (1.0 + values * (1.0 - sigma))


def norm_back(grad, normed, inverse, gain, per_group, count):
    dn = grad * gain
    first = group_sum(col_sum(dn), per_group) * (1.0 / count)
    second = group_sum(col_sum(dn * normed), per_group) * (1.0 / count)
    return inverse * (dn - first - normed * second)


def conv_back_image(pad_ref, crop, w_ref, side, pixels):
    total = None
    for tap in range(9):
        a, b = tap // 3, tap % 3
        rows = pad_ref[crop, 2 - b, side * (2 - a) : side * (2 - a) + pixels, :]
        part = mm(rows, w_ref[tap], NT)
        total = part if total is None else total + part
    return total


def act_back(read, dact_ref, stats_ref, norm_ref, stage, crops, pixels, channels, grads_ref, store):
    per_group = channels // GROUPS
    count = float(pixels * per_group)
    for k in chunks(channels):
        gain_row = norm_ref[2 * stage : 2 * stage + 1, k]
        bias_row = norm_ref[2 * stage + 1 : 2 * stage + 2, k]
        grad_gain = jnp.zeros((1, 128), F32)
        grad_bias = jnp.zeros((1, 128), F32)
        for c in range(crops):
            inverse = stats_ref[c, 2 * stage + 1 : 2 * stage + 2, k]
            normed = (read(c, k) - stats_ref[c, 2 * stage : 2 * stage + 1, k]) * inverse
            dout = dact_ref[c, :, k] * slope(normed * gain_row + bias_row)
            grad_gain = grad_gain + col_sum(dout * normed)
            grad_bias = grad_bias + col_sum(dout)
            store(c, k, norm_back(dout, normed, inverse, gain_row, per_group, count))
        grads_ref[0:1, k] = grad_gain
        grads_ref[1:2, k] = grad_bias


def second_kernel(
    side,
    dlat_ref,
    pj_ref,
    stats_ref,
    norm_ref,
    dn_hbm,
    conv_hbm,
    w_hbm,
    low_ref,
    dn_ref,
    conv_ref,
    w_ref,
    pad_ref,
    dact_ref,
    ngrad_ref,
    sem,
):
    crops, pixels, channels = conv_ref.shape
    lat = pixels // 4
    tokens, width = dlat_ref.shape
    pairs = ((dn_hbm, dn_ref), (w_hbm.at[1], w_ref), (conv_hbm, conv_ref))
    copies = [pltpu.make_async_copy(*pair, sem.at[k]) for k, pair in enumerate(pairs)]
    for copy in copies:
        copy.start()
    zero_borders(pad_ref, side)
    dlat = dlat_ref[...]
    dred = mm(dlat, pj_ref[...], NT).astype(BF)
    base = 2 * crops * pixels
    low_ref[base : base + tokens, :] = dred
    low_ref[base + tokens : base + 2 * tokens, 0:width] = dlat
    low_ref[base + tokens : base + 2 * tokens, width:] = jnp.zeros((tokens, channels - width), BF)
    order = pixel_order(pixels, side)
    copies[0].wait()
    pieces = [mm(dred, dn_ref[tap], NT).astype(BF) for tap in range(4)]
    for c in range(crops):
        mixed = jnp.concatenate([p[c * lat : (c + 1) * lat] for p in pieces], axis=0)
        low_ref[c * pixels : (c + 1) * pixels, :] = mm(order, mixed, TN).astype(BF)
        for k in chunks(channels):
            rows = low_ref[c * pixels : (c + 1) * pixels, k].astype(F32)
            put_shifted(pad_ref, c, k, rows, side)
    for copy in copies[1:]:
        copy.wait()
    for c in range(crops):
        dact_ref[c] = conv_back_image(pad_ref, c, w_ref, side, pixels)

    def read(c, k):
        return conv_ref[c, :, k]

    def store(c, k, value):
        at = (crops + c) * pixels
        low_ref[at : at + pixels, k] = value.astype(BF)

    act_back(read, dact_ref, stats_ref, norm_ref, 1, crops, pixels, channels, ngrad_ref, store)
    ngrad_ref[2:8, :] = jnp.zeros((6, channels), F32)
    lines = jnp.concatenate([ngrad_ref[...], jnp.zeros((8, channels), F32)], axis=0)
    low_ref[base + 2 * tokens : base + 2 * tokens + 16, :] = lines.astype(BF)


def second_call(dlat, pj, stats, norm, dn, conv, w, side):
    crops, pixels, channels = conv.shape
    tokens = dlat.shape[0]
    return pl.pallas_call(
        functools.partial(second_kernel, side),
        out_shape=jax.ShapeDtypeStruct((2 * crops * pixels + 2 * tokens + 16, channels), BF),
        in_specs=[vmem()] * 4 + [hbm()] * 3,
        out_specs=vmem(),
        scratch_shapes=[
            pltpu.VMEM(dn.shape, BF),
            pltpu.VMEM(conv.shape, F32),
            pltpu.VMEM(w.shape[1:], BF),
            pltpu.VMEM((crops, 3, pixels + 2 * side, channels), BF),
            pltpu.VMEM(conv.shape, F32),
            pltpu.VMEM((8, channels), F32),
            pltpu.SemaphoreType.DMA((3,)),
        ],
        compiler_params=pltpu.CompilerParams(vmem_limit_bytes=LIMIT),
        cost_estimate=SMALL_COST,
        name="second_backward",
    )(dlat, pj, stats, norm, dn, conv, w)


def first_kernel(
    side, n_part, place_ref, x_ref, stats_ref, norm_ref, low_ref, w_hbm, image_out, ngrad_ref, *scratch
):
    w_ref, pad_ref, dact_ref, image_ref, sem = scratch
    crops, pixels, channels = x_ref.shape
    copy = pltpu.make_async_copy(w_hbm.at[0], w_ref, sem.at[0])
    copy.start()
    zero_borders(pad_ref, side)

    def read(c, k):
        return x_ref[c, :, k].astype(F32)

    def store(c, k, value):
        rows = low_ref[c * pixels : (c + 1) * pixels, k].astype(F32)
        image_ref[c, :, k] = (value + rows).astype(BF)

    for c in range(crops):
        at = (crops + c) * pixels
        for k in chunks(channels):
            put_shifted(pad_ref, c, k, low_ref[at : at + pixels, k].astype(F32), side)
    copy.wait()
    for c in range(crops):
        dact_ref[c] = conv_back_image(pad_ref, c, w_ref, side, pixels)
    act_back(read, dact_ref, stats_ref, norm_ref, 0, crops, pixels, channels, ngrad_ref, store)
    ngrad_ref[2:8, :] = jnp.zeros((6, channels), F32)
    if n_part == 1:
        image_out[...] = image_ref[...]
        return
    span = pixels // n_part
    row = 0
    for k in range(n_part):
        at = pl.multiple_of((place_ref[0] ^ k) * span, span)
        for c in range(crops):
            for lanes in chunks(channels):
                image_out[row : row + span, :] = image_ref[c, pl.ds(at, span), lanes]
                row += span


def first_call(place, x, stats, norm, low, w, side, n_part):
    crops, pixels, channels = x.shape
    shape = (crops, pixels, channels) if n_part == 1 else (x.size // 128, 128)
    return pl.pallas_call(
        functools.partial(first_kernel, side, n_part),
        out_shape=[
            jax.ShapeDtypeStruct(shape, BF),
            jax.ShapeDtypeStruct((8, channels), F32),
        ],
        in_specs=[smem()] + [vmem()] * 4 + [hbm()],
        out_specs=[vmem()] * 2,
        scratch_shapes=[
            pltpu.VMEM(w.shape[1:], BF),
            pltpu.VMEM((crops, 3, pixels + 2 * side, channels), BF),
            pltpu.VMEM(x.shape, F32),
            pltpu.VMEM(x.shape, BF),
            pltpu.SemaphoreType.DMA((1,)),
        ],
        compiler_params=pltpu.CompilerParams(vmem_limit_bytes=LIMIT),
        cost_estimate=SMALL_COST,
        name="first_backward",
    )(place, x, stats, norm, low, w)


class Image:
    def __init__(self, array, count):
        self.rows = array.shape[0] // count
        self.chunks = {(0, k): (array, k * self.rows) for k in range(count)}
        self.order = list(IMAGE_PLAN)

    def leaving(self):
        bit = LINKS[self.order[0]][1]
        return sorted(key for key in self.chunks if key[1] & bit)

    def arrive(self, array, base):
        bit = LINKS[self.order[0]][1]
        for k, key in enumerate(self.leaving()):
            del self.chunks[key]
            self.chunks[key[0] ^ bit, key[1] & ~bit] = (array, base + k * self.rows)
        self.order.pop(0)


def image_kernel(rows, jobs, n_in, place_ref, *refs):
    ins, (out_ref, chunk_ref, sem) = refs[:n_in], refs[n_in:]
    loads = [
        pltpu.make_async_copy(ins[k].at[pl.ds(row, rows), :], chunk_ref.at[source], sem.at[source])
        for source, k, row in jobs
    ]
    for load in loads:
        load.start()
    for load in loads:
        load.wait()
    span, channels = out_ref.shape[1:]
    crops = out_ref.shape[0] // len(jobs)
    for source in range(len(jobs)):
        row = 0
        for c in range(crops):
            for lanes in chunks(channels):
                value = chunk_ref[source, row : row + span, :].astype(F32)
                out_ref[(place_ref[0] ^ source) * crops + c, :, lanes] = value
                row += span


def image_call(place, image, shape):
    arrays, jobs = [], []
    for (source, _), (array, row) in sorted(image.chunks.items(), key=lambda item: item[0]):
        jobs.append((source, operand_index(arrays, array), row))
    return pl.pallas_call(
        functools.partial(image_kernel, image.rows, jobs, len(arrays)),
        out_shape=jax.ShapeDtypeStruct(shape, F32),
        in_specs=[smem()] + [anywhere()] * len(arrays),
        out_specs=vmem(),
        scratch_shapes=[
            pltpu.VMEM((len(jobs), image.rows, 128), BF),
            pltpu.SemaphoreType.DMA((len(jobs),)),
        ],
        compiler_params=pltpu.CompilerParams(vmem_limit_bytes=LIMIT),
        cost_estimate=SMALL_COST,
        name="image_assembly",
    )(place, *arrays)


BLOCK = 64
TAIL = 48


def matrix_kernel(side, crops, pixels, width, plan, n_set, place_ref, *refs):
    sources, refs = refs[: 3 * n_set], refs[3 * n_set :]
    n_out = 2 * len(plan) if plan else 1
    targets, refs = refs[:n_out], refs[n_out:]
    saves, refs = refs[:n_set], refs[n_set:]
    lows, refs = refs[:n_set], refs[n_set:]
    norms, refs = refs[:n_set], refs[n_set:]
    outs, (pad_ref, in_sem, out_sem) = refs[:n_out], refs[n_out:]
    channels = pad_ref.shape[3]
    locals_ = list(saves) + list(lows) + list(norms)
    image = crops * pixels
    loads = []
    for save_at, low_at in ((image, 0), (2 * image, 2 * image), (0, image)):
        group = []
        for k in range(2 * n_set):
            at = save_at if k < n_set else low_at
            count = image if at < 2 * image else sources[k].shape[0] - 2 * image
            rows = pl.ds(at, count)
            group.append(
                pltpu.make_async_copy(
                    sources[k].at[rows, :], locals_[k].at[rows, :], in_sem.at[len(loads), k]
                )
            )
        loads.append(group)
    for k in range(2 * n_set, 3 * n_set):
        loads[1].append(pltpu.make_async_copy(sources[k], locals_[k], in_sem.at[1, k]))
    for group in loads:
        for load in group:
            load.start()
    stores = [
        pltpu.make_async_copy(outs[k], targets[k].at[pl.ds(0, outs[k].shape[0])], out_sem.at[k])
        for k in range(n_out)
    ]
    done = {}
    tokens = crops * pixels // 4
    odd = place_ref[1] % 2 == 1
    line = place_ref[1] // 2 % 2
    dp = place_ref[0]
    zero_borders(pad_ref, side)

    def arrive(group):
        for load in loads[group]:
            load.wait()

    def half(values):
        if not plan:
            return values
        parts = []
        for k in range(0, values.shape[1], 256):
            parts.append(jnp.where(odd, values[:, k + 128 : k + 256], values[:, k : k + 128]))
        return jnp.concatenate(parts, axis=1)

    def low_rows(at, count):
        return jnp.concatenate([half(low[at : at + count, :]) for low in lows], axis=0)

    def squeeze(index, bit):
        return (index >> (bit + 1) << bit) | (index & ((1 << bit) - 1))

    def place_rows(part, row, count, value):
        keep_ref, send_ref = outs[2 * part], outs[2 * part + 1]
        rows = keep_ref.shape[1]
        name = plan[part][1].split()[0]

        def put(lead, keep, send):
            keep_ref[lead, row : row + count, :] = keep
            send_ref[pl.ds(pl.multiple_of(lead * rows + row, 16), count), :] = send

        if name == "x":
            far = line == 1
            keep = jnp.where(far, value[:, 128:], value[:, :128])
            send = jnp.where(far, value[:, :128], value[:, 128:])
            for i in range(8):
                at = slice(i * count, (i + 1) * count)
                put(i ^ dp, keep[at], send[at])
            return
        bit = {"y": 0, "z1": 1, "z2": 2}[name]
        other = (dp >> bit) & 1 == 1
        for pair in range(2):
            lead = (pair ^ line) * 4
            for i in range(8):
                if i >> bit & 1:
                    continue
                j = i | 1 << bit
                lanes = slice(pair * 128, pair * 128 + 128)
                first = value[i * count : (i + 1) * count, lanes]
                second = value[j * count : (j + 1) * count, lanes]
                put(
                    lead + (squeeze(i, bit) ^ squeeze(dp, bit)),
                    jnp.where(other, second, first),
                    jnp.where(other, first, second),
                )

    def store(block, value):
        value = value.astype(BF)
        if not plan:
            outs[0][block * channels : (block + 1) * channels, 0 : value.shape[1]] = value
            return
        part = 0
        while block >= plan[part][0] // 4:
            block -= plan[part][0] // 4
            part += 1
        place_rows(part, block * BLOCK, BLOCK, value)
        done[part] = done.get(part, 0) + 4
        if done[part] == plan[part][0]:
            stores[2 * part].start()
            stores[2 * part + 1].start()

    def taps(save_at, low_at, first_block):
        for n, save in enumerate(saves):
            for c in range(crops):
                for k in chunks(channels):
                    rows = save[save_at + c * pixels : save_at + (c + 1) * pixels, k]
                    put_shifted(pad_ref, n * crops + c, k, rows.astype(F32), side)
        grad = low_rows(low_at, crops * pixels).T
        for tap in range(9):
            a, b = tap // 3, tap % 3
            rows = [
                pad_ref[c, b, side * a : side * a + pixels, :] for c in range(n_set * crops)
            ]
            store(first_block + tap, mm(grad, jnp.concatenate(rows, axis=0)).astype(BF).T)

    arrive(0)
    taps(crops * pixels, 0, 0)
    arrive(1)
    base = 2 * crops * pixels
    dred = low_rows(base, tokens).T
    for tap in range(4):
        at = base + tap * tokens
        rows = jnp.concatenate([save[at : at + tokens, :] for save in saves], axis=0)
        store(9 + tap, mm(dred, rows).astype(BF).T)
    arrive(2)
    taps(0, crops * pixels, 13)
    at = base + 4 * tokens
    rows = jnp.concatenate([save[at : at + tokens, :] for save in saves], axis=0)
    dlat = [low[base + tokens : base + 2 * tokens, 0:width] for low in lows]
    if not plan:
        store(22, mm(rows, dlat[0], TN))
        stores[0].start()
        stores[0].wait()
        return
    narrow = []
    for part in dlat:
        pieces = [part[:, k : k + 64] for k in range(0, width, 64)]
        narrow.append(
            jnp.concatenate(
                [
                    jnp.where(odd, pieces[1], pieces[0]),
                    jnp.where(odd, pieces[3], pieces[2]),
                ],
                axis=1,
            )
        )
    proj = mm(rows, jnp.concatenate(narrow, axis=0), TN).astype(BF)
    lines = []
    first = norms[0][0:2, :] + norms[1][0:2, :]
    at = base + 2 * tokens
    second = lows[0][at : at + 16, :].astype(F32) + lows[1][at : at + 16, :].astype(F32)
    for rows in (first, second[0:2]):
        for k in range(2):
            lines += [rows[k : k + 1, lanes] for lanes in chunks(channels)]
    lines = jnp.concatenate(lines, axis=0).astype(BF)
    folded = []
    for i in range(8):
        top = proj[i * 64 : i * 64 + 32]
        low = proj[i * 64 + 32 : (i + 1) * 64]
        block = jnp.concatenate([top[:, 0:64], low[:, 0:64], top[:, 64:], low[:, 64:]], axis=1)
        folded.append(
            jnp.concatenate([block, jnp.concatenate([lines, lines], axis=1)], axis=0)
        )
    last = len(plan) - 1
    place_rows(last, outs[2 * last].shape[1] - TAIL, TAIL, jnp.concatenate(folded, axis=0))
    stores[2 * last].start()
    stores[2 * last + 1].start()
    for store_ in stores:
        store_.wait()


def matrix_call(place, saves, lows, norms, side, crops, pixels, width, plan, room=None):
    channels = saves[0].shape[1]
    n_set = len(saves)
    if plan:
        outs, shapes = [], []
        for units, order in plan:
            rows = 8 * 16 * units
            shapes += [(8, 16 * units, 128), (rows, 128)]
            outs.append(jax.ShapeDtypeStruct(shapes[-2], BF))
            outs.append(jax.ShapeDtypeStruct((rows + room.get(order.split()[0], 0), 128), BF))
    else:
        outs = [jax.ShapeDtypeStruct((23 * channels, channels), BF)]
        shapes = [outs[0].shape]
    return pl.pallas_call(
        functools.partial(matrix_kernel, side, crops, pixels, width, plan, n_set),
        out_shape=outs,
        in_specs=[smem()] + [hbm()] * (3 * n_set),
        out_specs=[hbm()] * len(outs),
        scratch_shapes=[pltpu.VMEM(a.shape, a.dtype) for a in (*saves, *lows, *norms)]
        + [pltpu.VMEM(shape, BF) for shape in shapes]
        + [
            pltpu.VMEM((n_set * crops, 3, pixels + 2 * side, channels), BF),
            pltpu.SemaphoreType.DMA((3, 3 * n_set)),
            pltpu.SemaphoreType.DMA((len(outs),)),
        ],
        compiler_params=pltpu.CompilerParams(vmem_limit_bytes=LIMIT),
        cost_estimate=SMALL_COST,
        name="matrix_backward",
    )(place, *saves, *lows, *norms)


def swap(array, axis, bit):
    count = lax.axis_size(axis)
    return lax.ppermute(array, axis, [(i, i ^ bit) for i in range(count)])


def add_low(first, second):
    return (first.astype(F32) + second.astype(F32)).astype(BF)


LINKS = {"x": ("code", 2), "y": ("dp", 1), "z1": ("dp", 2), "z2": ("dp", 4)}
BITS = ("x", "z2", "z1", "y")
CODE_PLAN = ((36, "z1 y x z2"), (36, "y x z2 z1"))
MATRIX_PLAN = ((28, "x z1 y z2"), (28, "y x z2 z1"), (35, "z1 y x z2"))
IMAGE_PLAN = ("z2", "y", "z1")


class Part:
    def __init__(self, array, low, rows, order, arrival):
        self.array, self.low, self.rows = array, low, rows
        self.order, self.dims = order.split(), list(BITS)
        self.arrival, self.offset = arrival, None


def split_parts(keep, arrival, plan):
    shape = (keep.shape[0] * keep.shape[1],) + keep.shape[2:]
    keep, arrival = keep.reshape(shape), arrival.reshape(shape)
    assert 16 * sum(units for units, _ in plan) == shape[1]
    parts, low = [], 0
    for units, order in plan:
        parts.append(Part(keep, low, 16 * units, order, arrival))
        low += 16 * units
    return parts


def merge_kernel(jobs, moves, n_in, n_out, *refs):
    ins, outs, scratch = refs[:n_in], refs[n_in : n_in + n_out], refs[n_in + n_out :]
    sem = scratch[-1]
    loads, stores = [], []
    passing = []
    for k, (source, row, target, place, rows) in enumerate(moves):
        held = scratch[-2].at[k]
        at = 4 * len(jobs) + 2 * k
        load = pltpu.make_async_copy(ins[source].at[pl.ds(row, rows), :], held, sem.at[at])
        store = pltpu.make_async_copy(held, outs[target].at[pl.ds(place, rows), :], sem.at[at + 1])
        load.start()
        passing.append((load, store))
    for j, job in enumerate(jobs):
        mine, other = scratch[4 * j], scratch[4 * j + 1]
        source = ins[job["array"]].at[:, pl.ds(job["low"], job["rows"]), :]
        first = pltpu.make_async_copy(source, mine, sem.at[4 * j])
        if job["flat"] is None:
            source = ins[job["arrival"]].at[:, pl.ds(job["low"], job["rows"]), :]
        else:
            source = ins[job["arrival"]].at[pl.ds(job["flat"], other.shape[0]), :]
        second = pltpu.make_async_copy(source, other, sem.at[4 * j + 1])
        first.start()
        second.start()
        loads.append((first, second))
    for load, store in passing:
        load.wait()
        store.start()
        stores.append(store)
    for j, job in enumerate(jobs):
        mine, other, keep, send = scratch[4 * j : 4 * j + 4]
        for load in loads[j]:
            load.wait()
        rows, count = job["rows"], [0, 0]
        for lead in range(mine.shape[0]):
            at = slice(lead * rows, (lead + 1) * rows)
            value = add_low(mine[lead], other[lead] if job["flat"] is None else other[at, :])
            half = lead >> job["bit"] & 1
            if half == 0:
                keep[count[0]] = value
            else:
                send[count[1] * rows : (count[1] + 1) * rows, :] = value
            count[half] += 1
        target = outs[job["send"]].at[pl.ds(job["place"], send.shape[0]), :]
        for k, pair in enumerate(((keep, outs[job["keep"]]), (send, target))):
            copy = pltpu.make_async_copy(*pair, sem.at[4 * j + 2 + k])
            copy.start()
            stores.append(copy)
    for copy in stores:
        copy.wait()


def operand_index(arrays, array):
    for k, known in enumerate(arrays):
        if known is array:
            return k
    arrays.append(array)
    return len(arrays) - 1


def merge(parts, given=(), image=None):
    sizes, groups = {}, {}
    arrays, jobs, scratch = [], [], []
    for name, _, group in given:
        groups[name] = list(group)
        sizes[name] = sum(p.rows * 2 ** (len(p.dims) - 1) for p in group)
    links = {p.order[0] for p in parts}
    if image is not None:
        links.add(image.order[0])
    names = sorted(links)
    for k, part in enumerate(parts):
        lead = 2 ** len(part.dims)
        name = part.order[0]
        jobs.append(
            {
                "array": operand_index(arrays, part.array),
                "arrival": operand_index(arrays, part.arrival),
                "low": part.low,
                "rows": part.rows,
                "flat": part.offset,
                "keep": k,
                "bit": len(part.dims) - 1 - part.dims.index(name),
                "send": len(parts) + names.index(name),
                "place": sizes.get(name, 0),
            }
        )
        part.offset = sizes.get(name, 0)
        sizes[name] = part.offset + part.rows * lead // 2
        groups.setdefault(name, []).append(part)
        flat = jobs[-1]["flat"] is not None
        scratch += [
            pltpu.VMEM((lead, part.rows, 128), BF),
            pltpu.VMEM((lead * part.rows, 128) if flat else (lead, part.rows, 128), BF),
            pltpu.VMEM((lead // 2, part.rows, 128), BF),
            pltpu.VMEM((lead // 2 * part.rows, 128), BF),
        ]
    moves = []
    if image is not None:
        name = image.order[0]
        image.base = sizes.get(name, 0)
        for key in image.leaving():
            array, row = image.chunks[key]
            at = sizes.get(name, 0)
            moves.append(
                (operand_index(arrays, array), row, len(parts) + names.index(name), at, image.rows)
            )
            sizes[name] = at + image.rows
        groups.setdefault(name, []).append(image)
    outs = [jax.ShapeDtypeStruct((2 ** (len(p.dims) - 1), p.rows, 128), BF) for p in parts]
    outs += [jax.ShapeDtypeStruct((sizes[name], 128), BF) for name in names]
    aliases = {}
    for name, array, _ in given:
        if name in names:
            assert array.shape == (sizes[name], 128)
            aliases[len(arrays)] = len(parts) + names.index(name)
            arrays.append(array)
    result = pl.pallas_call(
        functools.partial(merge_kernel, jobs, moves, len(arrays), len(outs)),
        out_shape=outs,
        input_output_aliases=aliases,
        in_specs=[anywhere()] * len(arrays),
        out_specs=[anywhere()] * len(outs),
        scratch_shapes=scratch
        + [
            pltpu.VMEM((max(len(moves), 1), image.rows if image is not None else 16, 128), BF),
            pltpu.SemaphoreType.DMA((4 * len(parts) + 2 * len(moves),)),
        ],
        compiler_params=pltpu.CompilerParams(vmem_limit_bytes=LIMIT),
        cost_estimate=SMALL_COST,
        name="merge_parts",
    )(*arrays)
    for k, part in enumerate(parts):
        part.array, part.low, part.arrival = result[k], 0, None
    sends = [(name, result[len(parts) + k], groups[name]) for k, name in enumerate(names)]
    return sends + [entry for entry in given if entry[0] not in names]


def fly(sends):
    return [(name, swap(array, *LINKS[name]), group) for name, array, group in sends]


def land(flights, *others):
    tied = lax.optimization_barrier(tuple(array for _, array, _ in flights) + tuple(others))
    for (name, _, group), array in zip(flights, tied):
        for part in group:
            if isinstance(part, Image):
                part.arrive(array, part.base)
                continue
            part.order.pop(0)
            part.dims.remove(name)
            part.arrival = array
    return tied[len(flights) :]


def sum_parts(parts, ins, target):
    at = 0
    for part in parts:
        rows = part["rows"]
        value = ins[part["array"]][0].astype(F32)
        value = value + ins[part["arrival"]][part["offset"] : part["offset"] + rows, :].astype(F32)
        target[at : at + rows, :] = value
        at += rows


def matrix_update_kernel(parts, n_in, rates, *refs):
    n_all = n_in + 12
    sources, targets, refs = refs[:n_all], refs[n_all : n_all + 12], refs[n_all + 12 :]
    locals_, outs, refs = refs[:n_all], refs[n_all : n_all + 12], refs[n_all + 12 :]
    mat_ref, in_sem, out_sem = refs
    loads = [pltpu.make_async_copy(sources[k], locals_[k], in_sem.at[k]) for k in range(n_all)]
    for load in loads:
        load.start()
    stores = [pltpu.make_async_copy(outs[k], targets[k], out_sem.at[k]) for k in range(12)]
    conv_m, conv_v, conv_a, down_m, down_v, down_a, proj_m, proj_v, proj_a, *rest = locals_[n_in:]
    norm_m, norm_v, norm_a = rest
    for load in loads[:n_in]:
        load.wait()
    sum_parts(parts, locals_[:n_in], mat_ref)
    for load in loads[n_in:]:
        load.wait()

    def step(refs, index, grad, rate, results):
        master, moment, average = refs
        moment_new = MOMENTUM * moment[index] + grad
        master_new = master[index] - rate * (grad + MOMENTUM * moment_new)
        results[0][index] = moment_new
        results[1][index] = master_new
        results[2][index] = AVERAGE_DECAY * average[index] + (1.0 - AVERAGE_DECAY) * master_new

    weight_rate, norm_rate = rates
    block = conv_m.shape[0] // 18
    for conv in range(2):
        for tap in range(9):
            row = (13 + tap if conv == 0 else tap) * block
            index = (pl.ds(tap * 2 + conv, block, stride=18), slice(None))
            grad = mat_ref[row : row + block, :]
            step((conv_m, conv_v, conv_a), index, grad, weight_rate, outs[0:3])
    for store in stores[:3]:
        store.start()
    for tap in range(4):
        index = (pl.ds(tap, block, stride=4), slice(None))
        grad = mat_ref[(9 + tap) * block : (10 + tap) * block, :]
        step((down_m, down_v, down_a), index, grad, weight_rate, outs[3:6])
    tail = 22 * block
    for k in range(2):
        index = (slice(k * block // 2, (k + 1) * block // 2), slice(None))
        grad = mat_ref[tail : tail + block // 2, k * 64 : (k + 1) * 64]
        step((proj_m, proj_v, proj_a), index, grad, weight_rate, outs[6:9])
    tail += block // 2
    lines = norm_m.shape[1] // 128
    for k in range(4):
        for j in range(lines):
            index = (slice(k, k + 1), slice(j * 128, (j + 1) * 128))
            row = tail + k * lines + j
            step((norm_m, norm_v, norm_a), index, mat_ref[row : row + 1, :], norm_rate, outs[9:12])
    for store in stores[3:]:
        store.start()
    for store in stores:
        store.wait()


def code_update_kernel(parts, n_in, code_rate, mean_count, *refs):
    n_all = n_in + 6
    sources, targets, refs = refs[:n_all], refs[n_all : n_all + 4], refs[n_all + 4 :]
    locals_, outs, refs = refs[:n_all], refs[n_all : n_all + 4], refs[n_all + 4 :]
    code_ref, in_sem, out_sem = refs
    loads = [pltpu.make_async_copy(sources[k], locals_[k], in_sem.at[k]) for k in range(n_all)]
    for load in loads:
        load.start()
    stores = [pltpu.make_async_copy(outs[k], targets[k], out_sem.at[k]) for k in range(4)]
    code_m, code_v, code_a, own_ref, select_ref, chosen_ref = locals_[n_in:]
    for load in loads:
        load.wait()
    sum_parts(parts, locals_[:n_in], code_ref)
    cols, codes = code_m.shape
    tiles = codes // 128
    base = tiles * cols
    spans = select_ref.shape[0] // 128
    source = jnp.concatenate(
        [code_ref[base + k * cols : base + (k + 1) * cols, :] for k in range(spans)], axis=1
    ).astype(BF)
    base += spans * cols
    outs[3][...] = code_ref[base : base + tiles, :] * (1.0 / mean_count)
    wide = 512
    for k in range(codes // wide):
        lanes = slice(k * wide, (k + 1) * wide)
        four = range(k * wide // 128, (k + 1) * wide // 128)
        grad = jnp.concatenate([code_ref[t * cols : (t + 1) * cols, :] for t in four], axis=1)
        slope_sum = jnp.concatenate(
            [code_ref[base + tiles + t : base + tiles + t + 1, :] for t in four], axis=1
        )
        count = jnp.concatenate([code_ref[base + t : base + t + 1, :] for t in four], axis=1)
        grad = grad - own_ref[:, lanes].astype(F32) * slope_sum
        moment_new = MOMENTUM * code_v[:, lanes] + grad
        stepped = code_m[:, lanes] - code_rate * (grad + MOMENTUM * moment_new)
        renewed = mm(source, select_ref[:, lanes])
        share = chosen_ref[:, lanes] * (mean_count / (mean_count + count))
        master_new = stepped + share * (renewed - stepped)
        outs[0][:, lanes] = moment_new
        outs[1][:, lanes] = master_new
        outs[2][:, lanes] = AVERAGE_DECAY * code_a[:, lanes] + (1.0 - AVERAGE_DECAY) * master_new
    for store in stores:
        store.start()
    for store in stores:
        store.wait()


def update_call(kernel, name, parts, states, shapes, *settings):
    arrays, jobs = [], []
    for part in parts:
        jobs.append(
            {
                "array": operand_index(arrays, part.array),
                "arrival": operand_index(arrays, part.arrival),
                "offset": part.offset,
                "rows": part.rows,
            }
        )
    outs = [jax.ShapeDtypeStruct(shape, F32) for shape in shapes]
    args = arrays + list(states)
    return pl.pallas_call(
        functools.partial(kernel, jobs, len(arrays), *settings),
        out_shape=outs,
        in_specs=[hbm()] * len(args),
        out_specs=[hbm()] * len(outs),
        scratch_shapes=[pltpu.VMEM(a.shape, a.dtype) for a in args]
        + [pltpu.VMEM(out.shape, F32) for out in outs]
        + [
            pltpu.VMEM((sum(p.rows for p in parts), 128), F32),
            pltpu.SemaphoreType.DMA((len(args),)),
            pltpu.SemaphoreType.DMA((len(outs),)),
        ],
        compiler_params=pltpu.CompilerParams(vmem_limit_bytes=LIMIT),
        cost_estimate=SMALL_COST,
        name=name,
    )(*args)


def nesterov_step(master, moment, average, grad, rate):
    moment_new = MOMENTUM * moment + grad
    master_new = master - rate * (grad + MOMENTUM * moment_new)
    return (moment_new, master_new, AVERAGE_DECAY * average + (1.0 - AVERAGE_DECAY) * master_new)


def body(
    crops_in,
    crop_weight,
    cotangent,
    conv_copy,
    down_copy,
    proj_copy,
    norm_copy,
    codebook,
    conv_master,
    conv_moment,
    conv_average,
    down_master,
    down_moment,
    down_average,
    proj_master,
    proj_moment,
    proj_average,
    norm_master,
    norm_moment,
    norm_average,
    code_master,
    code_moment,
    code_average,
    repl_code,
    repl_src,
):
    dp_count = lax.axis_size("dp")
    code_count = lax.axis_size("code")
    dp_at = lax.axis_index("dp")
    code_at = lax.axis_index("code")
    halves = dp_count == 8 and code_count == 4
    place = jnp.stack([dp_at, code_at]).astype(jnp.int32)

    spread = (crops_in.shape[1] // dp_count, dp_count) + crops_in.shape[2:]
    local = lax.all_to_all(
        crops_in[0].reshape((dp_count, spread[0]) + spread[2:]), "dp", split_axis=0, concat_axis=0
    )
    crop_dev, pixels, channels = spread[0], dp_count * spread[2], spread[3]
    side = math.isqrt(pixels)
    lat = pixels // 4
    tokens = crop_dev * lat
    width = proj_copy.shape[1]
    code_dev = codebook.shape[0]
    codes_all = code_dev * code_count

    crops_set = crop_dev * dp_count
    flat_src = repl_src.reshape(-1)
    crop_id = flat_src // lat % crops_set
    owner = (crop_id // crop_dev == dp_at) & (flat_src // (crops_set * lat) == code_at)
    row_id = crop_id % crop_dev * lat + flat_src % lat
    depth_id = jnp.repeat(jnp.arange(DEPTH, dtype=jnp.int32), repl_src.shape[1])
    pick = (
        jnp.where(owner, depth_id * tokens + row_id, -1)[None, :]
        == jnp.arange(DEPTH * tokens, dtype=jnp.int32)[:, None]
    ).astype(BF)
    weight_col = crop_weight.astype(F32).reshape(crop_dev)
    dn = down_copy.transpose(1, 0, 2)
    gains = norm_copy.T.astype(F32)
    own_codes = lax.dynamic_slice_in_dim(codebook, dp_at * (width // dp_count), width // dp_count, 1).T
    select = (
        repl_code.reshape(-1)[:, None] - code_at * code_dev
        == jnp.arange(code_dev, dtype=jnp.int32)[None, :]
    )
    chosen = jnp.sum(select.astype(F32), axis=0)
    select = select.astype(BF)
    if halves:
        quarter = code_dev // 4
        corner = (dp_at & 1) * 2 + ((dp_at >> 1) & 1)
        mine = lax.dynamic_slice_in_dim(codebook, corner * quarter, quarter, 0)
        other = lax.dynamic_slice_in_dim(codebook, (corner ^ 3) * quarter, quarter, 0)
        core = swap(codebook, "code", 1)
        over_x = swap(mine, "code", 2)
        over_x, core, other, conv_copy, dn, gains, pick, weight_col, place = (
            lax.optimization_barrier(
                (over_x, core, other, conv_copy, dn, gains, pick, weight_col, place)
            )
        )
        over_y, over_z = swap(over_x, "dp", 1), swap(over_x, "dp", 2)
        last = swap(other, "code", 2)
        diag = [swap(over_x, "code", 1)]
        w = conv_copy.transpose(1, 2, 0, 3)
        over_y, over_z, last, local, w, diag[0] = lax.optimization_barrier(
            (over_y, over_z, last, local, w, diag[0])
        )
        diag = diag + [swap(piece, "code", 1) for piece in (over_y, over_z, last)]
    else:
        w = conv_copy.transpose(1, 2, 0, 3)
        every = lax.all_gather(codebook, "code", axis=0)
        pieces = [every[k] for k in range(code_count)]

    local = local.transpose(1, 0, 2, 3).reshape(crop_dev, pixels, channels)
    conv1, stats, save, latent = forward_call(local, gains, w, dn, proj_copy, side)
    if halves:
        pieces = [codebook, core, over_x, over_y, over_z, last] + diag
        saves = (save, swap(save, "code", 1))

    n_row = dp_count if halves else 1
    quantized, dlat, rows, extra, *code_grads = quant_call(
        place,
        latent,
        weight_col,
        cotangent.reshape(tokens, width),
        pick,
        pieces,
        halves,
        code_count,
        n_row,
    )
    pixels_all = crop_dev * pixels * dp_count * code_count
    weight_rate = WEIGHT_RATE / math.sqrt(pixels_all)
    norm_rate = NORM_RATE / math.sqrt(pixels_all)
    crops_all = crop_dev * dp_count * code_count
    mean_count = DEPTH * lat * crops_all / codes_all
    code_rate = CODE_RATE / math.sqrt(mean_count)
    low = second_call(dlat, proj_copy, stats, gains, dn, conv1, w, side)

    if halves:
        code_core = swap(code_grads[1], "code", 1)
        low_mate = swap(low, "code", 1)
        code_core, low, save_mate = lax.optimization_barrier((code_core, low, saves[1]))
        codes = split_parts(code_grads[0], code_core, CODE_PLAN)
        sends = merge(codes)
        tied = lax.optimization_barrier(tuple(array for _, array, _ in sends) + (low, low_mate))
        low, low_mate = tied[-2:]
        flights = fly([(name, tied[k], group) for k, (name, _, group) in enumerate(sends)])
        image, ngrad = first_call(place, local, stats, gains, low, w, side, dp_count)
        ngrad_mate = swap(ngrad, "code", 1)
        image = Image(image, dp_count)
        room = {}
        for part in codes:
            name = part.order[1]
            room[name] = room.get(name, 0) + part.rows * 2 ** (len(part.dims) - 2)
        results = matrix_call(
            place, (save, save_mate), (low, low_mate), (ngrad, ngrad_mate), side, crop_dev, pixels,
            width, MATRIX_PLAN, room,
        )
        mats, given = [], []
        results = land(flights, *results)
        for k, (units, order) in enumerate(MATRIX_PLAN):
            part = Part(results[2 * k], 0, 16 * units, order, None)
            part.offset = 0
            mats.append(part)
            given.append((part.order[0], results[2 * k + 1], [part]))
        own_codes, select, chosen = land(
            fly(merge(codes, given, image)), own_codes, select, chosen
        )
        parts = codes + mats
        for _ in range(3):
            active = [part for part in parts if part.order]
            land(fly(merge(active, image=image if image.order else None)))
        shape = (crop_dev * dp_count, pixels // dp_count, channels)
        input_back = image_call(place, image, shape)[None]

        def flat(array):
            return array.transpose(0, 2, 1, 3).reshape(-1, 128)

        states = [flat(array) for array in (conv_master, conv_moment, conv_average)]
        states += [a.reshape(-1, 128) for a in (down_master, down_moment, down_average)]
        states += [proj_master, proj_moment, proj_average]
        states += [a.T for a in (norm_master, norm_moment, norm_average)]
        out = update_call(
            matrix_update_kernel, "matrix_updates", mats, states, [a.shape for a in states],
            (weight_rate, norm_rate),
        )
        states = [a.T for a in (code_master, code_moment, code_average)]
        states += [own_codes, select, chosen[None, :]]
        shapes = [states[0].shape] * 3 + [(code_dev // 128, 128)]
        code_out = update_call(
            code_update_kernel, "code_updates", codes, states, shapes, code_rate, mean_count
        )
        rows_in = channels // dp_count
        conv_out = [
            a.reshape(rows_in, 9, 2, channels // code_count).transpose(0, 2, 1, 3) for a in out[0:3]
        ]
        return (
            quantized.reshape(1, crop_dev, lat, width),
            input_back,
            *conv_out,
            *[a.reshape(down_master.shape) for a in out[3:6]],
            *out[6:9],
            *[a.T for a in out[9:12]],
            *[a.T for a in code_out[:3]],
            code_out[3].reshape(code_dev),
        )

    image, ngrad = first_call(place, local, stats, gains, low, w, side, 1)
    (grads,) = matrix_call(
        place, (save,), (low,), (ngrad,), side, crop_dev, pixels, width, None
    )
    grads = grads.reshape(23, channels, channels)
    base = 2 * crop_dev * pixels + 2 * tokens
    norm_grad = jnp.concatenate([ngrad[0:2], low[base : base + 2].astype(F32)], axis=0)
    flat = lax.psum_scatter(code_grads[0], "code", scatter_dimension=0, tiled=True)[0]
    code_grad = lax.psum_scatter(flat, "dp", scatter_dimension=0, tiled=True).astype(F32)
    sums = lax.psum_scatter(extra, "code", scatter_dimension=1, tiled=True)
    sums = lax.psum(sums, "dp")
    source = mm(rows.reshape(DEPTH * tokens, width), pick, TN).astype(BF)
    source_rows = lax.psum_scatter(source, "dp", scatter_dimension=0, tiled=True)
    source_rows = lax.psum(source_rows, "code")

    def matrix(array, scatter):
        array = lax.psum_scatter(array, "dp", scatter_dimension=0, tiled=True)
        return lax.psum_scatter(array, "code", scatter_dimension=scatter, tiled=True).astype(F32)

    conv_part = matrix(jnp.stack([grads[13:22], grads[0:9]]).transpose(2, 0, 1, 3), 3)
    down_part = matrix(grads[9:13].transpose(1, 0, 2), 2)
    proj_part = matrix(grads[22, :, :width], 1)
    norm_grad = lax.psum(norm_grad, ("dp", "code"))
    input_back = lax.all_to_all(
        image[None], "dp", split_axis=2, concat_axis=1, tiled=True
    ).astype(F32)
    conv_out = nesterov_step(conv_master, conv_moment, conv_average, conv_part, weight_rate)
    down_out = nesterov_step(down_master, down_moment, down_average, down_part, weight_rate)
    proj_out = nesterov_step(proj_master, proj_moment, proj_average, proj_part, weight_rate)
    norm_out = nesterov_step(norm_master, norm_moment, norm_average, norm_grad.T, norm_rate)

    counts_all, slope_sum = sums[0], sums[1]
    share = mean_count / (mean_count + counts_all)
    code_load = counts_all / mean_count
    code_grad = code_grad - own_codes.astype(F32) * slope_sum[None, :]
    code_moment_new = MOMENTUM * code_moment.T + code_grad
    stepped = code_master.T - code_rate * (code_grad + MOMENTUM * code_moment_new)
    renewed = mm(source_rows, select)
    code_master_new = stepped + (chosen * share)[None, :] * (renewed - stepped)
    code_average_new = AVERAGE_DECAY * code_average.T + (1.0 - AVERAGE_DECAY) * code_master_new
    return (
        quantized.reshape(1, crop_dev, lat, width),
        input_back,
        *conv_out,
        *down_out,
        *proj_out,
        *norm_out,
        code_moment_new.T,
        code_master_new.T,
        code_average_new.T,
        code_load,
    )


def solution(mesh):
    in_specs = (
        P("code", None, "dp", None),
        P("code", "dp"),
        P("code", "dp", None, None),
        P(),
        P(),
        P(),
        P(),
        P("code", None),
        P("dp", None, None, "code"),
        P("dp", None, None, "code"),
        P("dp", None, None, "code"),
        P("dp", None, "code"),
        P("dp", None, "code"),
        P("dp", None, "code"),
        P("dp", "code"),
        P("dp", "code"),
        P("dp", "code"),
        P(),
        P(),
        P(),
        P("code", "dp"),
        P("code", "dp"),
        P("code", "dp"),
        P(),
        P(),
    )
    out_specs = (
        P("code", "dp", None, None),
        P("code", None, "dp", None),
        P("dp", None, None, "code"),
        P("dp", None, None, "code"),
        P("dp", None, None, "code"),
        P("dp", None, "code"),
        P("dp", None, "code"),
        P("dp", None, "code"),
        P("dp", "code"),
        P("dp", "code"),
        P("dp", "code"),
        P(),
        P(),
        P(),
        P("code", "dp"),
        P("code", "dp"),
        P("code", "dp"),
        P("code"),
    )
    return jax.shard_map(body, mesh=mesh, in_specs=in_specs, out_specs=out_specs, check_vma=False)
```
